32 devices in a mesh: mesh: 2 (over y), seq: 4 (over x, core), fsdp: 4 (over z).
Axes of the slice: x: 2, y: 2, z: 4, core: 2. Of those that a mesh axis runs over, the one named last changes fastest.
Arguments:
- latents: bfloat16 [4, 512, 5120], P('fsdp', 'mesh'), may hold values from -8 to 8
- noise: bfloat16 [4, 512, 5120], P('fsdp', 'mesh'), may hold values from -6 to 6
- noise_level: float32 [4], P('fsdp'), may hold values from 0.05 to 0.3
- group_index: int32 [4, 512], P('fsdp'), may hold values from 0 to 7, never falling along the last dimension, each value on 1 to 128 neighbouring positions
- projections: bfloat16 [2, 5120, 3, 3072], P('mesh', 'fsdp', None, 'seq'), may hold values from -1 to 1, as said below
- upstream: bfloat16 [4, 512, 3072], P('fsdp', None, 'seq'), may hold values from -0.29882812 to 0.29882812
Outputs:
- direction: bfloat16 [4, 512, 3072], P('fsdp', ('mesh', 'seq'))
- fake_grads: float32 [5120, 3, 3072], P(('mesh', 'fsdp'), None, 'seq')
The draws below stay inside these ranges and needn't reach their ends.
Inputs may be any that keep to these rules, and one draw needn't show every extreme that they name: `projections`: along the third dimension: query, key and value projection, in that order. `group_index`: along each clip the group numbers never fall; each of the 8 groups holds 1 to 128 tokens.
All inputs are finite; a program needn't handle non-finite values.
Results may differ from the reference program's by a relative error of at most 0.018.
Values may be sent and summed in bfloat16 or wider, within the bound.
No kernel may reach another device: no remote copies, remote signals or barrier semaphores. Data moves between devices by JAX's collectives and lax.ppermute only.
A program may use at most 128 MiB of HBM per device.

```python
import math
import jax
import jax.numpy as jnp
import numpy as np
from jax import lax

D = 5120
HEAD = 128
HEADS = 24
LEN = 512
GROUPS = 8
GROUP_MOST = 128
CLIPS = 4


def draw_latents(key, part):
    normal_rows = jax.random.normal(jax.random.fold_in(key, 11), (CLIPS, LEN, D), jnp.float32)
    drawn = jnp.clip(normal_rows, -6.0, 6.0)
    return drawn.astype(jnp.bfloat16)


def draw_projections(key, part):
    normal_rows = jax.random.normal(jax.random.fold_in(key, 21), (2, D, 3, HEADS * HEAD), jnp.float32) / math.sqrt(D)
    drawn = normal_rows
    return drawn.astype(jnp.bfloat16)


def steps_of(own_key, extent, split, least, top_value):
    factor_of = 1.0
    for axis_at, shards_of in split:
        steps = jax.random.uniform(jax.random.fold_in(jax.random.fold_in(own_key, 6), axis_at), (shards_of,), jnp.float32, least / len(split), top_value / len(split))
        factor_of = factor_of * jnp.repeat(jnp.exp(steps), extent[axis_at] // shards_of).reshape((-1,) + (1,) * (len(extent) - 1 - axis_at))
    return factor_of


def split_up(amount, total, reach, lean):
    weights = [(1 << 20) // math.isqrt(rank ** lean) + 1 for rank in range(2, amount + 1)]
    rest, counts = total - reach - (amount - 1), [1] * (amount - 1)
    while rest > 0:
        movable = [i for i in range(amount - 1) if counts[i] < reach]
        mass, budget = sum([weights[i] for i in movable]), rest
        for i in movable:
            addition = min(reach - counts[i], max(1, budget * weights[i] // mass), rest)
            counts[i] = counts[i] + addition
            rest = rest - addition
    return np.array([reach] + counts)


def uneven(rng, number_of, total, most, lean):
    if number_of == 2:
        one = jax.random.randint(rng, (), max(1, total - most), min(most, total - 1) + 1)
        return jnp.stack([one, total - one])
    lengths = jnp.asarray(split_up(number_of, total, most, lean), jnp.int32)
    twos = (number_of - 1) // 2
    giver, taker = lengths[1:1 + 2 * twos:2], lengths[2:2 + 2 * twos:2]
    margin = jnp.minimum(giver - 1, most - taker)
    moved = jax.random.randint(jax.random.fold_in(rng, 1), (twos,), 0, 1 << 20) % (margin + 1)
    lengths = lengths.at[1:1 + 2 * twos:2].set(giver - moved).at[2:2 + 2 * twos:2].set(taker + moved)
    return lengths[jax.random.permutation(jax.random.fold_in(rng, 2), number_of)]


def centred(key, extent, deviation, most, pieces=(), held_as=jnp.bfloat16):
    loudness = steps_of(key, extent, pieces, -0.22, 0.18) if pieces else 1.0
    result = jax.random.normal(key, extent, jnp.float32) * deviation * loudness
    return jnp.minimum(jnp.maximum(result, -most), most).astype(held_as)


def setup_inputs(seed: int = 0) -> dict:
    key_of = jax.random.split(jax.random.key(seed), 7)
    latents = draw_latents(jax.random.fold_in(key_of[6], 71), 0)
    noise = centred(key_of[1], (CLIPS, LEN, D), 1.0, 6.0, ((0, 4), (1, 2)))
    noise_level = jnp.clip(jnp.exp(math.log(0.3) - 1.7917595 * jax.random.uniform(key_of[2], (CLIPS,), jnp.float32) ** steps_of(key_of[2], (CLIPS,), ((0, 4),), -0.2, 0.2)), 0.05, 0.3)
    group_index = jax.vmap(lambda own: jnp.searchsorted(jnp.cumsum(uneven(own, GROUPS, LEN, GROUP_MOST, 1)), jnp.arange(LEN), side="right"))(jax.random.split(key_of[3], CLIPS)).reshape((CLIPS, LEN)).astype(jnp.int32)
    projections = draw_projections(jax.random.fold_in(key_of[6], 71), 0)
    upstream = centred(key_of[5], (CLIPS, LEN, HEADS * HEAD), 0.05, 0.29882812, ((0, 4), (2, 4)))
    return {"latents": latents, "noise": noise, "noise_level": noise_level, "group_index": group_index, "projections": projections, "upstream": upstream}


def attend(queries, key_rows, values, visible, score_scale):
    scores = jnp.einsum('qhd,khd->hqk', queries.astype(jnp.float32), key_rows.astype(jnp.float32)) * score_scale
    scores = jnp.where(visible[None], scores, jnp.float32(-1e+30))
    highest = lax.optimization_barrier(jnp.max(scores, axis=-1, keepdims=True))
    weights = jnp.exp(scores - highest)
    probabilities = weights / lax.optimization_barrier(jnp.sum(weights, axis=-1, keepdims=True))
    prob_low = probabilities.astype(jnp.bfloat16)
    attended = jnp.einsum('hqk,khd->qhd', prob_low.astype(jnp.float32), values.astype(jnp.float32)).astype(jnp.bfloat16)
    return (probabilities, prob_low, attended)

def reference(latents, noise, noise_level, group_index, projections, upstream):
    head_cols = HEADS * HEAD
    score_scale = 1.0 / math.sqrt(HEAD)

    def one_clip(running, inputs):
        clip_rows, clip_noise, noise_rate, groups, clip_upstream = inputs
        noised = ((1.0 - noise_rate) * clip_rows.astype(jnp.float32) + noise_rate * clip_noise.astype(jnp.float32)).astype(jnp.bfloat16)
        visible = groups[None, :] <= groups[:, None]
        outputs = []
        for model in range(2):
            triple = jnp.dot(noised, projections[model].reshape(D, 3 * head_cols), preferred_element_type=jnp.float32)
            triple = triple.astype(jnp.bfloat16).reshape(LEN, 3, HEADS, HEAD)
            outputs.append((triple, attend(triple[:, 0], triple[:, 1], triple[:, 2], visible, score_scale)))
        teacher_out = outputs[0][1][2].reshape(LEN, head_cols)
        fake_triple, fake_parts = outputs[1]
        probabilities, prob_low, fake_out = fake_parts
        direction = (fake_out.reshape(LEN, head_cols).astype(jnp.float32) - teacher_out.astype(jnp.float32)).astype(jnp.bfloat16)
        grad_out = clip_upstream.reshape(LEN, HEADS, HEAD).astype(jnp.float32)
        queries = fake_triple[:, 0].astype(jnp.float32)
        key_rows = fake_triple[:, 1].astype(jnp.float32)
        values = fake_triple[:, 2].astype(jnp.float32)
        value_grad = jnp.einsum('hqk,qhd->khd', prob_low.astype(jnp.float32), grad_out).astype(jnp.bfloat16)
        prob_grad = jnp.einsum('qhd,khd->hqk', grad_out, values)
        row_inner = lax.optimization_barrier(jnp.sum(probabilities * prob_grad, axis=-1, keepdims=True))
        score_grad = (probabilities * (prob_grad - row_inner) * score_scale).astype(jnp.bfloat16)
        query_grad = jnp.einsum('hqk,khd->qhd', score_grad.astype(jnp.float32), key_rows).astype(jnp.bfloat16)
        key_grad = jnp.einsum('hqk,qhd->khd', score_grad.astype(jnp.float32), queries).astype(jnp.bfloat16)
        cotangents = jnp.stack([query_grad, key_grad, value_grad], axis=1).reshape(LEN, 3 * head_cols)
        partial_value = lax.dot_general(noised, cotangents, (((0,), (0,)), ((), ())), preferred_element_type=jnp.float32)
        return (running + partial_value.astype(jnp.bfloat16).astype(jnp.float32), direction)
    zero_sum = jnp.zeros((D, 3 * head_cols), jnp.float32)
    summed, direction = lax.scan(one_clip, zero_sum, (latents, noise, noise_level, group_index, upstream))
    return (direction, summed.reshape(D, 3, head_cols))
```

```python
import math

import jax
import jax.numpy as jnp
from jax import lax
from jax.sharding import PartitionSpec as P

HEAD = 128


def contract(columns, factors):
    return lax.dot_general(
        columns, factors, (((0,), (0,)), ((), ())), preferred_element_type=jnp.float32
    )


def in_order(relative, index):
    size = relative.shape[0]
    doubled = jnp.concatenate([relative, relative], axis=0)
    return lax.dynamic_slice_in_dim(doubled, size - index, size, 0)


def spread_mesh(value):
    size = lax.axis_size("mesh")
    pieces = [value]
    for d in range(1, size):
        pairs = [((i + d) % size, i) for i in range(size)]
        pieces.append(lax.ppermute(value, "mesh", pairs))
    return in_order(jnp.stack(pieces), lax.axis_index("mesh"))


def spread_seq(value, cores, over_cores):
    size = lax.axis_size("seq")
    chips = size // cores
    index = lax.axis_index("seq")
    steps = cores if over_cores else chips
    pieces = [value]
    for d in range(1, steps):
        pairs = []
        for i in range(size):
            chip, core = divmod(i, cores)
            if over_cores:
                source = chip * cores + (core + d) % cores
            else:
                source = (chip + d) % chips * cores + core
            pairs.append((source, i))
        pieces.append(lax.ppermute(value, "seq", pairs))
    place = index % cores if over_cores else index // cores
    return in_order(jnp.stack(pieces), place)


def plane_gather(value, cores):
    first = spread_seq(spread_mesh(value[0]), cores, False)
    second = spread_mesh(spread_seq(value[1], cores, False))
    first = jnp.swapaxes(first, 0, 1)
    both = spread_seq(jnp.stack([first, second]), cores, True)
    both = jnp.transpose(both, (1, 4, 2, 3, 0, 5, 6))
    _, clips, mesh, chips, _, rows, width = both.shape
    return both.reshape(2, clips, mesh * chips * cores * rows, width)


def softmax(queries, key_rows, visible, score_scale):
    scores = (
        jnp.einsum("cqd,ckd->cqk", queries, key_rows, preferred_element_type=jnp.float32)
        * score_scale
    )
    scores = jnp.where(visible, scores, jnp.float32(-1e30))
    highest = jnp.max(scores, axis=-1, keepdims=True)
    weights = jnp.exp(scores - highest)
    return weights / jnp.sum(weights, axis=-1, keepdims=True)


def attention(teacher, fake, grad_out, visible, score_scale):
    def parts(triple):
        return triple[..., :HEAD], triple[..., HEAD : 2 * HEAD], triple[..., 2 * HEAD :]

    queries, key_rows, values = parts(teacher)
    prob_low = softmax(queries, key_rows, visible, score_scale).astype(jnp.bfloat16)
    teacher_out = jnp.einsum(
        "cqk,ckd->cqd", prob_low, values, preferred_element_type=jnp.float32
    ).astype(jnp.bfloat16)
    queries, key_rows, values = parts(fake)
    probabilities = softmax(queries, key_rows, visible, score_scale)
    prob_low = probabilities.astype(jnp.bfloat16)
    fake_out = jnp.einsum(
        "cqk,ckd->cqd", prob_low, values, preferred_element_type=jnp.float32
    ).astype(jnp.bfloat16)
    direction = (fake_out.astype(jnp.float32) - teacher_out.astype(jnp.float32)).astype(
        jnp.bfloat16
    )
    value_grad = jnp.einsum("cqk,cqd->ckd", prob_low, grad_out, preferred_element_type=jnp.float32)
    prob_grad = jnp.einsum("cqd,ckd->cqk", grad_out, values, preferred_element_type=jnp.float32)
    row_inner = jnp.sum(probabilities * prob_grad, axis=-1, keepdims=True)
    score_grad = (probabilities * (prob_grad - row_inner) * score_scale).astype(jnp.bfloat16)
    query_grad = jnp.einsum(
        "cqk,ckd->cqd", score_grad, key_rows, preferred_element_type=jnp.float32
    )
    key_grad = jnp.einsum("cqk,cqd->ckd", score_grad, queries, preferred_element_type=jnp.float32)
    cotangents = jnp.concatenate([query_grad, key_grad, value_grad], axis=-1)
    return direction, cotangents.astype(jnp.bfloat16)


def per_device(latents, noise, noise_level, group_index, projections, upstream):
    planes = lax.axis_size("fsdp")
    sides = lax.axis_size("mesh")
    lanes = lax.axis_size("seq")
    plane = lax.axis_index("fsdp")
    side = lax.axis_index("mesh")
    lane = lax.axis_index("seq")
    half = planes // 2
    cores = 2 if lanes % 2 == 0 else 1
    low_half = plane < half
    first_side = side == 0
    swap = [(0, 1), (1, 0)]

    rows, _, head_cols = projections.shape[1:]
    width = latents.shape[2]
    length = group_index.shape[1]
    heads = head_cols // HEAD
    pairs = (heads + 1) // 2
    score_scale = 1.0 / math.sqrt(HEAD)

    def by_distance(stacked):
        low, high = stacked[:half], stacked[::-1][:half]
        return jnp.stack([jnp.where(low_half, low, high), jnp.where(low_half, high, low)])

    piece = latents.shape[1] // lanes
    own_rows = lax.dynamic_slice_in_dim(latents[0], lane * piece, piece, 0)
    own_noise = lax.dynamic_slice_in_dim(noise[0], lane * piece, piece, 0)
    noise_rate = noise_level[0]
    noised = (
        (1.0 - noise_rate) * own_rows.astype(jnp.float32)
        + noise_rate * own_noise.astype(jnp.float32)
    ).astype(jnp.bfloat16)

    def tokens_of(blocks):
        clips = lax.all_to_all(blocks, "fsdp", split_axis=0, concat_axis=0, tiled=True)
        return plane_gather(by_distance(clips), cores)

    tokens = tokens_of(jnp.swapaxes(noised.reshape(piece, planes, rows), 0, 1))
    near = tokens[0].reshape(half * length, rows)
    far = tokens[1].reshape(half * length, rows)

    finals = []
    for head in range(heads):
        factors = projections[0, :, :, head * HEAD : (head + 1) * HEAD].reshape(rows, 3 * HEAD)
        far_part = jnp.dot(far, factors, preferred_element_type=jnp.float32)
        near_part = jnp.dot(near, factors, preferred_element_type=jnp.float32)
        running = far_part.astype(jnp.bfloat16)
        for hop in range(1, planes):
            hops = [(hop - 1, hop), (planes - hop, planes - 1 - hop)]
            arrived = lax.ppermute(running, "fsdp", hops).astype(jnp.float32)
            part = far_part if hop < half else near_part
            running = (arrived + part).astype(jnp.bfloat16)
        finals.append(running.reshape(half, length, 3 * HEAD))

    groups = by_distance(lax.all_gather(group_index, "fsdp", axis=0, tiled=True))[0]
    visible = groups[:, None, :] <= groups[:, :, None]
    kept_heads = [jnp.minimum(2 * j + side, heads - 1) for j in range(pairs)]
    own_up = jnp.stack(
        [lax.dynamic_slice_in_dim(upstream[0], h * HEAD, HEAD, 1) for h in kept_heads]
    )
    ups = [own_up]
    for k in range(1, half):
        ups.append(lax.ppermute(own_up, "fsdp", [(k, 0), (planes - 1 - k, planes - 1)]))
    ups = jnp.stack(ups, axis=1)

    shard_rows = rows // sides
    columns = tokens_of(
        jnp.transpose(noised.reshape(piece, sides, planes, shard_rows), (2, 0, 1, 3)).reshape(
            planes, piece, rows
        )
    )
    near_columns = columns[0].reshape(half * length, rows)
    far_columns = columns[1].reshape(half * length, rows)
    outer = (plane == 0) | (plane == planes - 1)
    distance = jnp.minimum(plane, planes - 1 - plane)

    def pick(hops_of):
        picked = hops_of[half - 1]
        for d in range(half - 2, -1, -1):
            picked = jnp.where(distance == d, hops_of[d], picked)
        return picked

    directions, grads = [], []
    for j in range(pairs):
        even, odd = finals[2 * j], finals[min(2 * j + 1, heads - 1)]
        kept = jnp.where(first_side, even, odd)
        swapped = lax.ppermute(jnp.where(first_side, odd, even), "mesh", swap)
        teacher = jnp.where(first_side, kept, swapped)
        fake = jnp.where(first_side, swapped, kept)
        direction, cotangents = attention(teacher, fake, ups[j], visible, score_scale)
        directions.append(direction)
        passed = [cotangents]
        for hop in range(1, planes):
            hops = [(hop - 1, hop), (planes - hop, planes - 1 - hop)]
            passed.append(lax.ppermute(passed[-1], "fsdp", hops))
        near_cot = pick(passed[:half]).reshape(half * length, 3 * HEAD)
        far_cot = pick(passed[::-1][:half]).reshape(half * length, 3 * HEAD)
        grad = contract(near_columns, near_cot) + contract(far_columns, far_cot)
        grad = grad.reshape(sides, shard_rows, 3, 1, HEAD)
        own_grad = jnp.where(first_side, grad[0], grad[1])
        sent = jnp.where(first_side, grad[1], grad[0]).astype(jnp.bfloat16)
        other = lax.ppermute(sent, "mesh", swap).astype(jnp.float32)
        grads.append(jnp.where(first_side, own_grad, other))
        grads.append(jnp.where(first_side, other, own_grad))
    summed = jnp.concatenate(grads[:heads], axis=2).reshape(shard_rows, 3, head_cols)

    directions = jnp.stack(directions, axis=2)
    local = directions[0]
    for k in range(1, half):
        moved = lax.ppermute(directions[k], "fsdp", [(0, k), (planes - 1, planes - 1 - k)])
        local = jnp.where(distance == k, moved, local)
    local = lax.all_to_all(
        local.reshape(length, pairs * HEAD), ("mesh", "seq"), split_axis=0, concat_axis=1, tiled=True
    )
    local = local.reshape(-1, sides, lanes, pairs, HEAD)
    local = jnp.transpose(local, (0, 2, 3, 1, 4)).reshape(-1, lanes, pairs * sides, HEAD)
    direction = local[:, :, :heads].reshape(1, -1, lanes * head_cols)
    return (direction, summed)


def solution(mesh):
    in_specs = (
        P("fsdp", "mesh", None),
        P("fsdp", "mesh", None),
        P("fsdp"),
        P("fsdp", None),
        P("mesh", "fsdp", None, "seq"),
        P("fsdp", None, "seq"),
    )
    out_specs = (P("fsdp", ("mesh", "seq"), None), P(("mesh", "fsdp"), None, "seq"))
    return jax.shard_map(
        per_device, mesh=mesh, in_specs=in_specs, out_specs=out_specs, check_vma=False
    )
```

```python
import math

import jax
import jax.numpy as jnp
from jax import lax
from jax.sharding import PartitionSpec as P

HEAD = 128


def contract(columns, factors):
    return lax.dot_general(
        columns, factors, (((0,), (0,)), ((), ())), preferred_element_type=jnp.float32
    )


def in_order(relative, index):
    size = relative.shape[0]
    doubled = jnp.concatenate([relative, relative], axis=0)
    return lax.dynamic_slice_in_dim(doubled, size - index, size, 0)


def spread_mesh(value):
    size = lax.axis_size("mesh")
    pieces = [value]
    for d in range(1, size):
        pairs = [((i + d) % size, i) for i in range(size)]
        pieces.append(lax.ppermute(value, "mesh", pairs))
    return in_order(jnp.stack(pieces), lax.axis_index("mesh"))


def spread_seq(value, cores, over_cores):
    size = lax.axis_size("seq")
    chips = size // cores
    index = lax.axis_index("seq")
    steps = cores if over_cores else chips
    pieces = [value]
    for d in range(1, steps):
        pairs = []
        for i in range(size):
            chip, core = divmod(i, cores)
            if over_cores:
                source = chip * cores + (core + d) % cores
            else:
                source = (chip + d) % chips * cores + core
            pairs.append((source, i))
        pieces.append(lax.ppermute(value, "seq", pairs))
    place = index % cores if over_cores else index // cores
    return in_order(jnp.stack(pieces), place)


def gather_step(step, pair, cores):
    first, second = pair
    if step == 0:
        return spread_mesh(first), spread_seq(second, cores, False)
    if step == 1:
        return spread_seq(first, cores, False), spread_mesh(second)
    first = jnp.swapaxes(first, 0, 1)
    both = spread_seq(jnp.stack([first, second]), cores, True)
    both = jnp.transpose(both, (1, 4, 2, 3, 0, 5, 6))
    _, clips, mesh, chips, _, rows, width = both.shape
    both = both.reshape(2, clips * mesh * chips * cores * rows, width)
    return both[0], both[1]


def plane_gather(pair, cores):
    for step in range(3):
        pair = gather_step(step, pair, cores)
    return pair


def plain_dot(left, right):
    return jnp.dot(left, right, preferred_element_type=jnp.float32)


def softmax(queries, key_rows, visible, score_scale):
    scores = (
        jnp.einsum("cqd,ckd->cqk", queries, key_rows, preferred_element_type=jnp.float32)
        * score_scale
    )
    scores = jnp.where(visible, scores, jnp.float32(-1e30))
    highest = jnp.max(scores, axis=-1, keepdims=True)
    weights = jnp.exp(scores - highest)
    return weights / jnp.sum(weights, axis=-1, keepdims=True)


def attention(teacher, fake, grad_out, groups):
    visible = groups[:, None, :] <= groups[:, :, None]
    score_scale = 1.0 / math.sqrt(HEAD)
    def parts(triple):
        return triple[..., :HEAD], triple[..., HEAD : 2 * HEAD], triple[..., 2 * HEAD :]

    queries, key_rows, values = parts(teacher)
    prob_low = softmax(queries, key_rows, visible, score_scale).astype(jnp.bfloat16)
    teacher_out = jnp.einsum(
        "cqk,ckd->cqd", prob_low, values, preferred_element_type=jnp.float32
    ).astype(jnp.bfloat16)
    queries, key_rows, values = parts(fake)
    probabilities = softmax(queries, key_rows, visible, score_scale)
    prob_low = probabilities.astype(jnp.bfloat16)
    fake_out = jnp.einsum(
        "cqk,ckd->cqd", prob_low, values, preferred_element_type=jnp.float32
    ).astype(jnp.bfloat16)
    direction = (fake_out.astype(jnp.float32) - teacher_out.astype(jnp.float32)).astype(
        jnp.bfloat16
    )
    value_grad = jnp.einsum("cqk,cqd->ckd", prob_low, grad_out, preferred_element_type=jnp.float32)
    prob_grad = jnp.einsum("cqd,ckd->cqk", grad_out, values, preferred_element_type=jnp.float32)
    row_inner = jnp.sum(probabilities * prob_grad, axis=-1, keepdims=True)
    score_grad = (probabilities * (prob_grad - row_inner) * score_scale).astype(jnp.bfloat16)
    query_grad = jnp.einsum(
        "cqk,ckd->cqd", score_grad, key_rows, preferred_element_type=jnp.float32
    )
    key_grad = jnp.einsum("cqk,cqd->ckd", score_grad, queries, preferred_element_type=jnp.float32)
    cotangents = jnp.concatenate([query_grad, key_grad, value_grad], axis=-1)
    return direction, cotangents.astype(jnp.bfloat16)


def per_device(latents, noise, noise_level, group_index, projections, upstream):
    planes = lax.axis_size("fsdp")
    sides = lax.axis_size("mesh")
    lanes = lax.axis_size("seq")
    plane = lax.axis_index("fsdp")
    side = lax.axis_index("mesh")
    lane = lax.axis_index("seq")
    half = planes // 2
    chains = 2 if half % 2 == 0 else 1
    share = half // chains
    cores = 2 if lanes % 2 == 0 else 1
    low_half = plane < half
    first_side = side == 0
    distance = jnp.minimum(plane, planes - 1 - plane)
    swap = [(0, 1), (1, 0)]

    rows, _, head_cols = projections.shape[1:]
    length = group_index.shape[1]
    heads = head_cols // HEAD
    pairs = (heads + 1) // 2
    shard_rows = rows // sides

    def hop_pairs(hop):
        return [(hop - 1, hop), (planes - hop, planes - 1 - hop)]

    def send_hops(values):
        sent = {}
        for parity in range(2):
            hops = [hop for hop in sorted(values) if hop % 2 == parity]
            if not hops:
                continue
            value = values[hops[-1]]
            for hop in hops[-2::-1]:
                here = (plane == hop - 1) | (plane == planes - hop)
                value = jnp.where(here, values[hop], value)
            sent[parity] = lax.ppermute(value, "fsdp", sum([hop_pairs(h) for h in hops], []))
        return sent

    def pick(by_distance):
        picked = by_distance[-1]
        for d in range(len(by_distance) - 2, -1, -1):
            picked = jnp.where(distance == d, by_distance[d], picked)
        return picked

    piece = latents.shape[1] // lanes
    own_rows = lax.dynamic_slice_in_dim(latents[0], lane * piece, piece, 0)
    own_noise = lax.dynamic_slice_in_dim(noise[0], lane * piece, piece, 0)
    noise_rate = noise_level[0]
    noised = (
        (1.0 - noise_rate) * own_rows.astype(jnp.float32)
        + noise_rate * own_noise.astype(jnp.float32)
    ).astype(jnp.bfloat16)

    def exchanged(blocks):
        clips = lax.all_to_all(blocks, "fsdp", split_axis=0, concat_axis=0, tiled=True)
        low, high = clips[:half], clips[::-1][:half]
        return jnp.where(low_half, low, high), jnp.where(low_half, high, low)

    near, far = exchanged(jnp.swapaxes(noised.reshape(piece, planes, rows), 0, 1))
    factors = jnp.transpose(projections[0].reshape(rows, 3, heads, HEAD), (2, 0, 1, 3))
    factors = factors.reshape(heads, rows, 3 * HEAD)
    near, far, factors = lax.optimization_barrier((near, far, factors))
    columns = exchanged(
        jnp.transpose(noised.reshape(piece, sides, planes, shard_rows), (2, 0, 1, 3)).reshape(
            planes, piece, rows
        )
    )
    tokens = []
    for chain in range(chains):
        members = slice(chain * share, (chain + 1) * share)
        tokens.append(plane_gather((near[members], far[members]), cores))

    def collected(value):
        found = [value]
        for k in range(1, half):
            found.append(lax.ppermute(value, "fsdp", [(k, 0), (planes - 1 - k, planes - 1)]))
        return found

    kept_heads = [jnp.minimum(2 * j + side, heads - 1) for j in range(pairs)]
    ups = collected(
        jnp.stack([lax.dynamic_slice_in_dim(upstream[0], h * HEAD, HEAD, 1) for h in kept_heads])
    )
    groups = collected(group_index[0])

    parts = {}

    def part(chain, head, is_far):
        key = (chain, head, is_far)
        if key not in parts:
            parts[key] = plain_dot(tokens[chain][is_far], factors[head])
        return parts[key]

    ready = [min(2 * j + 1, heads - 1) + planes - 1 for j in range(pairs)]
    leaves = []
    for j in range(pairs):
        leaves.append(max([ready[j] + 1, heads] + [stage + 1 for stage in leaves[-1:]]))
    stages = leaves[-1] + planes

    pending = [{} for _ in range(chains)]
    finals = [{} for _ in range(chains)]
    passed = [[[] for _ in range(pairs)] for _ in range(chains)]
    directions = [[None] * pairs for _ in range(chains)]
    grads = [None] * heads
    for stage in range(stages):
        for chain in range(chains):
            arrived = lax.optimization_barrier(pending[chain])
            coming = {}
            values = {}
            for hop in range(1, planes + 1):
                head = stage - hop + 1
                if not 0 <= head < heads:
                    continue
                total = part(chain, head, hop <= half)
                if hop > 1:
                    total = total + arrived["sums"][(hop - 1) % 2].astype(jnp.float32)
                values[hop] = total.astype(jnp.bfloat16)
            done = values.pop(planes, None)
            if values:
                coming["sums"] = send_hops(values)
            if done is not None:
                finals[chain][stage - planes + 1] = done.reshape(share, length, 3 * HEAD)
            if chain == 0 and stage <= 2:
                columns = arrived.get("columns", columns)
                columns = gather_step(stage, columns, cores)
                if stage < 2:
                    coming["columns"] = columns
            for j in range(pairs):
                if stage == ready[j]:
                    even, odd = finals[chain][2 * j], finals[chain][min(2 * j + 1, heads - 1)]
                    kept = jnp.where(first_side, even, odd)
                    sent = jnp.where(first_side, odd, even)
                    coming["swapped"] = (kept, lax.ppermute(sent, "mesh", swap))
                if stage == ready[j] + 1:
                    kept, swapped = arrived["swapped"]
                    members = range(chain * share, (chain + 1) * share)
                    direction, cotangents = attention(
                        jnp.where(first_side, kept, swapped),
                        jnp.where(first_side, swapped, kept),
                        jnp.stack([ups[k][j] for k in members]),
                        jnp.stack([groups[k] for k in members]),
                    )
                    directions[chain][j] = direction
                    passed[chain][j].append(cotangents)
            values = {}
            for j in range(pairs):
                hop = stage - leaves[j]
                if 1 <= hop < planes:
                    passed[chain][j].append(arrived["cots"][hop % 2])
                if 0 <= hop < planes - 1:
                    values[hop + 1] = passed[chain][j][hop]
            if values:
                coming["cots"] = send_hops(values)
            pending[chain] = coming
        for j in range(pairs):
            if stage != leaves[j] + planes - 1:
                continue
            grad = None
            for chain in range(chains):
                for is_far in range(2):
                    hops = passed[chain][j][::-1] if is_far else passed[chain][j]
                    cot = pick(hops[:half]).reshape(share * length, 3 * HEAD)
                    size = share * length
                    block = columns[is_far][chain * size : (chain + 1) * size]
                    product = contract(block, cot)
                    grad = product if grad is None else grad + product
            grad = grad.reshape(sides, shard_rows, 3, 1, HEAD)
            own_grad = jnp.where(first_side, grad[0], grad[1])
            sent = jnp.where(first_side, grad[1], grad[0]).astype(jnp.bfloat16)
            other = lax.ppermute(sent, "mesh", swap).astype(jnp.float32)
            grads[2 * j] = jnp.where(first_side, own_grad, other)
            if 2 * j + 1 < heads:
                grads[2 * j + 1] = jnp.where(first_side, other, own_grad)
    summed = jnp.concatenate(grads, axis=2).reshape(shard_rows, 3, head_cols)

    clip_directions = []
    for chain in range(chains):
        stacked = jnp.stack(directions[chain], axis=2)
        clip_directions.extend(stacked[k] for k in range(share))
    local = clip_directions[0]
    for k in range(1, half):
        moved = lax.ppermute(clip_directions[k], "fsdp", [(0, k), (planes - 1, planes - 1 - k)])
        local = jnp.where(distance == k, moved, local)
    local = lax.all_to_all(
        local.reshape(length, pairs * HEAD), ("mesh", "seq"), split_axis=0, concat_axis=1, tiled=True
    )
    local = local.reshape(-1, sides, lanes, pairs, HEAD)
    local = jnp.transpose(local, (0, 2, 3, 1, 4)).reshape(-1, lanes, pairs * sides, HEAD)
    direction = local[:, :, :heads].reshape(1, -1, lanes * head_cols)
    return (direction, summed)


def solution(mesh):
    in_specs = (
        P("fsdp", "mesh", None),
        P("fsdp", "mesh", None),
        P("fsdp"),
        P("fsdp", None),
        P("mesh", "fsdp", None, "seq"),
        P("fsdp", None, "seq"),
    )
    out_specs = (P("fsdp", ("mesh", "seq"), None), P(("mesh", "fsdp"), None, "seq"))
    return jax.shard_map(
        per_device, mesh=mesh, in_specs=in_specs, out_specs=out_specs, check_vma=False
    )
```

```python
import math

import jax
import jax.numpy as jnp
from jax import lax
from jax.sharding import PartitionSpec as P

HEAD = 128


def shifted_by(value, axis, d, inner=1, outer=1):
    pairs = []
    for i in range(lax.axis_size(axis)):
        place = i // inner % outer
        pairs.append((i + ((place + d) % outer - place) * inner, i))
    return lax.ppermute(value, axis, pairs)


def spread(value, axis, inner, outer, at):
    pieces = [value] + [shifted_by(value, axis, d, inner, outer) for d in range(1, outer)]
    return jnp.stack(pieces, axis=at)


def turned(value, at, start):
    size = value.shape[at]
    return lax.dynamic_slice_in_dim(jnp.concatenate([value, value], axis=at), start, size, at)


def own_order(value, factors, back=False):
    sizes = [size for size, _ in factors]
    parts = value.reshape(sizes + [-1] + list(value.shape[1:]))
    for at, (size, place) in enumerate(factors):
        parts = turned(parts, at, size - place if back else place)
    return parts.reshape(value.shape)


def gather_step(step, pair, sides, chips, cores):
    first, second = pair
    if step == 0:
        return spread(first, "mesh", 1, sides, 1), spread(second, "seq", cores, chips, 1)
    if step == 1:
        return spread(first, "seq", cores, chips, 2), spread(second, "mesh", 1, sides, 1)
    both = spread(jnp.stack([first, second]), "seq", 1, cores, 4)
    both = both.reshape(2, -1, both.shape[-1])
    return both[0], both[1]


def dots(left, right, dims):
    return lax.dot_general(left, right, (dims, ((), ())), preferred_element_type=jnp.float32)


def softmax(queries, key_rows, visible, score_scale):
    scores = (
        jnp.einsum("cqd,ckd->cqk", queries, key_rows, preferred_element_type=jnp.float32)
        * score_scale
    )
    scores = jnp.where(visible, scores, jnp.float32(-1e30))
    highest = jnp.max(scores, axis=-1, keepdims=True)
    weights = jnp.exp(scores - highest)
    return weights / jnp.sum(weights, axis=-1, keepdims=True)


def attention(teacher, fake, grad_out, groups):
    visible = groups[:, None, :] <= groups[:, :, None]
    score_scale = 1.0 / math.sqrt(HEAD)
    queries, key_rows, values = teacher
    prob_low = softmax(queries, key_rows, visible, score_scale).astype(jnp.bfloat16)
    teacher_out = jnp.einsum(
        "cqk,ckd->cqd", prob_low, values, preferred_element_type=jnp.float32
    ).astype(jnp.bfloat16)
    queries, key_rows, values = fake
    probabilities = softmax(queries, key_rows, visible, score_scale)
    prob_low = probabilities.astype(jnp.bfloat16)
    fake_out = jnp.einsum(
        "cqk,ckd->cqd", prob_low, values, preferred_element_type=jnp.float32
    ).astype(jnp.bfloat16)
    direction = (fake_out.astype(jnp.float32) - teacher_out.astype(jnp.float32)).astype(
        jnp.bfloat16
    )
    value_grad = jnp.einsum("cqk,cqd->ckd", prob_low, grad_out, preferred_element_type=jnp.float32)
    prob_grad = jnp.einsum("cqd,ckd->cqk", grad_out, values, preferred_element_type=jnp.float32)
    row_inner = jnp.sum(probabilities * prob_grad, axis=-1, keepdims=True)
    score_grad = (probabilities * (prob_grad - row_inner) * score_scale).astype(jnp.bfloat16)
    query_grad = jnp.einsum(
        "cqk,ckd->cqd", score_grad, key_rows, preferred_element_type=jnp.float32
    )
    key_grad = jnp.einsum("cqk,cqd->ckd", score_grad, queries, preferred_element_type=jnp.float32)
    cotangents = jnp.stack([query_grad, key_grad, value_grad])
    return direction, cotangents.astype(jnp.bfloat16)


def per_device(latents, noise, noise_level, group_index, projections, upstream):
    planes = lax.axis_size("fsdp")
    sides = lax.axis_size("mesh")
    lanes = lax.axis_size("seq")
    plane = lax.axis_index("fsdp")
    side = lax.axis_index("mesh")
    lane = lax.axis_index("seq")
    half = planes // 2
    chains = 2 if half % 2 == 0 else 1
    share = half // chains
    cores = 2 if lanes % 2 == 0 else 1
    chips = lanes // cores
    order = [(sides, side), (chips, lane // cores), (cores, lane % cores)]
    low_half = plane < half
    first_side = side == 0
    distance = jnp.minimum(plane, planes - 1 - plane)
    swap = [(0, 1), (1, 0)]

    rows, _, head_cols = projections.shape[1:]
    length = group_index.shape[1]
    heads = head_cols // HEAD
    pairs = (heads + 1) // 2
    shard_rows = rows // sides

    def hop_pairs(hop):
        return [(hop - 1, hop), (planes - hop, planes - 1 - hop)]

    def send_hops(values):
        sent = {}
        for parity in range(2):
            hops = [hop for hop in sorted(values) if hop % 2 == parity]
            if not hops:
                continue
            value = values[hops[-1]]
            for hop in hops[-2::-1]:
                here = (plane == hop - 1) | (plane == planes - hop)
                value = jnp.where(here, values[hop], value)
            sent[parity] = lax.ppermute(value, "fsdp", sum([hop_pairs(h) for h in hops], []))
        return sent

    def pick(by_distance):
        picked = by_distance[-1]
        for d in range(len(by_distance) - 2, -1, -1):
            picked = jnp.where(distance == d, by_distance[d], picked)
        return picked

    piece = latents.shape[1] // lanes
    own_rows = lax.dynamic_slice_in_dim(latents[0], lane * piece, piece, 0)
    own_noise = lax.dynamic_slice_in_dim(noise[0], lane * piece, piece, 0)
    noise_rate = noise_level[0]
    noised = (
        (1.0 - noise_rate) * own_rows.astype(jnp.float32)
        + noise_rate * own_noise.astype(jnp.float32)
    ).astype(jnp.bfloat16)

    def exchanged(blocks):
        clips = lax.all_to_all(blocks, "fsdp", split_axis=0, concat_axis=0, tiled=True)
        low, high = clips[:half], clips[::-1][:half]
        return jnp.where(low_half, low, high), jnp.where(low_half, high, low)

    near, far = exchanged(jnp.swapaxes(noised.reshape(piece, planes, rows), 0, 1))
    steps = []
    for chain in range(chains):
        members = slice(chain * share, (chain + 1) * share)
        steps.append(gather_step(0, (near[members], far[members]), sides, chips, cores))
    steps, noised = lax.optimization_barrier((steps, noised))
    columns = exchanged(
        jnp.transpose(noised.reshape(piece, sides, planes, shard_rows), (2, 0, 1, 3)).reshape(
            planes, piece, rows
        )
    )
    tokens = []
    for chain in range(chains):
        found = gather_step(1, steps[chain], sides, chips, cores)
        tokens.append(gather_step(2, found, sides, chips, cores))

    def collected(value):
        found = [value]
        for k in range(1, half):
            found.append(lax.ppermute(value, "fsdp", [(k, 0), (planes - 1 - k, planes - 1)]))
        return found

    own_up = own_order(upstream[0], order)
    kept_heads = [jnp.minimum(2 * j + side, heads - 1) for j in range(pairs)]
    ups = collected(
        jnp.stack([lax.dynamic_slice_in_dim(own_up, h * HEAD, HEAD, 1) for h in kept_heads])
    )
    groups = collected(own_order(group_index[0], order))

    def products(rows_of):
        return jnp.swapaxes(dots(rows_of, projections[0], ((1,), (0,))), 0, 1)

    ready = [min(2 * j + 1, heads - 1) + planes - 1 for j in range(pairs)]
    leaves = []
    for j in range(pairs):
        leaves.append(max([ready[j] + 1, heads] + [stage + 1 for stage in leaves[-1:]]))
    stages = leaves[-1] + planes

    pending = [{} for _ in range(chains)]
    finals = [{} for _ in range(chains)]
    passed = [[[] for _ in range(pairs)] for _ in range(chains)]
    directions = [[] for _ in range(pairs)]
    sums = [None] * pairs
    parts = [[None, None] for _ in range(chains)]
    summed = [jnp.zeros((3, shard_rows, head_cols), jnp.float32)]
    settled = []

    def settle(own_grad, other):
        head = 2 * len(settled)
        settled.append(head)
        other = other.astype(jnp.float32)
        first = jnp.where(first_side, own_grad, other)
        second = jnp.where(first_side, other, own_grad)
        both = jnp.concatenate([first, second], axis=2)[:, :, : (heads - head) * HEAD]
        summed[0] = lax.dynamic_update_slice(summed[0], both, (0, 0, head * HEAD))

    for stage in range(stages):
        for chain in range(chains):
            arrived = lax.optimization_barrier(pending[chain])
            coming = {}
            if stage == 0:
                parts[chain][1] = products(tokens[chain][1])
                coming["near"] = tokens[chain][0]
            if stage == 1:
                coming["near"] = products(arrived["near"])
            if stage == 2:
                parts[chain][0] = arrived["near"]
            if "other" in arrived:
                settle(*arrived["other"])
            values = {}
            for hop in range(1, planes + 1):
                head = stage - hop + 1
                if not 0 <= head < heads:
                    continue
                block = slice(head * HEAD, (head + 1) * HEAD)
                total = parts[chain][hop <= half][:, :, block]
                if hop > 1:
                    total = total + arrived["sums"][(hop - 1) % 2].astype(jnp.float32)
                values[hop] = total.astype(jnp.bfloat16)
            done = values.pop(planes, None)
            if values:
                coming["sums"] = send_hops(values)
            if done is not None:
                finals[chain][stage - planes + 1] = done
            if chain == 0 and stage <= 3:
                if stage == 0:
                    coming["columns"] = columns
                else:
                    columns = gather_step(stage - 1, arrived["columns"], sides, chips, cores)
                    coming["columns"] = columns
            if chain == 0 and stage == 4:
                columns = arrived["columns"]
            for j in range(pairs):
                if stage == ready[j]:
                    even, odd = finals[chain][2 * j], finals[chain][min(2 * j + 1, heads - 1)]
                    kept = jnp.where(first_side, even, odd)
                    sent = jnp.where(first_side, odd, even)
                    coming["swapped"] = (kept, lax.ppermute(sent, "mesh", swap))
                if stage == ready[j] + 1:
                    kept, swapped = arrived["swapped"]
                    swapped = swapped.reshape(3, share, sides, length // sides, HEAD)
                    swapped = swapped[:, :, ::-1].reshape(3, share, length, HEAD)
                    kept = kept.reshape(3, share, length, HEAD)
                    members = range(chain * share, (chain + 1) * share)
                    direction, cotangents = attention(
                        jnp.where(first_side, kept, swapped),
                        jnp.where(first_side, swapped, kept),
                        jnp.stack([ups[k][j] for k in members]),
                        jnp.stack([groups[k] for k in members]),
                    )
                    passed[chain][j].append(cotangents)
                    coming["directions"] = []
                    for k in members:
                        moved = direction[k - chain * share]
                        if k > 0:
                            hops = [(0, k), (planes - 1, planes - 1 - k)]
                            moved = lax.ppermute(moved, "fsdp", hops)
                        coming["directions"].append(moved)
                if stage == ready[j] + 2:
                    directions[j].extend(arrived["directions"])
            values = {}
            for j in range(pairs):
                hop = stage - leaves[j]
                if 1 <= hop < planes:
                    passed[chain][j].append(arrived["cots"][hop % 2])
                if 0 <= hop < planes - 1:
                    values[hop + 1] = passed[chain][j][hop]
            if values:
                coming["cots"] = send_hops(values)
            for j in range(pairs):
                if stage != leaves[j] + planes - 1:
                    continue
                size = share * length
                for is_far in range(2):
                    hops = passed[chain][j][::-1] if is_far else passed[chain][j]
                    cot = pick(hops[:half]).reshape(3, size, HEAD)
                    block = columns[is_far][chain * size : (chain + 1) * size]
                    product = dots(block, cot, ((0,), (1,)))
                    sums[j] = product if sums[j] is None else sums[j] + product
                if chain < chains - 1:
                    coming["grad"] = sums[j]
                    continue
                grad = jnp.swapaxes(sums[j], 0, 1).reshape(3, sides, shard_rows, HEAD)
                own_grad = jnp.where(first_side, grad[:, 0], grad[:, 1])
                sent = jnp.where(first_side, grad[:, 1], grad[:, 0]).astype(jnp.bfloat16)
                coming["other"] = (own_grad, lax.ppermute(sent, "mesh", swap))
            pending[chain] = coming
        if stage == ready[-1] + 2:
            local = []
            for j in range(pairs):
                picked = directions[j][0]
                for k in range(1, half):
                    picked = jnp.where(distance == k, directions[j][k], picked)
                local.append(picked)
            local = own_order(jnp.concatenate(local, axis=1), order, back=True)
            local = lax.all_to_all(
                local, ("mesh", "seq"), split_axis=0, concat_axis=1, tiled=True
            )
    settle(*pending[-1]["other"])
    summed = jnp.swapaxes(summed[0], 0, 1)

    local = local.reshape(-1, sides, lanes, pairs, HEAD)
    local = jnp.transpose(local, (0, 2, 3, 1, 4)).reshape(-1, lanes, pairs * sides, HEAD)
    direction = local[:, :, :heads].reshape(1, -1, lanes * head_cols)
    return (direction, summed)


def solution(mesh):
    in_specs = (
        P("fsdp", "mesh", None),
        P("fsdp", "mesh", None),
        P("fsdp"),
        P("fsdp", None),
        P("mesh", "fsdp", None, "seq"),
        P("fsdp", None, "seq"),
    )
    out_specs = (P("fsdp", ("mesh", "seq"), None), P(("mesh", "fsdp"), None, "seq"))
    return jax.shard_map(
        per_device, mesh=mesh, in_specs=in_specs, out_specs=out_specs, check_vma=False
    )
```

```python
import math

import jax
import jax.numpy as jnp
from jax import lax
from jax.experimental import pallas as pl
from jax.experimental.pallas import tpu as pltpu
from jax.sharding import PartitionSpec as P

HEAD = 128


def shifted_by(value, axis, d, inner=1, outer=1):
    pairs = []
    for i in range(lax.axis_size(axis)):
        place = i // inner % outer
        pairs.append((i + ((place + d) % outer - place) * inner, i))
    return lax.ppermute(value, axis, pairs)


def spread(value, axis, inner, outer, at):
    pieces = [value] + [shifted_by(value, axis, d, inner, outer) for d in range(1, outer)]
    return jnp.stack(pieces, axis=at)


def turned(value, at, start):
    size = value.shape[at]
    return lax.dynamic_slice_in_dim(jnp.concatenate([value, value], axis=at), start, size, at)


def own_order(value, factors, back=False):
    sizes = [size for size, _ in factors]
    parts = value.reshape(sizes + [-1] + list(value.shape[1:]))
    for at, (size, place) in enumerate(factors):
        parts = turned(parts, at, size - place if back else place)
    return parts.reshape(value.shape)


def gather_step(step, pair, sides, chips, cores):
    first, second = pair
    if step == 0:
        return spread(first, "mesh", 1, sides, 1), spread(second, "seq", cores, chips, 1)
    if step == 1:
        return spread(first, "seq", cores, chips, 2), spread(second, "mesh", 1, sides, 1)
    both = spread(jnp.stack([first, second]), "seq", 1, cores, 4)
    both = both.reshape(2, -1, both.shape[-1])
    return both[0], both[1]


def dots(left, right, dims):
    return lax.dot_general(left, right, (dims, ((), ())), preferred_element_type=jnp.float32)


def attention_kernel(
    block, sides, side_ref, kept_ref, swapped_ref, up_ref, key_group_ref, group_ref,
    direction_ref, cot_ref, teacher_ref, fake_ref, key_grad_ref, value_grad_ref,
):
    length = kept_ref.shape[2]
    span = length // sides
    score_scale = 1.0 / math.sqrt(HEAD)
    first_side = side_ref[0] == 0
    for at in range(sides):
        here = pl.ds(at * span, span)
        there = pl.ds((sides - 1 - at) * span, span)
        kept, swapped = kept_ref[:, 0, here, :], swapped_ref[:, 0, there, :]
        teacher_ref[:, here, :] = jnp.where(first_side, kept, swapped)
        fake_ref[:, here, :] = jnp.where(first_side, swapped, kept)

    def softmax(triple_ref, rows, visible):
        scores = dots(triple_ref[0, rows, :], triple_ref[1], ((1,), (1,)))
        scores = jnp.where(visible, scores * score_scale, jnp.float32(-1e30))
        weights = jnp.exp(scores - jnp.max(scores, axis=-1, keepdims=True))
        return weights * (1.0 / jnp.sum(weights, axis=-1, keepdims=True))

    for start in range(0, length, block):
        rows = pl.ds(start, block)
        visible = key_group_ref[0, :1, :] <= group_ref[0, rows, :1]
        prob_low = softmax(teacher_ref, rows, visible).astype(jnp.bfloat16)
        teacher_out = dots(prob_low, teacher_ref[2], ((1,), (0,))).astype(jnp.bfloat16)
        probabilities = softmax(fake_ref, rows, visible)
        prob_low = probabilities.astype(jnp.bfloat16)
        values = fake_ref[2]
        fake_out = dots(prob_low, values, ((1,), (0,))).astype(jnp.bfloat16)
        direction_ref[0, rows, :] = (
            fake_out.astype(jnp.float32) - teacher_out.astype(jnp.float32)
        ).astype(jnp.bfloat16)
        grad_out = up_ref[0, rows, :]
        prob_grad = dots(grad_out, values, ((1,), (1,)))
        row_inner = jnp.sum(probabilities * prob_grad, axis=-1, keepdims=True)
        score_grad = probabilities * (prob_grad - row_inner) * score_scale
        query_grad = dots(score_grad.astype(jnp.bfloat16), fake_ref[1], ((1,), (0,)))
        cot_ref[0, 0, rows, :] = query_grad.astype(jnp.bfloat16)
        score_grad = jnp.transpose(score_grad).astype(jnp.bfloat16)
        key_part = dots(score_grad, fake_ref[0, rows, :], ((1,), (0,)))
        prob_low = jnp.transpose(probabilities).astype(jnp.bfloat16)
        value_part = dots(prob_low, grad_out, ((1,), (0,)))
        if start == 0:
            key_grad_ref[...] = key_part
            value_grad_ref[...] = value_part
        else:
            key_grad_ref[...] += key_part
            value_grad_ref[...] += value_part
    cot_ref[1, 0] = key_grad_ref[...].astype(jnp.bfloat16)
    cot_ref[2, 0] = value_grad_ref[...].astype(jnp.bfloat16)


def attention(side, sides, kept, swapped, grad_out, groups):
    _, clips, length, _ = kept.shape
    block = math.gcd(length, 256)
    area = clips * length * length

    def spec(rows, columns):
        return pl.BlockSpec((1, rows, columns), lambda clip: (clip, 0, 0))

    triple = pl.BlockSpec((3, 1, length, HEAD), lambda clip: (0, clip, 0, 0))
    return pl.pallas_call(
        lambda *refs: attention_kernel(block, sides, *refs),
        grid=(clips,),
        in_specs=[
            pl.BlockSpec(memory_space=pltpu.SMEM),
            triple, triple, spec(length, HEAD), spec(8, length), spec(length, HEAD),
        ],
        out_specs=[spec(length, HEAD), triple],
        out_shape=[
            jax.ShapeDtypeStruct((clips, length, HEAD), jnp.bfloat16),
            jax.ShapeDtypeStruct((3, clips, length, HEAD), jnp.bfloat16),
        ],
        scratch_shapes=[pltpu.VMEM((3, length, HEAD), jnp.bfloat16)] * 2
        + [pltpu.VMEM((length, HEAD), jnp.float32)] * 2,
        compiler_params=pltpu.CompilerParams(vmem_limit_bytes=60 * 1024 * 1024),
        cost_estimate=pl.CostEstimate(
            flops=18 * area * HEAD,
            bytes_accessed=20 * clips * length * HEAD,
            transcendentals=2 * area,
        ),
        name="attention",
    )(side.reshape(1), kept, swapped, grad_out, *groups)


def per_device(latents, noise, noise_level, group_index, projections, upstream):
    planes = lax.axis_size("fsdp")
    sides = lax.axis_size("mesh")
    lanes = lax.axis_size("seq")
    plane = lax.axis_index("fsdp")
    side = lax.axis_index("mesh")
    lane = lax.axis_index("seq")
    half = planes // 2
    chains = 2 if half % 2 == 0 else 1
    share = half // chains
    cores = 2 if lanes % 2 == 0 else 1
    chips = lanes // cores
    order = [(sides, side), (chips, lane // cores), (cores, lane % cores)]
    low_half = plane < half
    first_side = side == 0
    distance = jnp.minimum(plane, planes - 1 - plane)
    swap = [(0, 1), (1, 0)]

    rows, _, head_cols = projections.shape[1:]
    length = group_index.shape[1]
    heads = head_cols // HEAD
    pairs = (heads + 1) // 2
    shard_rows = rows // sides

    def hop_pairs(hop):
        return [(hop - 1, hop), (planes - hop, planes - 1 - hop)]

    def send_hops(values):
        sent = {}
        for parity in range(2):
            hops = [hop for hop in sorted(values) if hop % 2 == parity]
            if not hops:
                continue
            value = values[hops[-1]]
            for hop in hops[-2::-1]:
                here = (plane == hop - 1) | (plane == planes - hop)
                value = jnp.where(here, values[hop], value)
            sent[parity] = lax.ppermute(value, "fsdp", sum([hop_pairs(h) for h in hops], []))
        return sent

    def pick(by_distance):
        picked = by_distance[-1]
        for d in range(len(by_distance) - 2, -1, -1):
            picked = jnp.where(distance == d, by_distance[d], picked)
        return picked

    piece = latents.shape[1] // lanes
    own_rows = lax.dynamic_slice_in_dim(latents[0], lane * piece, piece, 0)
    own_noise = lax.dynamic_slice_in_dim(noise[0], lane * piece, piece, 0)
    noise_rate = noise_level[0]
    noised = (
        (1.0 - noise_rate) * own_rows.astype(jnp.float32)
        + noise_rate * own_noise.astype(jnp.float32)
    ).astype(jnp.bfloat16)

    def exchanged(blocks):
        pieces = []
        for k in range(half):
            found = []
            for to in range(planes):
                value = jnp.where(low_half, blocks[to], blocks[planes - 1 - to])
                if to != k:
                    value = lax.ppermute(
                        value, "fsdp", [(k, to), (planes - 1 - k, planes - 1 - to)]
                    )
                found.append(value)
            pieces.append((pick(found[:half]), pick(found[::-1][:half])))
        return pieces

    pieces = exchanged(jnp.swapaxes(noised.reshape(piece, planes, rows), 0, 1))
    tokens = []
    for chain in range(chains):
        members = pieces[chain * share : (chain + 1) * share]
        found = tuple(jnp.stack(both) for both in zip(*members))
        for step in range(3):
            found = gather_step(step, found, sides, chips, cores)
        tokens.append(found)
    tokens[-1], noised = lax.optimization_barrier((tokens[-1], noised))
    columns = exchanged(
        jnp.transpose(noised.reshape(piece, sides, planes, shard_rows), (2, 0, 1, 3)).reshape(
            planes, piece, rows
        )
    )
    columns = tuple(jnp.stack(both) for both in zip(*columns))

    def collected(value):
        found = [value]
        for k in range(1, half):
            found.append(lax.ppermute(value, "fsdp", [(k, 0), (planes - 1 - k, planes - 1)]))
        return found

    own_up = own_order(upstream[0], order)
    kept_heads = [jnp.minimum(2 * j + side, heads - 1) for j in range(pairs)]
    ups = collected(
        jnp.stack([lax.dynamic_slice_in_dim(own_up, h * HEAD, HEAD, 1) for h in kept_heads])
    )
    groups = collected(own_order(group_index[0], order))
    group_forms = []
    for chain in range(chains):
        own = jnp.stack(groups[chain * share : (chain + 1) * share])
        group_forms.append(
            (
                jnp.broadcast_to(own[:, None, :], (share, 8, length)),
                jnp.broadcast_to(own[:, :, None], (share, length, HEAD)),
            )
        )

    def products(rows_of, factors):
        return jnp.swapaxes(dots(rows_of, factors, ((1,), (0,))), 0, 1)

    ready = [min(2 * j + 1, heads - 1) + planes - 1 for j in range(pairs)]
    leaves = []
    for j in range(pairs):
        leaves.append(max([ready[j] + 1, heads] + [stage + 1 for stage in leaves[-1:]]))
    stages = leaves[-1] + planes

    pending = [{} for _ in range(chains)]
    finals = [{} for _ in range(chains)]
    passed = [[[] for _ in range(pairs)] for _ in range(chains)]
    directions = [[] for _ in range(pairs)]
    sums = [None] * pairs
    parts = [[None, None] for _ in range(chains)]
    summed = [jnp.zeros((3, shard_rows, head_cols), jnp.float32)]
    settled = []

    def settle(own_grad, other):
        head = 2 * len(settled)
        settled.append(head)
        other = other.astype(jnp.float32)
        first = jnp.where(first_side, own_grad, other)
        second = jnp.where(first_side, other, own_grad)
        both = jnp.concatenate([first, second], axis=2)[:, :, : (heads - head) * HEAD]
        summed[0] = lax.dynamic_update_slice(summed[0], both, (0, 0, head * HEAD))

    for stage in range(stages):
        for chain in range(chains):
            arrived = lax.optimization_barrier(pending[chain])
            coming = {}
            if stage == 0:
                head_block = projections[0, :, :, :HEAD]
                parts[chain][1] = products(tokens[chain][1], head_block)
                coming["far"], coming["near"] = tokens[chain][1], tokens[chain][0]
            if stage == 1:
                parts[chain][1] = products(arrived["far"], projections[0])
                coming["near"] = products(arrived["near"], projections[0])
            if stage == 2:
                parts[chain][0] = arrived["near"]
            if "other" in arrived:
                settle(*arrived["other"])
            values = {}
            for hop in range(1, planes + 1):
                head = stage - hop + 1
                if not 0 <= head < heads:
                    continue
                block = slice(head * HEAD, (head + 1) * HEAD)
                total = parts[chain][hop <= half][:, :, block]
                if hop > 1:
                    total = total + arrived["sums"][(hop - 1) % 2].astype(jnp.float32)
                values[hop] = total.astype(jnp.bfloat16)
            done = values.pop(planes, None)
            if values:
                coming["sums"] = send_hops(values)
            if done is not None:
                finals[chain][stage - planes + 1] = done
            if chain == 0 and stage <= 3:
                if stage == 0:
                    coming["columns"] = columns
                else:
                    columns = gather_step(stage - 1, arrived["columns"], sides, chips, cores)
                    coming["columns"] = columns
            if chain == 0 and stage == 4:
                columns = arrived["columns"]
            for j in range(pairs):
                if stage == ready[j]:
                    even, odd = finals[chain][2 * j], finals[chain][min(2 * j + 1, heads - 1)]
                    kept = jnp.where(first_side, even, odd)
                    sent = jnp.where(first_side, odd, even)
                    coming["swapped"] = (kept, lax.ppermute(sent, "mesh", swap))
                if stage == ready[j] + 1:
                    kept, swapped = arrived["swapped"]
                    members = range(chain * share, (chain + 1) * share)
                    direction, cotangents = attention(
                        side,
                        sides,
                        kept.reshape(3, share, length, HEAD),
                        swapped.reshape(3, share, length, HEAD),
                        jnp.stack([ups[k][j] for k in members]),
                        group_forms[chain],
                    )
                    passed[chain][j].append(cotangents)
                    coming["directions"] = []
                    for k in members:
                        moved = direction[k - chain * share]
                        if k > 0:
                            hops = [(0, k), (planes - 1, planes - 1 - k)]
                            moved = lax.ppermute(moved, "fsdp", hops)
                        coming["directions"].append(moved)
                if stage == ready[j] + 2:
                    directions[j].extend(arrived["directions"])
            values = {}
            for j in range(pairs):
                hop = stage - leaves[j]
                if 1 <= hop < planes:
                    passed[chain][j].append(arrived["cots"][hop % 2])
                if 0 <= hop < planes - 1:
                    values[hop + 1] = passed[chain][j][hop]
            if values:
                coming["cots"] = send_hops(values)
            for j in range(pairs):
                if stage != leaves[j] + planes - 1:
                    continue
                size = share * length
                for is_far in range(2):
                    hops = passed[chain][j][::-1] if is_far else passed[chain][j]
                    cot = pick(hops[:half]).reshape(3, size, HEAD)
                    block = columns[is_far][chain * size : (chain + 1) * size]
                    product = dots(block, cot, ((0,), (1,)))
                    sums[j] = product if sums[j] is None else sums[j] + product
                if chain < chains - 1:
                    coming["grad"] = sums[j]
                    continue
                grad = jnp.swapaxes(sums[j], 0, 1).reshape(3, sides, shard_rows, HEAD)
                own_grad = jnp.where(first_side, grad[:, 0], grad[:, 1])
                sent = jnp.where(first_side, grad[:, 1], grad[:, 0]).astype(jnp.bfloat16)
                coming["other"] = (own_grad, lax.ppermute(sent, "mesh", swap))
            pending[chain] = coming
        if stage == ready[-1] + 2:
            local = []
            for j in range(pairs):
                picked = directions[j][0]
                for k in range(1, half):
                    picked = jnp.where(distance == k, directions[j][k], picked)
                local.append(picked)
            local = jnp.concatenate(local, axis=1)
            local = local.reshape(sides, chips, cores, -1, pairs * HEAD)
            axes = [("mesh", 1, sides), ("seq", cores, chips), ("seq", 1, cores)]
            for at, (axis, inner, outer) in enumerate(axes):
                blocks = [lax.index_in_dim(local, -d % outer, at, False) for d in range(outer)]
                for d in range(1, outer):
                    blocks[d] = shifted_by(blocks[d], axis, d, inner, outer)
                local = jnp.stack(blocks, axis=at)
            local = own_order(local.reshape(sides * lanes, -1, pairs * HEAD), order, back=True)
    settle(*pending[-1]["other"])
    summed = jnp.swapaxes(summed[0], 0, 1)

    local = local.reshape(sides, lanes, -1, pairs, HEAD)
    local = jnp.transpose(local, (2, 1, 3, 0, 4)).reshape(-1, lanes, pairs * sides, HEAD)
    direction = local[:, :, :heads].reshape(1, -1, lanes * head_cols)
    return (direction, summed)


def solution(mesh):
    in_specs = (
        P("fsdp", "mesh", None),
        P("fsdp", "mesh", None),
        P("fsdp"),
        P("fsdp", None),
        P("mesh", "fsdp", None, "seq"),
        P("fsdp", None, "seq"),
    )
    out_specs = (P("fsdp", ("mesh", "seq"), None), P(("mesh", "fsdp"), None, "seq"))
    return jax.shard_map(
        per_device, mesh=mesh, in_specs=in_specs, out_specs=out_specs, check_vma=False
    )
```

```python
import math

import jax
import jax.numpy as jnp
from jax import lax
from jax.experimental import pallas as pl
from jax.experimental.pallas import tpu as pltpu
from jax.sharding import PartitionSpec as P

HEAD = 128


def shifted_by(value, axis, d, inner=1, outer=1):
    pairs = []
    for i in range(lax.axis_size(axis)):
        place = i // inner % outer
        pairs.append((i + ((place + d) % outer - place) * inner, i))
    return lax.ppermute(value, axis, pairs)


def spread(value, axis, inner, outer, at):
    pieces = [value] + [shifted_by(value, axis, d, inner, outer) for d in range(1, outer)]
    return jnp.stack(pieces, axis=at)


def turned(value, at, start):
    size = value.shape[at]
    return lax.dynamic_slice_in_dim(jnp.concatenate([value, value], axis=at), start, size, at)


def own_order(value, factors, back=False):
    sizes = [size for size, _ in factors]
    parts = value.reshape(sizes + [-1] + list(value.shape[1:]))
    for at, (size, place) in enumerate(factors):
        parts = turned(parts, at, size - place if back else place)
    return parts.reshape(value.shape)


def gather_step(step, pair, sides, chips, cores):
    first, second = pair
    if step == 0:
        return spread(first, "mesh", 1, sides, 1), spread(second, "seq", cores, chips, 1)
    if step == 1:
        return spread(first, "seq", cores, chips, 2), spread(second, "mesh", 1, sides, 1)
    both = spread(jnp.stack([first, second]), "seq", 1, cores, 4)
    both = both.reshape(2, -1, both.shape[-1])
    return both[0], both[1]


def dots(left, right, dims):
    return lax.dot_general(left, right, (dims, ((), ())), preferred_element_type=jnp.float32)


def attention_kernel(
    block, sides, side_ref, kept_ref, swapped_ref, up_ref, key_group_ref, group_ref,
    direction_ref, cot_ref, teacher_ref, fake_ref, key_grad_ref, value_grad_ref,
):
    length = kept_ref.shape[2]
    span = length // sides
    score_scale = 1.0 / math.sqrt(HEAD)
    first_side = side_ref[0] == 0
    for at in range(sides):
        here = pl.ds(at * span, span)
        there = pl.ds((sides - 1 - at) * span, span)
        kept, swapped = kept_ref[:, 0, here, :], swapped_ref[:, 0, there, :]
        teacher_ref[:, here, :] = jnp.where(first_side, kept, swapped)
        fake_ref[:, here, :] = jnp.where(first_side, swapped, kept)

    def softmax(triple_ref, rows, visible):
        scores = dots(triple_ref[0, rows, :], triple_ref[1], ((1,), (1,)))
        scores = jnp.where(visible, scores * score_scale, jnp.float32(-1e30))
        weights = jnp.exp(scores - jnp.max(scores, axis=-1, keepdims=True))
        return weights * (1.0 / jnp.sum(weights, axis=-1, keepdims=True))

    for start in range(0, length, block):
        rows = pl.ds(start, block)
        visible = key_group_ref[0, :1, :] <= group_ref[0, rows, :1]
        prob_low = softmax(teacher_ref, rows, visible).astype(jnp.bfloat16)
        teacher_out = dots(prob_low, teacher_ref[2], ((1,), (0,))).astype(jnp.bfloat16)
        probabilities = softmax(fake_ref, rows, visible)
        prob_low = probabilities.astype(jnp.bfloat16)
        values = fake_ref[2]
        fake_out = dots(prob_low, values, ((1,), (0,))).astype(jnp.bfloat16)
        direction_ref[0, rows, :] = (
            fake_out.astype(jnp.float32) - teacher_out.astype(jnp.float32)
        ).astype(jnp.bfloat16)
        grad_out = up_ref[0, rows, :]
        prob_grad = dots(grad_out, values, ((1,), (1,)))
        row_inner = jnp.sum(probabilities * prob_grad, axis=-1, keepdims=True)
        score_grad = probabilities * (prob_grad - row_inner) * score_scale
        query_grad = dots(score_grad.astype(jnp.bfloat16), fake_ref[1], ((1,), (0,)))
        cot_ref[0, 0, rows, :] = query_grad.astype(jnp.bfloat16)
        score_grad = jnp.transpose(score_grad).astype(jnp.bfloat16)
        key_part = dots(score_grad, fake_ref[0, rows, :], ((1,), (0,)))
        prob_low = jnp.transpose(probabilities).astype(jnp.bfloat16)
        value_part = dots(prob_low, grad_out, ((1,), (0,)))
        if start == 0:
            key_grad_ref[...] = key_part
            value_grad_ref[...] = value_part
        else:
            key_grad_ref[...] += key_part
            value_grad_ref[...] += value_part
    cot_ref[1, 0] = key_grad_ref[...].astype(jnp.bfloat16)
    cot_ref[2, 0] = value_grad_ref[...].astype(jnp.bfloat16)


def attention(side, sides, kept, swapped, grad_out, groups):
    _, clips, length, _ = kept.shape
    block = math.gcd(length, 256)
    area = clips * length * length

    def spec(rows, columns):
        return pl.BlockSpec((1, rows, columns), lambda clip: (clip, 0, 0))

    triple = pl.BlockSpec((3, 1, length, HEAD), lambda clip: (0, clip, 0, 0))
    return pl.pallas_call(
        lambda *refs: attention_kernel(block, sides, *refs),
        grid=(clips,),
        in_specs=[
            pl.BlockSpec(memory_space=pltpu.SMEM),
            triple, triple, spec(length, HEAD), spec(8, length), spec(length, HEAD),
        ],
        out_specs=[spec(length, HEAD), triple],
        out_shape=[
            jax.ShapeDtypeStruct((clips, length, HEAD), jnp.bfloat16),
            jax.ShapeDtypeStruct((3, clips, length, HEAD), jnp.bfloat16),
        ],
        scratch_shapes=[pltpu.VMEM((3, length, HEAD), jnp.bfloat16)] * 2
        + [pltpu.VMEM((length, HEAD), jnp.float32)] * 2,
        compiler_params=pltpu.CompilerParams(vmem_limit_bytes=60 * 1024 * 1024),
        cost_estimate=pl.CostEstimate(
            flops=18 * area * HEAD,
            bytes_accessed=20 * clips * length * HEAD,
            transcendentals=2 * area,
        ),
        name="attention",
    )(side.reshape(1), kept, swapped, grad_out, *groups)


def per_device(latents, noise, noise_level, group_index, projections, upstream):
    planes = lax.axis_size("fsdp")
    sides = lax.axis_size("mesh")
    lanes = lax.axis_size("seq")
    plane = lax.axis_index("fsdp")
    side = lax.axis_index("mesh")
    lane = lax.axis_index("seq")
    cores = 2 if lanes % 2 == 0 else 1
    chips = lanes // cores
    order = [(sides, side), (chips, lane // cores), (cores, lane % cores)]
    first_side = side == 0
    swap = [(0, 1), (1, 0)]

    rows, _, head_cols = projections.shape[1:]
    length = group_index.shape[1]
    heads = head_cols // HEAD
    pairs = (heads + 1) // 2
    shard_rows = rows // sides

    piece = latents.shape[1] // lanes
    own_rows = lax.dynamic_slice_in_dim(latents[0], lane * piece, piece, 0)
    own_noise = lax.dynamic_slice_in_dim(noise[0], lane * piece, piece, 0)
    noise_rate = noise_level[0]
    noised = (
        (1.0 - noise_rate) * own_rows.astype(jnp.float32)
        + noise_rate * own_noise.astype(jnp.float32)
    ).astype(jnp.bfloat16)

    def exchanged(blocks):
        found = []
        for d in range(planes):
            to = lax.rem(plane + planes - d, planes)
            block = lax.dynamic_index_in_dim(blocks, to, 1, False)
            found.append(shifted_by(block, "fsdp", d, 1, planes) if d else block)
        found = turned(jnp.stack(found), 0, planes - plane)
        return found.reshape(planes, piece, rows)

    def gathered(clips):
        found = clips[: planes // 2], clips[planes // 2 :]
        for step in range(3):
            found = gather_step(step, found, sides, chips, cores)
        return found

    tokens = jnp.concatenate(gathered(exchanged(noised.reshape(piece, planes, rows))))

    sums = []
    for j in range(pairs):
        factors = projections[0, :, :, 2 * j * HEAD : 2 * (j + 1) * HEAD]
        part = dots(tokens, factors, ((1,), (0,))).astype(jnp.bfloat16)
        part = part.reshape(planes, length, 3, -1).swapaxes(1, 2)
        sums.append(lax.psum_scatter(part, "fsdp", scatter_dimension=0, tiled=True)[0])

    tokens, noised = lax.optimization_barrier((tokens, noised))
    columns = noised.reshape(piece, sides, planes, shard_rows).swapaxes(1, 2)
    columns = jnp.concatenate(gathered(exchanged(columns)))

    own_up = own_order(upstream[0], order)
    groups = own_order(group_index[0], order)
    groups = (
        jnp.broadcast_to(groups[None, None, :], (1, 8, length)),
        jnp.broadcast_to(groups[None, :, None], (1, length, HEAD)),
    )
    directions, cots = [], []
    for j in range(pairs):
        even, odd = sums[j][:, :, :HEAD], sums[j][:, :, -HEAD:]
        kept = jnp.where(first_side, even, odd)
        swapped = lax.ppermute(jnp.where(first_side, odd, even), "mesh", swap)
        kept_head = jnp.minimum(2 * j + side, heads - 1)
        grad_out = lax.dynamic_slice_in_dim(own_up, kept_head * HEAD, HEAD, 1)
        direction, cotangents = attention(
            side, sides, kept[:, None], swapped[:, None], grad_out[None], groups
        )
        directions.append(direction[0])
        cots.append(lax.all_gather(cotangents[:, 0], "fsdp", axis=0))

    local = jnp.concatenate(directions, axis=1)
    local = local.reshape(sides, chips, cores, -1, pairs * HEAD)
    axes = [("mesh", 1, sides), ("seq", cores, chips), ("seq", 1, cores)]
    for at, (axis, inner, outer) in enumerate(axes):
        blocks = [lax.index_in_dim(local, -d % outer, at, False) for d in range(outer)]
        for d in range(1, outer):
            blocks[d] = shifted_by(blocks[d], axis, d, inner, outer)
        local = jnp.stack(blocks, axis=at)
    local = own_order(local.reshape(sides * lanes, -1, pairs * HEAD), order, back=True)
    local = local.reshape(sides, lanes, -1, pairs, HEAD)
    local = jnp.transpose(local, (2, 1, 3, 0, 4)).reshape(-1, lanes, pairs * sides, HEAD)
    direction = local[:, :, :heads].reshape(1, -1, lanes * head_cols)

    summed = jnp.zeros((3, shard_rows, head_cols), jnp.float32)
    for j in range(pairs):
        grad = None
        for clip in range(planes):
            block = columns[clip * length : (clip + 1) * length]
            product = dots(block, cots[j][clip], ((0,), (1,)))
            grad = product if grad is None else grad + product
        grad = jnp.swapaxes(grad, 0, 1).reshape(3, sides, shard_rows, HEAD)
        own_grad = jnp.where(first_side, grad[:, 0], grad[:, 1])
        sent = jnp.where(first_side, grad[:, 1], grad[:, 0]).astype(jnp.bfloat16)
        other = lax.ppermute(sent, "mesh", swap).astype(jnp.float32)
        first = jnp.where(first_side, own_grad, other)
        second = jnp.where(first_side, other, own_grad)
        both = jnp.concatenate([first, second], axis=2)[:, :, : (heads - 2 * j) * HEAD]
        summed = lax.dynamic_update_slice(summed, both, (0, 0, 2 * j * HEAD))
    return (direction, jnp.swapaxes(summed, 0, 1))


def solution(mesh):
    in_specs = (
        P("fsdp", "mesh", None),
        P("fsdp", "mesh", None),
        P("fsdp"),
        P("fsdp", None),
        P("mesh", "fsdp", None, "seq"),
        P("fsdp", None, "seq"),
    )
    out_specs = (P("fsdp", ("mesh", "seq"), None), P(("mesh", "fsdp"), None, "seq"))
    return jax.shard_map(
        per_device, mesh=mesh, in_specs=in_specs, out_specs=out_specs, check_vma=False
    )
```

```python
import math

import jax
import jax.numpy as jnp
from jax import lax
from jax.experimental import pallas as pl
from jax.experimental.pallas import tpu as pltpu
from jax.sharding import PartitionSpec as P

HEAD = 128


def shifted_by(value, axis, d, inner=1, outer=1):
    pairs = []
    for i in range(lax.axis_size(axis)):
        place = i // inner % outer
        pairs.append((i + ((place + d) % outer - place) * inner, i))
    return lax.ppermute(value, axis, pairs)


def spread(value, axis, inner, outer, at):
    pieces = [value] + [shifted_by(value, axis, d, inner, outer) for d in range(1, outer)]
    return jnp.stack(pieces, axis=at)


def turned(value, at, start):
    size = value.shape[at]
    return lax.dynamic_slice_in_dim(jnp.concatenate([value, value], axis=at), start, size, at)


def own_order(value, factors, back=False):
    sizes = [size for size, _ in factors]
    parts = value.reshape(sizes + [-1] + list(value.shape[1:]))
    for at, (size, place) in enumerate(factors):
        parts = turned(parts, at, size - place if back else place)
    return parts.reshape(value.shape)


def gather_step(step, pair, sides, chips, cores):
    first, second = pair
    if step == 0:
        return spread(first, "mesh", 1, sides, 1), spread(second, "seq", cores, chips, 1)
    if step == 1:
        return spread(first, "seq", cores, chips, 2), spread(second, "mesh", 1, sides, 1)
    both = spread(jnp.stack([first, second]), "seq", 1, cores, 4)
    both = both.reshape(2, -1, both.shape[-1])
    return both[0], both[1]


def dots(left, right, dims):
    return lax.dot_general(left, right, (dims, ((), ())), preferred_element_type=jnp.float32)


def attention_kernel(
    block, sides, side_ref, kept_ref, swapped_ref, up_ref, key_group_ref, group_ref,
    direction_ref, cot_ref, teacher_ref, fake_ref, key_grad_ref, value_grad_ref,
):
    length = kept_ref.shape[2]
    span = length // sides
    score_scale = 1.0 / math.sqrt(HEAD)
    first_side = side_ref[0] == 0
    for at in range(sides):
        here = pl.ds(at * span, span)
        there = pl.ds((sides - 1 - at) * span, span)
        kept, swapped = kept_ref[:, 0, here, :], swapped_ref[:, 0, there, :]
        teacher_ref[:, here, :] = jnp.where(first_side, kept, swapped)
        fake_ref[:, here, :] = jnp.where(first_side, swapped, kept)

    def softmax(triple_ref, rows, visible):
        scores = dots(triple_ref[0, rows, :], triple_ref[1], ((1,), (1,)))
        scores = jnp.where(visible, scores * score_scale, jnp.float32(-1e30))
        weights = jnp.exp(scores - jnp.max(scores, axis=-1, keepdims=True))
        return weights * (1.0 / jnp.sum(weights, axis=-1, keepdims=True))

    for start in range(0, length, block):
        rows = pl.ds(start, block)
        visible = key_group_ref[0, :1, :] <= group_ref[0, rows, :1]
        prob_low = softmax(teacher_ref, rows, visible).astype(jnp.bfloat16)
        teacher_out = dots(prob_low, teacher_ref[2], ((1,), (0,))).astype(jnp.bfloat16)
        probabilities = softmax(fake_ref, rows, visible)
        prob_low = probabilities.astype(jnp.bfloat16)
        values = fake_ref[2]
        fake_out = dots(prob_low, values, ((1,), (0,))).astype(jnp.bfloat16)
        direction_ref[0, rows, :] = (
            fake_out.astype(jnp.float32) - teacher_out.astype(jnp.float32)
        ).astype(jnp.bfloat16)
        grad_out = up_ref[0, rows, :]
        prob_grad = dots(grad_out, values, ((1,), (1,)))
        row_inner = jnp.sum(probabilities * prob_grad, axis=-1, keepdims=True)
        score_grad = probabilities * (prob_grad - row_inner) * score_scale
        query_grad = dots(score_grad.astype(jnp.bfloat16), fake_ref[1], ((1,), (0,)))
        cot_ref[0, 0, rows, :] = query_grad.astype(jnp.bfloat16)
        score_grad = jnp.transpose(score_grad).astype(jnp.bfloat16)
        key_part = dots(score_grad, fake_ref[0, rows, :], ((1,), (0,)))
        prob_low = jnp.transpose(probabilities).astype(jnp.bfloat16)
        value_part = dots(prob_low, grad_out, ((1,), (0,)))
        if start == 0:
            key_grad_ref[...] = key_part
            value_grad_ref[...] = value_part
        else:
            key_grad_ref[...] += key_part
            value_grad_ref[...] += value_part
    cot_ref[1, 0] = key_grad_ref[...].astype(jnp.bfloat16)
    cot_ref[2, 0] = value_grad_ref[...].astype(jnp.bfloat16)


def attention(side, sides, kept, swapped, grad_out, groups):
    _, clips, length, _ = kept.shape
    block = math.gcd(length, 256)
    area = clips * length * length

    def spec(rows, columns):
        return pl.BlockSpec((1, rows, columns), lambda clip: (clip, 0, 0))

    triple = pl.BlockSpec((3, 1, length, HEAD), lambda clip: (0, clip, 0, 0))
    return pl.pallas_call(
        lambda *refs: attention_kernel(block, sides, *refs),
        grid=(clips,),
        in_specs=[
            pl.BlockSpec(memory_space=pltpu.SMEM),
            triple, triple, spec(length, HEAD), spec(8, length), spec(length, HEAD),
        ],
        out_specs=[spec(length, HEAD), triple],
        out_shape=[
            jax.ShapeDtypeStruct((clips, length, HEAD), jnp.bfloat16),
            jax.ShapeDtypeStruct((3, clips, length, HEAD), jnp.bfloat16),
        ],
        scratch_shapes=[pltpu.VMEM((3, length, HEAD), jnp.bfloat16)] * 2
        + [pltpu.VMEM((length, HEAD), jnp.float32)] * 2,
        compiler_params=pltpu.CompilerParams(vmem_limit_bytes=60 * 1024 * 1024),
        cost_estimate=pl.CostEstimate(
            flops=18 * area * HEAD,
            bytes_accessed=20 * clips * length * HEAD,
            transcendentals=2 * area,
        ),
        name="attention",
    )(side.reshape(1), kept, swapped, grad_out, *groups)


def per_device(latents, noise, noise_level, group_index, projections, upstream):
    planes = lax.axis_size("fsdp")
    sides = lax.axis_size("mesh")
    lanes = lax.axis_size("seq")
    plane = lax.axis_index("fsdp")
    side = lax.axis_index("mesh")
    lane = lax.axis_index("seq")
    cores = 2 if lanes % 2 == 0 else 1
    chips = lanes // cores
    order = [(sides, side), (chips, lane // cores), (cores, lane % cores)]
    first_side = side == 0
    swap = [(0, 1), (1, 0)]

    rows, _, head_cols = projections.shape[1:]
    length = group_index.shape[1]
    heads = head_cols // HEAD
    pairs = (heads + 1) // 2
    shard_rows = rows // sides

    piece = latents.shape[1] // lanes
    own_rows = lax.dynamic_slice_in_dim(latents[0], lane * piece, piece, 0)
    own_noise = lax.dynamic_slice_in_dim(noise[0], lane * piece, piece, 0)
    noise_rate = noise_level[0]
    noised = (
        (1.0 - noise_rate) * own_rows.astype(jnp.float32)
        + noise_rate * own_noise.astype(jnp.float32)
    ).astype(jnp.bfloat16)

    def exchanged(blocks, in_order):
        found = []
        for d in range(planes):
            to = lax.rem(plane + planes - d, planes)
            block = lax.dynamic_index_in_dim(blocks, to, 1, False)
            found.append(shifted_by(block, "fsdp", d, 1, planes) if d else block)
        found = jnp.stack(found)
        if in_order:
            found = turned(found, 0, planes - plane)
        return found.reshape(planes, piece, rows)

    def lined_up(value):
        right, left = [value], [value]
        for _ in range(planes - 1):
            right.append(lax.ppermute(right[-1], "fsdp", [(p, p + 1) for p in range(planes - 1)]))
            left.append(lax.ppermute(left[-1], "fsdp", [(p + 1, p) for p in range(planes - 1)]))
        return [value] + [
            jnp.where(plane + d < planes, left[d], right[planes - d]) for d in range(1, planes)
        ]

    def gathered(clips):
        found = clips[: planes // 2], clips[planes // 2 :]
        for step in range(3):
            found = gather_step(step, found, sides, chips, cores)
        return found

    tokens = jnp.concatenate(gathered(exchanged(noised.reshape(piece, planes, rows), True)))

    sums = []
    for j in range(pairs):
        factors = projections[0, :, :, 2 * j * HEAD : 2 * (j + 1) * HEAD]
        part = dots(tokens, factors, ((1,), (0,))).astype(jnp.bfloat16)
        part = part.reshape(planes, length, 3, -1).swapaxes(1, 2)
        sums.append(lax.psum_scatter(part, "fsdp", scatter_dimension=0, tiled=True)[0])

    tokens, noised = lax.optimization_barrier((tokens, noised))
    columns = noised.reshape(piece, sides, planes, shard_rows).swapaxes(1, 2)
    columns = jnp.concatenate(gathered(exchanged(columns, False)))

    def settled(summed, j, own_grad, other):
        other = other.astype(jnp.float32)
        first = jnp.where(first_side, own_grad, other)
        second = jnp.where(first_side, other, own_grad)
        both = jnp.concatenate([first, second], axis=2)[:, :, : (heads - 2 * j) * HEAD]
        return lax.dynamic_update_slice(summed, both, (0, 0, 2 * j * HEAD))

    own_up = own_order(upstream[0], order)
    groups = own_order(group_index[0], order)
    groups = (
        jnp.broadcast_to(groups[None, None, :], (1, 8, length)),
        jnp.broadcast_to(groups[None, :, None], (1, length, HEAD)),
    )
    summed = jnp.zeros((3, shard_rows, head_cols), jnp.float32)
    directions, done = [], []
    for j in range(pairs):
        (even, odd), done = lax.optimization_barrier(
            ((sums[j][:, :, :HEAD], sums[j][:, :, -HEAD:]), done)
        )
        kept = jnp.where(first_side, even, odd)
        swapped = lax.ppermute(jnp.where(first_side, odd, even), "mesh", swap)
        if done:
            summed = settled(summed, j - 1, *done)
        kept_head = jnp.minimum(2 * j + side, heads - 1)
        grad_out = lax.dynamic_slice_in_dim(own_up, kept_head * HEAD, HEAD, 1)
        direction, cotangents = attention(
            side, sides, kept[:, None], swapped[:, None], grad_out[None], groups
        )
        directions.append(direction[0])
        grad = None
        for clip, cot in enumerate(lined_up(cotangents[:, 0])):
            block = columns[clip * length : (clip + 1) * length]
            product = dots(block, cot, ((0,), (1,)))
            grad = product if grad is None else grad + product
        grad = jnp.swapaxes(grad, 0, 1).reshape(3, sides, shard_rows, HEAD)
        own_grad = jnp.where(first_side, grad[:, 0], grad[:, 1])
        sent = jnp.where(first_side, grad[:, 1], grad[:, 0]).astype(jnp.bfloat16)
        done = [own_grad, lax.ppermute(sent, "mesh", swap)]
    summed = settled(summed, pairs - 1, *done)

    local = jnp.concatenate(directions, axis=1)
    local = local.reshape(sides, chips, cores, -1, pairs * HEAD)
    axes = [("mesh", 1, sides), ("seq", cores, chips), ("seq", 1, cores)]
    for at, (axis, inner, outer) in enumerate(axes):
        blocks = [lax.index_in_dim(local, -d % outer, at, False) for d in range(outer)]
        for d in range(1, outer):
            blocks[d] = shifted_by(blocks[d], axis, d, inner, outer)
        local = jnp.stack(blocks, axis=at)
    local = own_order(local.reshape(sides * lanes, -1, pairs * HEAD), order, back=True)
    local = local.reshape(sides, lanes, -1, pairs, HEAD)
    local = jnp.transpose(local, (2, 1, 3, 0, 4)).reshape(-1, lanes, pairs * sides, HEAD)
    direction = local[:, :, :heads].reshape(1, -1, lanes * head_cols)

    return (direction, jnp.swapaxes(summed, 0, 1))


def solution(mesh):
    in_specs = (
        P("fsdp", "mesh", None),
        P("fsdp", "mesh", None),
        P("fsdp"),
        P("fsdp", None),
        P("mesh", "fsdp", None, "seq"),
        P("fsdp", None, "seq"),
    )
    out_specs = (P("fsdp", ("mesh", "seq"), None), P(("mesh", "fsdp"), None, "seq"))
    return jax.shard_map(
        per_device, mesh=mesh, in_specs=in_specs, out_specs=out_specs, check_vma=False
    )
```

```python
import math

import jax
import jax.numpy as jnp
from jax import lax
from jax.experimental import pallas as pl
from jax.experimental.pallas import tpu as pltpu
from jax.sharding import PartitionSpec as P

HEAD = 128


def shifted_by(value, axis, d, inner=1, outer=1):
    pairs = []
    for i in range(lax.axis_size(axis)):
        place = i // inner % outer
        pairs.append((i + ((place + d) % outer - place) * inner, i))
    return lax.ppermute(value, axis, pairs)


def spread(value, axis, inner, outer, at):
    pieces = [value] + [shifted_by(value, axis, d, inner, outer) for d in range(1, outer)]
    return jnp.stack(pieces, axis=at)


def turned(value, at, start):
    size = value.shape[at]
    return lax.dynamic_slice_in_dim(jnp.concatenate([value, value], axis=at), start, size, at)


def own_order(value, factors, back=False):
    sizes = [size for size, _ in factors]
    parts = value.reshape(sizes + [-1] + list(value.shape[1:]))
    for at, (size, place) in enumerate(factors):
        parts = turned(parts, at, size - place if back else place)
    return parts.reshape(value.shape)


def gather_step(step, pair, sides, chips, cores):
    first, second = pair
    if step == 0:
        return spread(first, "mesh", 1, sides, 1), spread(second, "seq", cores, chips, 1)
    if step == 1:
        return spread(first, "seq", cores, chips, 2), spread(second, "mesh", 1, sides, 1)
    both = spread(jnp.stack([first, second]), "seq", 1, cores, 4)
    both = both.reshape(2, -1, both.shape[-1])
    return both[0], both[1]


def dots(left, right, dims):
    return lax.dot_general(left, right, (dims, ((), ())), preferred_element_type=jnp.float32)


def attention_kernel(
    block, sides, side_ref, kept_ref, swapped_ref, up_ref, key_group_ref, group_ref,
    direction_ref, cot_ref, teacher_ref, fake_ref, key_grad_ref, value_grad_ref,
):
    length = kept_ref.shape[1]
    span = length // sides
    score_scale = 1.0 / math.sqrt(HEAD)
    first_side = side_ref[0] == 0
    for at in range(sides):
        here = pl.ds(at * span, span)
        there = pl.ds((sides - 1 - at) * span, span)
        kept, swapped = kept_ref[0, here, :], swapped_ref[0, there, :]
        teacher_ref[here, :] = jnp.where(first_side, kept, swapped)
        fake_ref[here, :] = jnp.where(first_side, swapped, kept)
    queries, key_rows, values = (pl.ds(at * HEAD, HEAD) for at in range(3))

    def softmax(triple_ref, rows, visible):
        scores = dots(triple_ref[rows, queries], triple_ref[:, key_rows], ((1,), (1,)))
        scores = jnp.where(visible, scores * score_scale, jnp.float32(-1e30))
        weights = jnp.exp(scores - jnp.max(scores, axis=-1, keepdims=True))
        return weights * (1.0 / jnp.sum(weights, axis=-1, keepdims=True))

    for start in range(0, length, block):
        rows = pl.ds(start, block)
        visible = key_group_ref[0, :1, :] <= group_ref[0, rows, :1]
        prob_low = softmax(teacher_ref, rows, visible).astype(jnp.bfloat16)
        teacher_out = dots(prob_low, teacher_ref[:, values], ((1,), (0,))).astype(jnp.bfloat16)
        probabilities = softmax(fake_ref, rows, visible)
        prob_low = probabilities.astype(jnp.bfloat16)
        fake_out = dots(prob_low, fake_ref[:, values], ((1,), (0,))).astype(jnp.bfloat16)
        direction_ref[0, rows, :] = (
            fake_out.astype(jnp.float32) - teacher_out.astype(jnp.float32)
        ).astype(jnp.bfloat16)
        grad_out = up_ref[0, rows, :]
        prob_grad = dots(grad_out, fake_ref[:, values], ((1,), (1,)))
        row_inner = jnp.sum(probabilities * prob_grad, axis=-1, keepdims=True)
        score_grad = probabilities * (prob_grad - row_inner) * score_scale
        query_grad = dots(score_grad.astype(jnp.bfloat16), fake_ref[:, key_rows], ((1,), (0,)))
        cot_ref[0, 0, rows, :] = query_grad.astype(jnp.bfloat16)
        score_grad = jnp.transpose(score_grad).astype(jnp.bfloat16)
        key_part = dots(score_grad, fake_ref[rows, queries], ((1,), (0,)))
        prob_low = jnp.transpose(probabilities).astype(jnp.bfloat16)
        value_part = dots(prob_low, grad_out, ((1,), (0,)))
        if start == 0:
            key_grad_ref[...] = key_part
            value_grad_ref[...] = value_part
        else:
            key_grad_ref[...] += key_part
            value_grad_ref[...] += value_part
    cot_ref[1, 0] = key_grad_ref[...].astype(jnp.bfloat16)
    cot_ref[2, 0] = value_grad_ref[...].astype(jnp.bfloat16)


def attention(side, sides, kept, swapped, grad_out, groups):
    clips, length, width = kept.shape
    block = math.gcd(length, 256)
    area = clips * length * length

    def spec(rows, columns):
        return pl.BlockSpec((1, rows, columns), lambda clip: (clip, 0, 0))

    triple = spec(length, width)
    return pl.pallas_call(
        lambda *refs: attention_kernel(block, sides, *refs),
        grid=(clips,),
        in_specs=[
            pl.BlockSpec(memory_space=pltpu.SMEM),
            triple, triple, spec(length, HEAD), spec(8, length), spec(length, HEAD),
        ],
        out_specs=[
            spec(length, HEAD),
            pl.BlockSpec((3, 1, length, HEAD), lambda clip: (0, clip, 0, 0)),
        ],
        out_shape=[
            jax.ShapeDtypeStruct((clips, length, HEAD), jnp.bfloat16),
            jax.ShapeDtypeStruct((3, clips, length, HEAD), jnp.bfloat16),
        ],
        scratch_shapes=[pltpu.VMEM((length, width), jnp.bfloat16)] * 2
        + [pltpu.VMEM((length, HEAD), jnp.float32)] * 2,
        compiler_params=pltpu.CompilerParams(vmem_limit_bytes=16 * 1024 * 1024),
        cost_estimate=pl.CostEstimate(
            flops=18 * area * HEAD,
            bytes_accessed=20 * clips * length * HEAD,
            transcendentals=2 * area,
        ),
        name="attention",
    )(side.reshape(1), kept, swapped, grad_out, *groups)


def per_device(latents, noise, noise_level, group_index, projections, upstream):
    planes = lax.axis_size("fsdp")
    sides = lax.axis_size("mesh")
    lanes = lax.axis_size("seq")
    plane = lax.axis_index("fsdp")
    side = lax.axis_index("mesh")
    lane = lax.axis_index("seq")
    half = planes // 2
    chains = 2 if half % 2 == 0 else 1
    share = half // chains
    cores = 2 if lanes % 2 == 0 else 1
    chips = lanes // cores
    order = [(sides, side), (chips, lane // cores), (cores, lane % cores)]
    low_half = plane < half
    first_side = side == 0
    distance = jnp.minimum(plane, planes - 1 - plane)
    swap = [(0, 1), (1, 0)]

    rows, _, head_cols = projections.shape[1:]
    length = group_index.shape[1]
    heads = head_cols // HEAD
    pairs = (heads + 1) // 2
    shard_rows = rows // sides

    def hop_pairs(hop):
        return [(hop - 1, hop), (planes - hop, planes - 1 - hop)]

    def send_hops(values):
        sent = {}
        for parity in range(2):
            hops = [hop for hop in sorted(values) if hop % 2 == parity]
            if not hops:
                continue
            value = values[hops[-1]]
            for hop in hops[-2::-1]:
                here = (plane == hop - 1) | (plane == planes - hop)
                value = jnp.where(here, values[hop], value)
            sent[parity] = lax.ppermute(value, "fsdp", sum([hop_pairs(h) for h in hops], []))
        return sent

    def pick(by_distance):
        picked = by_distance[-1]
        for d in range(len(by_distance) - 2, -1, -1):
            picked = jnp.where(distance == d, by_distance[d], picked)
        return picked

    piece = latents.shape[1] // lanes
    own_rows = lax.dynamic_slice_in_dim(latents[0], lane * piece, piece, 0)
    own_noise = lax.dynamic_slice_in_dim(noise[0], lane * piece, piece, 0)
    noise_rate = noise_level[0]
    noised = (
        (1.0 - noise_rate) * own_rows.astype(jnp.float32)
        + noise_rate * own_noise.astype(jnp.float32)
    ).astype(jnp.bfloat16)

    def exchanged(blocks):
        found = []
        for d in range(planes):
            to = lax.rem(plane + planes - d, planes)
            block = lax.dynamic_index_in_dim(blocks, to, 1, False)
            found.append(shifted_by(block, "fsdp", d, 1, planes) if d else block)
        found = [block.reshape(piece, rows) for block in found]
        near, far = [], []
        for k in range(half):
            for side_of, mirrored in ((near, False), (far, True)):
                picked = None
                for p in range(planes):
                    clip = k if (p < half) != mirrored else planes - 1 - k
                    block = found[(clip - p) % planes]
                    picked = block if picked is None else jnp.where(plane == p, block, picked)
                side_of.append(picked)
        return jnp.stack(near), jnp.stack(far)

    tokens = exchanged(noised.reshape(piece, planes, rows))
    tokens = gather_step(0, tokens, sides, chips, cores)
    factors = jnp.transpose(projections[0].reshape(rows, 3, heads, HEAD), (2, 0, 1, 3))
    factors = factors.reshape(heads, rows, 3 * HEAD)
    tokens, factors = lax.optimization_barrier((tokens, factors))
    for step in range(1, 3):
        tokens = gather_step(step, tokens, sides, chips, cores)

    def collected(value):
        found = [value]
        for k in range(1, half):
            found.append(lax.ppermute(value, "fsdp", [(k, 0), (planes - 1 - k, planes - 1)]))
        return found

    ready = [min(2 * j + 1, heads - 1) + planes - 1 for j in range(pairs)]
    leaves = []
    for j in range(pairs):
        leaves.append(max([ready[j] + 1, heads] + [stage + 1 for stage in leaves[-1:]]))
    stages = leaves[-1] + planes

    pending = [{} for _ in range(chains)]
    finals = [{} for _ in range(chains)]
    passed = [[[] for _ in range(pairs)] for _ in range(chains)]
    directions = [[] for _ in range(chains)]
    clip_directions = []
    sums = [None] * pairs
    size = share * length

    def own_tokens(chain):
        return [side_of[chain * size : (chain + 1) * size] for side_of in tokens]

    def product(chain, is_far, head):
        return dots(own_tokens(chain)[is_far], factors[head], ((1,), (0,)))

    parts = [{(1, 0): product(chain, 1, 0)} for chain in range(chains)]
    (own_up, noised), parts = lax.optimization_barrier(((upstream[0], noised), parts))
    own_up = own_order(own_up, order)
    kept_heads = [jnp.minimum(2 * j + side, heads - 1) for j in range(pairs)]
    ups = collected(
        jnp.stack([lax.dynamic_slice_in_dim(own_up, h * HEAD, HEAD, 1) for h in kept_heads])
    )
    groups = collected(own_order(group_index[0], order))
    summed = [jnp.zeros((3, shard_rows, head_cols), jnp.float32)]

    def settle(j, own_grad, other):
        head = 2 * j
        other = other.astype(jnp.float32)
        first = jnp.where(first_side, own_grad, other)
        second = jnp.where(first_side, other, own_grad)
        both = jnp.concatenate([first, second], axis=2)[:, :, : (heads - head) * HEAD]
        summed[0] = lax.dynamic_update_slice(summed[0], both, (0, 0, head * HEAD))

    for stage in range(stages):
        for chain in range(chains):
            arrived, tokens = lax.optimization_barrier((pending[chain], tokens))
            coming = {}
            parts[chain].update(arrived.get("parts", {}))
            coming["parts"] = {
                (is_far, head): product(chain, is_far, head)
                for is_far, head in ((1, stage + 1), (0, stage + 1 - half))
                if 0 <= head < heads
            }
            for j, returned in arrived.get("other", {}).items():
                settle(j, *returned)
            values = {}
            for hop in range(1, planes + 1):
                head = stage - hop + 1
                if not 0 <= head < heads:
                    continue
                total = parts[chain][hop <= half, head]
                if hop > 1:
                    total = total + arrived["sums"][(hop - 1) % 2].astype(jnp.float32)
                values[hop] = total.astype(jnp.bfloat16)
            done = values.pop(planes, None)
            if values:
                coming["sums"] = send_hops(values)
            if done is not None:
                finals[chain][stage - planes + 1] = done
            if chain == chains - 1 and stage == 0:
                columns = noised.reshape(piece, sides, planes, shard_rows)
                coming["columns"] = exchanged(columns.swapaxes(1, 2))
                coming["ups"], coming["groups"] = ups, groups
            if chain == chains - 1 and stage == 1:
                ups, groups = arrived["ups"], arrived["groups"]
                group_forms = []
                for at in range(chains):
                    own = jnp.stack(groups[at * share : (at + 1) * share])
                    group_forms.append(
                        (
                            jnp.broadcast_to(own[:, None, :], (share, 8, length)),
                            jnp.broadcast_to(own[:, :, None], (share, length, HEAD)),
                        )
                    )
            if chain == chains - 1 and 1 <= stage <= 3:
                coming["columns"] = gather_step(
                    stage - 1, arrived["columns"], sides, chips, cores
                )
            if chain == chains - 1 and stage == 4:
                columns = arrived["columns"]
            for j in range(pairs):
                if stage == ready[j]:
                    even, odd = finals[chain][2 * j], finals[chain][min(2 * j + 1, heads - 1)]
                    kept = jnp.where(first_side, even, odd)
                    sent = jnp.where(first_side, odd, even)
                    coming["swapped"] = (kept, lax.ppermute(sent, "mesh", swap))
                if stage == ready[j] + 1:
                    kept, swapped = arrived["swapped"]
                    members = range(chain * share, (chain + 1) * share)
                    direction, cotangents = attention(
                        side,
                        sides,
                        kept.reshape(share, length, 3 * HEAD),
                        swapped.reshape(share, length, 3 * HEAD),
                        jnp.stack([ups[k][j] for k in members]),
                        group_forms[chain],
                    )
                    passed[chain][j].append(cotangents.reshape(3, size, HEAD))
                    directions[chain].append(direction)
                    if j < pairs - 1:
                        continue
                    joined = jnp.concatenate(directions[chain], axis=2)
                    coming["directions"] = []
                    for k in members:
                        moved = joined[k - chain * share]
                        if k > 0:
                            hops = [(0, k), (planes - 1, planes - 1 - k)]
                            moved = lax.ppermute(moved, "fsdp", hops)
                        coming["directions"].append(moved)
            if stage == ready[-1] + 2:
                clip_directions.extend(arrived["directions"])
            values = {}
            for j in range(pairs):
                hop = stage - leaves[j]
                if 1 <= hop < planes:
                    passed[chain][j].append(arrived["cots"][hop % 2])
                if 0 <= hop < planes - 1:
                    values[hop + 1] = passed[chain][j][hop]
            if values:
                coming["cots"] = send_hops(values)
            for j in range(pairs):
                late = j < pairs - 1
                if late and stage == leaves[j] + planes - 1:
                    coming["passed"] = passed[chain][j]
                if stage != leaves[j] + planes - 1 + late:
                    continue
                all_hops = arrived["passed"] if late else passed[chain][j]
                for is_far in range(2):
                    hops = all_hops[::-1] if is_far else all_hops
                    block = columns[is_far][chain * size : (chain + 1) * size]
                    added = dots(block, pick(hops[:half]), ((0,), (1,)))
                    sums[j] = added if sums[j] is None else sums[j] + added
                if chain < chains - 1:
                    continue
                grad = jnp.swapaxes(sums[j], 0, 1).reshape(3, sides, shard_rows, HEAD)
                own_grad = jnp.where(first_side, grad[:, 0], grad[:, 1])
                sent = jnp.where(first_side, grad[:, 1], grad[:, 0]).astype(jnp.bfloat16)
                returned = (own_grad, lax.ppermute(sent, "mesh", swap))
                coming.setdefault("other", {})[j] = returned
            pending[chain] = coming
        if stage == ready[-1] + 2:
            local = pick(clip_directions)
            local = local.reshape(sides, chips, cores, -1, pairs * HEAD)
            axes = [("mesh", 1, sides), ("seq", cores, chips), ("seq", 1, cores)]
            for at, (axis, inner, outer) in enumerate(axes):
                blocks = [lax.index_in_dim(local, -d % outer, at, False) for d in range(outer)]
                for d in range(1, outer):
                    blocks[d] = shifted_by(blocks[d], axis, d, inner, outer)
                local = jnp.stack(blocks, axis=at)
            local = own_order(local.reshape(sides * lanes, -1, pairs * HEAD), order, back=True)
    for j, returned in pending[-1]["other"].items():
        settle(j, *returned)
    summed = jnp.swapaxes(summed[0], 0, 1)

    local = local.reshape(sides, lanes, -1, pairs, HEAD)
    local = jnp.transpose(local, (2, 1, 3, 0, 4)).reshape(-1, lanes, pairs * sides, HEAD)
    direction = local[:, :, :heads].reshape(1, -1, lanes * head_cols)
    return (direction, summed)


def solution(mesh):
    in_specs = (
        P("fsdp", "mesh", None),
        P("fsdp", "mesh", None),
        P("fsdp"),
        P("fsdp", None),
        P("mesh", "fsdp", None, "seq"),
        P("fsdp", None, "seq"),
    )
    out_specs = (P("fsdp", ("mesh", "seq"), None), P(("mesh", "fsdp"), None, "seq"))
    return jax.shard_map(
        per_device, mesh=mesh, in_specs=in_specs, out_specs=out_specs, check_vma=False
    )
```

```python
import math

import jax
import jax.numpy as jnp
from jax import lax
from jax.experimental import pallas as pl
from jax.experimental.pallas import tpu as pltpu
from jax.sharding import PartitionSpec as P

HEAD = 128


def shifted_by(value, axis, d, inner=1, outer=1):
    pairs = []
    for i in range(lax.axis_size(axis)):
        place = i // inner % outer
        pairs.append((i + ((place + d) % outer - place) * inner, i))
    return lax.ppermute(value, axis, pairs)


def spread(value, axis, inner, outer, at):
    pieces = [value] + [shifted_by(value, axis, d, inner, outer) for d in range(1, outer)]
    return jnp.stack(pieces, axis=at)


def turned(value, at, start):
    size = value.shape[at]
    return lax.dynamic_slice_in_dim(jnp.concatenate([value, value], axis=at), start, size, at)


def own_order(value, factors, back=False):
    sizes = [size for size, _ in factors]
    parts = value.reshape(sizes + [-1] + list(value.shape[1:]))
    for at, (size, place) in enumerate(factors):
        parts = turned(parts, at, size - place if back else place)
    return parts.reshape(value.shape)


def gather_step(step, pair, sides, chips, cores):
    first, second = pair
    if step == 0:
        return spread(first, "mesh", 1, sides, 1), spread(second, "seq", cores, chips, 1)
    if step == 1:
        return spread(first, "seq", cores, chips, 2), spread(second, "mesh", 1, sides, 1)
    both = spread(jnp.stack([first, second]), "seq", 1, cores, 4)
    both = both.reshape(2, -1, both.shape[-1])
    return both[0], both[1]


def dots(left, right, dims):
    return lax.dot_general(left, right, (dims, ((), ())), preferred_element_type=jnp.float32)


def attention_kernel(
    block, sides, side_ref, kept_ref, swapped_ref, up_ref, key_group_ref, group_ref,
    direction_ref, cot_ref, teacher_ref, fake_ref, key_grad_ref, value_grad_ref,
):
    length = kept_ref.shape[1]
    span = length // sides
    score_scale = 1.0 / math.sqrt(HEAD)
    first_side = side_ref[0] == 0
    for at in range(sides):
        here = pl.ds(at * span, span)
        there = pl.ds((sides - 1 - at) * span, span)
        kept, swapped = kept_ref[0, here, :], swapped_ref[0, there, :]
        teacher_ref[here, :] = jnp.where(first_side, kept, swapped)
        fake_ref[here, :] = jnp.where(first_side, swapped, kept)
    queries, key_rows, values = (pl.ds(at * HEAD, HEAD) for at in range(3))

    def softmax(triple_ref, rows, visible):
        scores = dots(triple_ref[rows, queries], triple_ref[:, key_rows], ((1,), (1,)))
        scores = jnp.where(visible, scores * score_scale, jnp.float32(-1e30))
        weights = jnp.exp(scores - jnp.max(scores, axis=-1, keepdims=True))
        return weights * (1.0 / jnp.sum(weights, axis=-1, keepdims=True))

    for start in range(0, length, block):
        rows = pl.ds(start, block)
        visible = key_group_ref[0, :1, :] <= group_ref[0, rows, :1]
        prob_low = softmax(teacher_ref, rows, visible).astype(jnp.bfloat16)
        teacher_out = dots(prob_low, teacher_ref[:, values], ((1,), (0,))).astype(jnp.bfloat16)
        probabilities = softmax(fake_ref, rows, visible)
        prob_low = probabilities.astype(jnp.bfloat16)
        fake_out = dots(prob_low, fake_ref[:, values], ((1,), (0,))).astype(jnp.bfloat16)
        direction_ref[0, rows, :] = (
            fake_out.astype(jnp.float32) - teacher_out.astype(jnp.float32)
        ).astype(jnp.bfloat16)
        grad_out = up_ref[0, rows, :]
        prob_grad = dots(grad_out, fake_ref[:, values], ((1,), (1,)))
        row_inner = jnp.sum(probabilities * prob_grad, axis=-1, keepdims=True)
        score_grad = probabilities * (prob_grad - row_inner) * score_scale
        query_grad = dots(score_grad.astype(jnp.bfloat16), fake_ref[:, key_rows], ((1,), (0,)))
        cot_ref[0, 0, rows, :] = query_grad.astype(jnp.bfloat16)
        score_grad = jnp.transpose(score_grad).astype(jnp.bfloat16)
        key_part = dots(score_grad, fake_ref[rows, queries], ((1,), (0,)))
        prob_low = jnp.transpose(probabilities).astype(jnp.bfloat16)
        value_part = dots(prob_low, grad_out, ((1,), (0,)))
        if start == 0:
            key_grad_ref[...] = key_part
            value_grad_ref[...] = value_part
        else:
            key_grad_ref[...] += key_part
            value_grad_ref[...] += value_part
    cot_ref[1, 0] = key_grad_ref[...].astype(jnp.bfloat16)
    cot_ref[2, 0] = value_grad_ref[...].astype(jnp.bfloat16)


def attention(side, sides, kept, swapped, grad_out, groups):
    clips, length, width = kept.shape
    block = math.gcd(length, 256)
    area = clips * length * length

    def spec(rows, columns):
        return pl.BlockSpec((1, rows, columns), lambda clip: (clip, 0, 0))

    triple = spec(length, width)
    return pl.pallas_call(
        lambda *refs: attention_kernel(block, sides, *refs),
        grid=(clips,),
        in_specs=[
            pl.BlockSpec(memory_space=pltpu.SMEM),
            triple, triple, spec(length, HEAD), spec(8, length), spec(length, HEAD),
        ],
        out_specs=[
            spec(length, HEAD),
            pl.BlockSpec((3, 1, length, HEAD), lambda clip: (0, clip, 0, 0)),
        ],
        out_shape=[
            jax.ShapeDtypeStruct((clips, length, HEAD), jnp.bfloat16),
            jax.ShapeDtypeStruct((3, clips, length, HEAD), jnp.bfloat16),
        ],
        scratch_shapes=[pltpu.VMEM((length, width), jnp.bfloat16)] * 2
        + [pltpu.VMEM((length, HEAD), jnp.float32)] * 2,
        compiler_params=pltpu.CompilerParams(vmem_limit_bytes=16 * 1024 * 1024),
        cost_estimate=pl.CostEstimate(
            flops=18 * area * HEAD,
            bytes_accessed=20 * clips * length * HEAD,
            transcendentals=2 * area,
        ),
        name="attention",
    )(side.reshape(1), kept, swapped, grad_out, *groups)


def per_device(latents, noise, noise_level, group_index, projections, upstream):
    planes = lax.axis_size("fsdp")
    sides = lax.axis_size("mesh")
    lanes = lax.axis_size("seq")
    plane = lax.axis_index("fsdp")
    side = lax.axis_index("mesh")
    lane = lax.axis_index("seq")
    half = planes // 2
    chains = 2 if half % 2 == 0 else 1
    share = half // chains
    cores = 2 if lanes % 2 == 0 else 1
    chips = lanes // cores
    order = [(sides, side), (chips, lane // cores), (cores, lane % cores)]
    low_half = plane < half
    first_side = side == 0
    distance = jnp.minimum(plane, planes - 1 - plane)
    swap = [(0, 1), (1, 0)]

    rows, _, head_cols = projections.shape[1:]
    length = group_index.shape[1]
    heads = head_cols // HEAD
    pairs = (heads + 1) // 2
    shard_rows = rows // sides

    def hop_pairs(hop):
        return [(hop - 1, hop), (planes - hop, planes - 1 - hop)]

    def send_hops(values):
        sent = {}
        for parity in range(2):
            hops = [hop for hop in sorted(values) if hop % 2 == parity]
            if not hops:
                continue
            value = values[hops[-1]]
            for hop in hops[-2::-1]:
                here = (plane == hop - 1) | (plane == planes - hop)
                value = jnp.where(here, values[hop], value)
            sent[parity] = lax.ppermute(value, "fsdp", sum([hop_pairs(h) for h in hops], []))
        return sent

    def pick(by_distance):
        picked = by_distance[-1]
        for d in range(len(by_distance) - 2, -1, -1):
            picked = jnp.where(distance == d, by_distance[d], picked)
        return picked

    piece = latents.shape[1] // lanes
    own_rows = lax.dynamic_slice_in_dim(latents[0], lane * piece, piece, 0)
    own_noise = lax.dynamic_slice_in_dim(noise[0], lane * piece, piece, 0)
    noise_rate = noise_level[0]
    noised = (
        (1.0 - noise_rate) * own_rows.astype(jnp.float32)
        + noise_rate * own_noise.astype(jnp.float32)
    ).astype(jnp.bfloat16)

    def block_from(blocks, d):
        to = lax.rem(plane + planes - d, planes)
        block = lax.dynamic_index_in_dim(blocks, to, 1, False)
        return shifted_by(block, "fsdp", d, 1, planes) if d else block

    def by_distance(found):
        found = [block.reshape(piece, rows) for block in found]
        near, far = [], []
        for k in range(half):
            for side_of, mirrored in ((near, False), (far, True)):
                picked = None
                for p in range(planes):
                    clip = k if (p < half) != mirrored else planes - 1 - k
                    block = found[(clip - p) % planes]
                    picked = block if picked is None else jnp.where(plane == p, block, picked)
                side_of.append(picked)
        return jnp.stack(near), jnp.stack(far)

    factors = jnp.transpose(projections[0].reshape(rows, 3, heads, HEAD), (2, 0, 1, 3))
    factors = factors.reshape(heads, rows, 3 * HEAD)
    blocks = noised.reshape(piece, planes, rows)
    found, factors = lax.optimization_barrier(
        ([block_from(blocks, d) for d in range(planes)], factors)
    )
    tokens = by_distance(found)
    for step in range(3):
        tokens = gather_step(step, tokens, sides, chips, cores)

    def collected(value):
        found = [value]
        for k in range(1, half):
            found.append(lax.ppermute(value, "fsdp", [(k, 0), (planes - 1 - k, planes - 1)]))
        return found

    ready = [min(2 * j + 1, heads - 1) + planes - 1 for j in range(pairs)]
    leaves = []
    for j in range(pairs):
        leaves.append(max([ready[j] + 1, heads] + [stage + 1 for stage in leaves[-1:]]))
    stages = leaves[-1] + planes

    pending = [{} for _ in range(chains)]
    finals = [{} for _ in range(chains)]
    passed = [[[] for _ in range(pairs)] for _ in range(chains)]
    directions = [[] for _ in range(chains)]
    clip_directions = []
    sums = [None] * pairs
    size = share * length

    def own_tokens(chain):
        return [side_of[chain * size : (chain + 1) * size] for side_of in tokens]

    def product(chain, is_far, head):
        return dots(own_tokens(chain)[is_far], factors[head], ((1,), (0,)))

    parts = [{(1, 0): product(chain, 1, 0)} for chain in range(chains)]
    (own_up, noised), parts[0] = lax.optimization_barrier(((upstream[0], noised), parts[0]))
    own_up = own_order(own_up, order)
    kept_heads = [jnp.minimum(2 * j + side, heads - 1) for j in range(pairs)]
    ups = collected(
        jnp.stack([lax.dynamic_slice_in_dim(own_up, h * HEAD, HEAD, 1) for h in kept_heads])
    )
    groups = collected(own_order(group_index[0], order))
    blocks = noised.reshape(piece, sides, planes, shard_rows).swapaxes(1, 2)
    found, columns = [block_from(blocks, 0)], None
    summed = [jnp.zeros((3, shard_rows, head_cols), jnp.float32)]

    def settle(j, own_grad, other):
        head = 2 * j
        other = other.astype(jnp.float32)
        first = jnp.where(first_side, own_grad, other)
        second = jnp.where(first_side, other, own_grad)
        both = jnp.concatenate([first, second], axis=2)[:, :, : (heads - head) * HEAD]
        summed[0] = lax.dynamic_update_slice(summed[0], both, (0, 0, head * HEAD))

    for stage in range(stages):
        for chain in range(chains):
            arrived, tokens = lax.optimization_barrier((pending[chain], tokens))
            coming = {}
            parts[chain].update(arrived.get("parts", {}))
            coming["parts"] = {
                (is_far, head): product(chain, is_far, head)
                for is_far, head in ((1, stage + 1), (0, stage + 1 - half))
                if 0 <= head < heads
            }
            for j, returned in arrived.get("other", {}).items():
                settle(j, *returned)
            values = {}
            for hop in range(1, planes + 1):
                head = stage - hop + 1
                if not 0 <= head < heads:
                    continue
                total = parts[chain][hop <= half, head]
                if hop > 1:
                    total = total + arrived["sums"][(hop - 1) % 2].astype(jnp.float32)
                values[hop] = total.astype(jnp.bfloat16)
            done = values.pop(planes, None)
            if values:
                coming["sums"] = send_hops(values)
            if done is not None:
                finals[chain][stage - planes + 1] = done
            slot = stage * chains + chain
            if "block" in arrived:
                found.append(arrived["block"])
            if 1 <= slot < planes:
                coming["block"] = block_from(blocks, slot)
            turn, odd_slot = divmod(slot - (planes - 1 + chains), chains)
            if odd_slot == 0 and turn >= 0:
                columns = by_distance(found) if turn == 0 else arrived.get("columns", columns)
                if turn < 3:
                    coming["columns"] = gather_step(turn, columns, sides, chips, cores)
                if turn == 3:
                    coming["columns"] = [jnp.swapaxes(each, 0, 1) for each in columns]
            if chain == chains - 1 and stage == 0:
                coming["ups"], coming["groups"] = ups, groups
            if chain == chains - 1 and stage == 1:
                ups, groups = arrived["ups"], arrived["groups"]
                group_forms = []
                for at in range(chains):
                    own = jnp.stack(groups[at * share : (at + 1) * share])
                    group_forms.append(
                        (
                            jnp.broadcast_to(own[:, None, :], (share, 8, length)),
                            jnp.broadcast_to(own[:, :, None], (share, length, HEAD)),
                        )
                    )
            for j in range(pairs):
                if stage == ready[j]:
                    even, odd = finals[chain][2 * j], finals[chain][min(2 * j + 1, heads - 1)]
                    kept = jnp.where(first_side, even, odd)
                    sent = jnp.where(first_side, odd, even)
                    coming["swapped"] = (kept, lax.ppermute(sent, "mesh", swap))
                if stage == ready[j] + 1:
                    kept, swapped = arrived["swapped"]
                    members = range(chain * share, (chain + 1) * share)
                    direction, cotangents = attention(
                        side,
                        sides,
                        kept.reshape(share, length, 3 * HEAD),
                        swapped.reshape(share, length, 3 * HEAD),
                        jnp.stack([ups[k][j] for k in members]),
                        group_forms[chain],
                    )
                    passed[chain][j].append(cotangents.reshape(3, size, HEAD))
                    directions[chain].append(direction)
                    if j < pairs - 1:
                        continue
                    joined = jnp.concatenate(directions[chain], axis=2)
                    coming["directions"] = []
                    for k in members:
                        moved = joined[k - chain * share]
                        if k > 0:
                            hops = [(0, k), (planes - 1, planes - 1 - k)]
                            moved = lax.ppermute(moved, "fsdp", hops)
                        coming["directions"].append(moved)
            if stage == ready[-1] + 2:
                clip_directions.extend(arrived["directions"])
            values = {}
            for j in range(pairs):
                hop = stage - leaves[j]
                if 1 <= hop < planes:
                    passed[chain][j].append(arrived["cots"][hop % 2])
                if 0 <= hop < planes - 1:
                    values[hop + 1] = passed[chain][j][hop]
            if values:
                coming["cots"] = send_hops(values)
            for j in range(pairs):
                late = j < pairs - 1
                if late and stage == leaves[j] + planes - 1:
                    coming["passed"] = passed[chain][j]
                if stage != leaves[j] + planes - 1 + late:
                    continue
                all_hops = arrived["passed"] if late else passed[chain][j]
                for is_far in range(2):
                    hops = all_hops[::-1] if is_far else all_hops
                    block = columns[is_far][:, chain * size : (chain + 1) * size]
                    added = dots(block, pick(hops[:half]), ((1,), (1,)))
                    sums[j] = added if sums[j] is None else sums[j] + added
                if chain < chains - 1:
                    continue
                grad = jnp.swapaxes(sums[j], 0, 1).reshape(3, sides, shard_rows, HEAD)
                own_grad = jnp.where(first_side, grad[:, 0], grad[:, 1])
                sent = jnp.where(first_side, grad[:, 1], grad[:, 0]).astype(jnp.bfloat16)
                returned = (own_grad, lax.ppermute(sent, "mesh", swap))
                coming.setdefault("other", {})[j] = returned
            pending[chain] = coming
        if stage == ready[-1] + 2:
            local = pick(clip_directions)
            local = local.reshape(sides, chips, cores, -1, pairs * HEAD)
            axes = [("mesh", 1, sides), ("seq", cores, chips), ("seq", 1, cores)]
            for at, (axis, inner, outer) in enumerate(axes):
                blocks = [lax.index_in_dim(local, -d % outer, at, False) for d in range(outer)]
                for d in range(1, outer):
                    blocks[d] = shifted_by(blocks[d], axis, d, inner, outer)
                local = jnp.stack(blocks, axis=at)
            local = own_order(local.reshape(sides * lanes, -1, pairs * HEAD), order, back=True)
    for j, returned in pending[-1]["other"].items():
        settle(j, *returned)
    summed = jnp.swapaxes(summed[0], 0, 1)

    local = local.reshape(sides, lanes, -1, pairs, HEAD)
    local = jnp.transpose(local, (2, 1, 3, 0, 4)).reshape(-1, lanes, pairs * sides, HEAD)
    direction = local[:, :, :heads].reshape(1, -1, lanes * head_cols)
    return (direction, summed)


def solution(mesh):
    in_specs = (
        P("fsdp", "mesh", None),
        P("fsdp", "mesh", None),
        P("fsdp"),
        P("fsdp", None),
        P("mesh", "fsdp", None, "seq"),
        P("fsdp", None, "seq"),
    )
    out_specs = (P("fsdp", ("mesh", "seq"), None), P(("mesh", "fsdp"), None, "seq"))
    return jax.shard_map(
        per_device, mesh=mesh, in_specs=in_specs, out_specs=out_specs, check_vma=False
    )
```

```python
import math

import jax
import jax.numpy as jnp
from jax import lax
from jax.experimental import pallas as pl
from jax.experimental.pallas import tpu as pltpu
from jax.sharding import PartitionSpec as P

HEAD = 128


def shifted_by(value, axis, d, inner=1, outer=1):
    pairs = []
    for i in range(lax.axis_size(axis)):
        place = i // inner % outer
        pairs.append((i + ((place + d) % outer - place) * inner, i))
    return lax.ppermute(value, axis, pairs)


def spread(value, axis, inner, outer, at):
    pieces = [value] + [shifted_by(value, axis, d, inner, outer) for d in range(1, outer)]
    return jnp.stack(pieces, axis=at)


def turned(value, at, start):
    size = value.shape[at]
    return lax.dynamic_slice_in_dim(jnp.concatenate([value, value], axis=at), start, size, at)


def own_order(value, factors, back=False):
    sizes = [size for size, _ in factors]
    parts = value.reshape(sizes + [-1] + list(value.shape[1:]))
    for at, (size, place) in enumerate(factors):
        parts = turned(parts, at, size - place if back else place)
    return parts.reshape(value.shape)


def gather_step(step, pair, sides, chips, cores):
    first, second = pair
    if step == 0:
        return spread(first, "mesh", 1, sides, 1), spread(second, "seq", cores, chips, 1)
    if step == 1:
        return spread(first, "seq", cores, chips, 2), spread(second, "mesh", 1, sides, 1)
    both = spread(jnp.stack([first, second]), "seq", 1, cores, 4)
    both = both.reshape(2, -1, both.shape[-1])
    return both[0], both[1]


def dots(left, right, dims):
    return lax.dot_general(left, right, (dims, ((), ())), preferred_element_type=jnp.float32)


def attention_kernel(
    block, sides, side_ref, kept_ref, swapped_ref, up_ref, key_group_ref, group_ref,
    direction_ref, cot_ref, teacher_ref, fake_ref, key_grad_ref, value_grad_ref,
):
    length = kept_ref.shape[1]
    span = length // sides
    score_scale = 1.0 / math.sqrt(HEAD)
    first_side = side_ref[0] == 0
    for at in range(sides):
        here = pl.ds(at * span, span)
        there = pl.ds((sides - 1 - at) * span, span)
        kept, swapped = kept_ref[0, here, :], swapped_ref[0, there, :]
        teacher_ref[here, :] = jnp.where(first_side, kept, swapped)
        fake_ref[here, :] = jnp.where(first_side, swapped, kept)
    queries, key_rows, values = (pl.ds(at * HEAD, HEAD) for at in range(3))

    def softmax(triple_ref, rows, visible):
        scores = dots(triple_ref[rows, queries], triple_ref[:, key_rows], ((1,), (1,)))
        scores = jnp.where(visible, scores * score_scale, jnp.float32(-1e30))
        weights = jnp.exp(scores - jnp.max(scores, axis=-1, keepdims=True))
        return weights * (1.0 / jnp.sum(weights, axis=-1, keepdims=True))

    for start in range(0, length, block):
        rows = pl.ds(start, block)
        visible = key_group_ref[0, :1, :] <= group_ref[0, rows, :1]
        prob_low = softmax(teacher_ref, rows, visible).astype(jnp.bfloat16)
        teacher_out = dots(prob_low, teacher_ref[:, values], ((1,), (0,))).astype(jnp.bfloat16)
        probabilities = softmax(fake_ref, rows, visible)
        prob_low = probabilities.astype(jnp.bfloat16)
        fake_out = dots(prob_low, fake_ref[:, values], ((1,), (0,))).astype(jnp.bfloat16)
        direction_ref[0, rows, :] = (
            fake_out.astype(jnp.float32) - teacher_out.astype(jnp.float32)
        ).astype(jnp.bfloat16)
        grad_out = up_ref[0, rows, :]
        prob_grad = dots(grad_out, fake_ref[:, values], ((1,), (1,)))
        row_inner = jnp.sum(probabilities * prob_grad, axis=-1, keepdims=True)
        score_grad = probabilities * (prob_grad - row_inner) * score_scale
        query_grad = dots(score_grad.astype(jnp.bfloat16), fake_ref[:, key_rows], ((1,), (0,)))
        cot_ref[0, 0, rows, :] = query_grad.astype(jnp.bfloat16)
        score_grad = jnp.transpose(score_grad).astype(jnp.bfloat16)
        key_part = dots(score_grad, fake_ref[rows, queries], ((1,), (0,)))
        prob_low = jnp.transpose(probabilities).astype(jnp.bfloat16)
        value_part = dots(prob_low, grad_out, ((1,), (0,)))
        if start == 0:
            key_grad_ref[...] = key_part
            value_grad_ref[...] = value_part
        else:
            key_grad_ref[...] += key_part
            value_grad_ref[...] += value_part
    cot_ref[1, 0] = key_grad_ref[...].astype(jnp.bfloat16)
    cot_ref[2, 0] = value_grad_ref[...].astype(jnp.bfloat16)


def attention(side, sides, kept, swapped, grad_out, groups):
    clips, length, width = kept.shape
    block = math.gcd(length, 256)
    area = clips * length * length

    def spec(rows, columns):
        return pl.BlockSpec((1, rows, columns), lambda clip: (clip, 0, 0))

    triple = spec(length, width)
    return pl.pallas_call(
        lambda *refs: attention_kernel(block, sides, *refs),
        grid=(clips,),
        in_specs=[
            pl.BlockSpec(memory_space=pltpu.SMEM),
            triple, triple, spec(length, HEAD), spec(8, length), spec(length, HEAD),
        ],
        out_specs=[
            spec(length, HEAD),
            pl.BlockSpec((3, 1, length, HEAD), lambda clip: (0, clip, 0, 0)),
        ],
        out_shape=[
            jax.ShapeDtypeStruct((clips, length, HEAD), jnp.bfloat16),
            jax.ShapeDtypeStruct((3, clips, length, HEAD), jnp.bfloat16),
        ],
        scratch_shapes=[pltpu.VMEM((length, width), jnp.bfloat16)] * 2
        + [pltpu.VMEM((length, HEAD), jnp.float32)] * 2,
        compiler_params=pltpu.CompilerParams(vmem_limit_bytes=16 * 1024 * 1024),
        cost_estimate=pl.CostEstimate(
            flops=18 * area * HEAD,
            bytes_accessed=20 * clips * length * HEAD,
            transcendentals=2 * area,
        ),
        name="attention",
    )(side.reshape(1), kept, swapped, grad_out, *groups)


def per_device(latents, noise, noise_level, group_index, projections, upstream):
    planes = lax.axis_size("fsdp")
    sides = lax.axis_size("mesh")
    lanes = lax.axis_size("seq")
    plane = lax.axis_index("fsdp")
    side = lax.axis_index("mesh")
    lane = lax.axis_index("seq")
    half = planes // 2
    chains = 2 if half % 2 == 0 else 1
    share = half // chains
    cores = 2 if lanes % 2 == 0 else 1
    chips = lanes // cores
    order = [(sides, side), (chips, lane // cores), (cores, lane % cores)]
    low_half = plane < half
    first_side = side == 0
    distance = jnp.minimum(plane, planes - 1 - plane)
    swap = [(0, 1), (1, 0)]

    rows, _, head_cols = projections.shape[1:]
    length = group_index.shape[1]
    heads = head_cols // HEAD
    pairs = (heads + 1) // 2
    shard_rows = rows // sides

    def hop_pairs(hop):
        return [(hop - 1, hop), (planes - hop, planes - 1 - hop)]

    def send_hops(values):
        sent = {}
        for parity in range(2):
            hops = [hop for hop in sorted(values) if hop % 2 == parity]
            if not hops:
                continue
            value = values[hops[-1]]
            for hop in hops[-2::-1]:
                here = (plane == hop - 1) | (plane == planes - hop)
                value = jnp.where(here, values[hop], value)
            sent[parity] = lax.ppermute(value, "fsdp", sum([hop_pairs(h) for h in hops], []))
        return sent

    def pick(by_distance):
        picked = by_distance[-1]
        for d in range(len(by_distance) - 2, -1, -1):
            picked = jnp.where(distance == d, by_distance[d], picked)
        return picked

    piece = latents.shape[1] // lanes
    own_rows = lax.dynamic_slice_in_dim(latents[0], lane * piece, piece, 0)
    own_noise = lax.dynamic_slice_in_dim(noise[0], lane * piece, piece, 0)
    noise_rate = noise_level[0]
    noised = (
        (1.0 - noise_rate) * own_rows.astype(jnp.float32)
        + noise_rate * own_noise.astype(jnp.float32)
    ).astype(jnp.bfloat16)

    def block_from(blocks, d):
        to = lax.rem(plane + planes - d, planes)
        block = lax.dynamic_index_in_dim(blocks, to, 0, False)
        return shifted_by(block, "fsdp", d, 1, planes) if d else block

    def by_distance(found):
        found = [block.reshape(piece, rows) for block in found]
        near, far = [], []
        for k in range(half):
            for side_of, mirrored in ((near, False), (far, True)):
                picked = None
                for p in range(planes):
                    clip = k if (p < half) != mirrored else planes - 1 - k
                    block = found[(clip - p) % planes]
                    picked = block if picked is None else jnp.where(plane == p, block, picked)
                side_of.append(picked)
        return jnp.stack(near), jnp.stack(far)

    factors = jnp.swapaxes(projections[0].reshape(rows, 3, heads, HEAD), 1, 2)
    factors = factors.reshape(rows, heads * 3 * HEAD)
    own_up = own_order(upstream[0], order)
    kept_heads = [jnp.minimum(2 * j + side, heads - 1) for j in range(pairs)]
    kept_up = jnp.stack(
        [lax.dynamic_slice_in_dim(own_up, h * HEAD, HEAD, 1) for h in kept_heads]
    )
    blocks = jnp.swapaxes(noised.reshape(piece, planes, rows), 0, 1)
    blocks = [block_from(blocks, d) for d in range(planes)]
    column_blocks = jnp.transpose(
        noised.reshape(piece, sides, planes, shard_rows), (2, 0, 1, 3)
    ).reshape(planes, piece, rows)
    found, factors, kept_up, column_blocks = lax.optimization_barrier(
        (blocks, factors, kept_up, column_blocks)
    )
    tokens = by_distance(found)
    for step in range(3):
        tokens = gather_step(step, tokens, sides, chips, cores)

    def collected(value):
        found = [value]
        for k in range(1, half):
            found.append(lax.ppermute(value, "fsdp", [(k, 0), (planes - 1 - k, planes - 1)]))
        return found

    ready = [min(2 * j + 1, heads - 1) + planes - 1 for j in range(pairs)]
    leaves = []
    for j in range(pairs):
        leaves.append(max([ready[j] + 1, heads] + [stage + 1 for stage in leaves[-1:]]))
    stages = leaves[-1] + planes

    pending = [{} for _ in range(chains)]
    finals = [{} for _ in range(chains)]
    passed = [[[] for _ in range(pairs)] for _ in range(chains)]
    directions = [[] for _ in range(chains)]
    clip_directions = []
    sums = [None] * pairs
    size = share * length

    def own_tokens(chain):
        return [side_of[chain * size : (chain + 1) * size] for side_of in tokens]

    first = 3 * HEAD
    parts = [dots(own_tokens(chain)[1], factors[:, :first], ((1,), (0,))) for chain in range(chains)]
    wide = [None, None]
    (kept_up, column_blocks), parts[0] = lax.optimization_barrier(
        ((kept_up, column_blocks), parts[0])
    )
    ups = collected(kept_up)
    groups = collected(own_order(group_index[0], order))
    found, columns = [block_from(column_blocks, 0)], None
    summed = [jnp.zeros((3, shard_rows, head_cols), jnp.float32)]

    def settle(j, own_grad, other):
        head = 2 * j
        other = other.astype(jnp.float32)
        first = jnp.where(first_side, own_grad, other)
        second = jnp.where(first_side, other, own_grad)
        both = jnp.concatenate([first, second], axis=2)[:, :, : (heads - head) * HEAD]
        summed[0] = lax.dynamic_update_slice(summed[0], both, (0, 0, head * HEAD))

    for stage in range(stages):
        for chain in range(chains):
            arrived, tokens = lax.optimization_barrier((pending[chain], tokens))
            coming = {}
            if "wide" in arrived:
                wide[2 - stage] = arrived["wide"]
            if chain == 0 and stage == 0 and heads > 1:
                coming["wide"] = dots(tokens[1], factors[:, first:], ((1,), (0,)))
            if chain == 0 and stage == 1:
                coming["wide"] = dots(tokens[0], factors, ((1,), (0,)))
            for j, returned in arrived.get("other", {}).items():
                settle(j, *returned)
            values = {}
            for hop in range(1, planes + 1):
                head = stage - hop + 1
                if not 0 <= head < heads:
                    continue
                if hop <= half and head == 0:
                    total = parts[chain]
                else:
                    column = first * (head - (hop <= half))
                    total = wide[hop <= half][chain * size : (chain + 1) * size]
                    total = total[:, column : column + first]
                if hop > 1:
                    total = total + arrived["sums"][(hop - 1) % 2].astype(jnp.float32)
                values[hop] = total.astype(jnp.bfloat16)
            done = values.pop(planes, None)
            if values:
                coming["sums"] = send_hops(values)
            if done is not None:
                finals[chain][stage - planes + 1] = done
            slot = stage * chains + chain
            if "block" in arrived:
                found.append(arrived["block"])
            if 1 <= slot < planes:
                coming["block"] = block_from(column_blocks, slot)
            turn, odd_slot = divmod(slot - (planes - 1 + chains), chains)
            if odd_slot == 0 and turn >= 0:
                columns = by_distance(found) if turn == 0 else arrived.get("columns", columns)
                if turn < 3:
                    coming["columns"] = gather_step(turn, columns, sides, chips, cores)
                if turn == 3:
                    coming["columns"] = [jnp.swapaxes(each, 0, 1) for each in columns]
            if chain == chains - 1 and stage == 0:
                coming["ups"], coming["groups"] = ups, groups
            if chain == chains - 1 and stage == 1:
                ups, groups = arrived["ups"], arrived["groups"]
                group_forms = []
                for at in range(chains):
                    own = jnp.stack(groups[at * share : (at + 1) * share])
                    group_forms.append(
                        (
                            jnp.broadcast_to(own[:, None, :], (share, 8, length)),
                            jnp.broadcast_to(own[:, :, None], (share, length, HEAD)),
                        )
                    )
            for j in range(pairs):
                if stage == ready[j]:
                    even, odd = finals[chain][2 * j], finals[chain][min(2 * j + 1, heads - 1)]
                    kept = jnp.where(first_side, even, odd)
                    sent = jnp.where(first_side, odd, even)
                    coming["swapped"] = (kept, lax.ppermute(sent, "mesh", swap))
                if stage == ready[j] + 1:
                    kept, swapped = arrived["swapped"]
                    members = range(chain * share, (chain + 1) * share)
                    direction, cotangents = attention(
                        side,
                        sides,
                        kept.reshape(share, length, 3 * HEAD),
                        swapped.reshape(share, length, 3 * HEAD),
                        jnp.stack([ups[k][j] for k in members]),
                        group_forms[chain],
                    )
                    passed[chain][j].append(cotangents.reshape(3, size, HEAD))
                    directions[chain].append(direction)
                    if j < pairs - 1:
                        continue
                    joined = jnp.concatenate(directions[chain], axis=2)
                    coming["directions"] = []
                    for k in members:
                        moved = joined[k - chain * share]
                        if k > 0:
                            hops = [(0, k), (planes - 1, planes - 1 - k)]
                            moved = lax.ppermute(moved, "fsdp", hops)
                        coming["directions"].append(moved)
            if stage == ready[-1] + 2:
                clip_directions.extend(arrived["directions"])
            values = {}
            for j in range(pairs):
                hop = stage - leaves[j]
                if 1 <= hop < planes:
                    passed[chain][j].append(arrived["cots"][hop % 2])
                if 0 <= hop < planes - 1:
                    values[hop + 1] = passed[chain][j][hop]
            if values:
                coming["cots"] = send_hops(values)
            for j in range(pairs):
                late = j < pairs - 1
                if late and stage == leaves[j] + planes - 1:
                    coming["passed"] = passed[chain][j]
                if stage != leaves[j] + planes - 1 + late:
                    continue
                all_hops = arrived["passed"] if late else passed[chain][j]
                for is_far in range(2):
                    hops = all_hops[::-1] if is_far else all_hops
                    block = columns[is_far][:, chain * size : (chain + 1) * size]
                    added = dots(block, pick(hops[:half]), ((1,), (1,)))
                    sums[j] = added if sums[j] is None else sums[j] + added
                if chain < chains - 1:
                    continue
                grad = jnp.swapaxes(sums[j], 0, 1).reshape(3, sides, shard_rows, HEAD)
                own_grad = jnp.where(first_side, grad[:, 0], grad[:, 1])
                sent = jnp.where(first_side, grad[:, 1], grad[:, 0]).astype(jnp.bfloat16)
                returned = (own_grad, lax.ppermute(sent, "mesh", swap))
                coming.setdefault("other", {})[j] = returned
            pending[chain] = coming
        if stage == ready[-1] + 2:
            local = pick(clip_directions)
            local = local.reshape(sides, chips, cores, -1, pairs * HEAD)
            axes = [("mesh", 1, sides), ("seq", cores, chips), ("seq", 1, cores)]
            for at, (axis, inner, outer) in enumerate(axes):
                blocks = [lax.index_in_dim(local, -d % outer, at, False) for d in range(outer)]
                for d in range(1, outer):
                    blocks[d] = shifted_by(blocks[d], axis, d, inner, outer)
                local = jnp.stack(blocks, axis=at)
            local = own_order(local.reshape(sides * lanes, -1, pairs * HEAD), order, back=True)
    for j, returned in pending[-1]["other"].items():
        settle(j, *returned)
    summed = jnp.swapaxes(summed[0], 0, 1)

    local = local.reshape(sides, lanes, -1, pairs, HEAD)
    local = jnp.transpose(local, (2, 1, 3, 0, 4)).reshape(-1, lanes, pairs * sides, HEAD)
    direction = local[:, :, :heads].reshape(1, -1, lanes * head_cols)
    return (direction, summed)


def solution(mesh):
    in_specs = (
        P("fsdp", "mesh", None),
        P("fsdp", "mesh", None),
        P("fsdp"),
        P("fsdp", None),
        P("mesh", "fsdp", None, "seq"),
        P("fsdp", None, "seq"),
    )
    out_specs = (P("fsdp", ("mesh", "seq"), None), P(("mesh", "fsdp"), None, "seq"))
    return jax.shard_map(
        per_device, mesh=mesh, in_specs=in_specs, out_specs=out_specs, check_vma=False
    )
```

```python
import math

import jax
import jax.numpy as jnp
from jax import lax
from jax.experimental import pallas as pl
from jax.experimental.pallas import tpu as pltpu
from jax.sharding import PartitionSpec as P

HEAD = 128


def shifted_by(value, axis, d, inner=1, outer=1):
    pairs = []
    for i in range(lax.axis_size(axis)):
        place = i // inner % outer
        pairs.append((i + ((place + d) % outer - place) * inner, i))
    return lax.ppermute(value, axis, pairs)


def spread(value, axis, inner, outer, at):
    pieces = [value] + [shifted_by(value, axis, d, inner, outer) for d in range(1, outer)]
    return jnp.stack(pieces, axis=at)


def turned(value, at, start):
    size = value.shape[at]
    return lax.dynamic_slice_in_dim(jnp.concatenate([value, value], axis=at), start, size, at)


def own_order(value, factors, back=False):
    sizes = [size for size, _ in factors]
    parts = value.reshape(sizes + [-1] + list(value.shape[1:]))
    for at, (size, place) in enumerate(factors):
        parts = turned(parts, at, size - place if back else place)
    return parts.reshape(value.shape)


def gather_step(step, pair, sides, chips, cores):
    first, second = pair
    if step == 0:
        return spread(first, "mesh", 1, sides, 1), spread(second, "seq", cores, chips, 1)
    if step == 1:
        return spread(first, "seq", cores, chips, 2), spread(second, "mesh", 1, sides, 1)
    both = spread(jnp.stack([first, second]), "seq", 1, cores, 4)
    both = both.reshape(2, -1, both.shape[-1])
    return both[0], both[1]


def dots(left, right, dims):
    return lax.dot_general(left, right, (dims, ((), ())), preferred_element_type=jnp.float32)


def attention_kernel(
    block, sides, side_ref, kept_ref, swapped_ref, up_ref, key_group_ref, group_ref,
    direction_ref, cot_ref, teacher_ref, fake_ref, key_grad_ref, value_grad_ref,
):
    length = kept_ref.shape[1]
    span = length // sides
    score_scale = 1.0 / math.sqrt(HEAD)
    first_side = side_ref[0] == 0
    for at in range(sides):
        here = pl.ds(at * span, span)
        there = pl.ds((sides - 1 - at) * span, span)
        kept, swapped = kept_ref[0, here, :], swapped_ref[0, there, :]
        teacher_ref[here, :] = jnp.where(first_side, kept, swapped)
        fake_ref[here, :] = jnp.where(first_side, swapped, kept)
    queries, key_rows, values = (pl.ds(at * HEAD, HEAD) for at in range(3))

    def softmax(triple_ref, rows, visible):
        scores = dots(triple_ref[rows, queries], triple_ref[:, key_rows], ((1,), (1,)))
        scores = jnp.where(visible, scores * score_scale, jnp.float32(-1e30))
        weights = jnp.exp(scores - jnp.max(scores, axis=-1, keepdims=True))
        return weights * (1.0 / jnp.sum(weights, axis=-1, keepdims=True))

    for start in range(0, length, block):
        rows = pl.ds(start, block)
        visible = key_group_ref[0, :1, :] <= group_ref[0, rows, :1]
        prob_low = softmax(teacher_ref, rows, visible).astype(jnp.bfloat16)
        teacher_out = dots(prob_low, teacher_ref[:, values], ((1,), (0,))).astype(jnp.bfloat16)
        probabilities = softmax(fake_ref, rows, visible)
        prob_low = probabilities.astype(jnp.bfloat16)
        fake_out = dots(prob_low, fake_ref[:, values], ((1,), (0,))).astype(jnp.bfloat16)
        direction_ref[0, rows, :] = (
            fake_out.astype(jnp.float32) - teacher_out.astype(jnp.float32)
        ).astype(jnp.bfloat16)
        grad_out = up_ref[0, rows, :]
        prob_grad = dots(grad_out, fake_ref[:, values], ((1,), (1,)))
        row_inner = jnp.sum(probabilities * prob_grad, axis=-1, keepdims=True)
        score_grad = probabilities * (prob_grad - row_inner) * score_scale
        query_grad = dots(score_grad.astype(jnp.bfloat16), fake_ref[:, key_rows], ((1,), (0,)))
        cot_ref[0, 0, rows, :] = query_grad.astype(jnp.bfloat16)
        score_grad = jnp.transpose(score_grad).astype(jnp.bfloat16)
        key_part = dots(score_grad, fake_ref[rows, queries], ((1,), (0,)))
        prob_low = jnp.transpose(probabilities).astype(jnp.bfloat16)
        value_part = dots(prob_low, grad_out, ((1,), (0,)))
        if start == 0:
            key_grad_ref[...] = key_part
            value_grad_ref[...] = value_part
        else:
            key_grad_ref[...] += key_part
            value_grad_ref[...] += value_part
    cot_ref[1, 0] = key_grad_ref[...].astype(jnp.bfloat16)
    cot_ref[2, 0] = value_grad_ref[...].astype(jnp.bfloat16)


def attention(side, sides, kept, swapped, grad_out, groups):
    clips, length, width = kept.shape
    block = math.gcd(length, 256)
    area = clips * length * length

    def spec(rows, columns):
        return pl.BlockSpec((1, rows, columns), lambda clip: (clip, 0, 0))

    triple = spec(length, width)
    return pl.pallas_call(
        lambda *refs: attention_kernel(block, sides, *refs),
        grid=(clips,),
        in_specs=[
            pl.BlockSpec(memory_space=pltpu.SMEM),
            triple, triple, spec(length, HEAD), spec(8, length), spec(length, HEAD),
        ],
        out_specs=[
            spec(length, HEAD),
            pl.BlockSpec((3, 1, length, HEAD), lambda clip: (0, clip, 0, 0)),
        ],
        out_shape=[
            jax.ShapeDtypeStruct((clips, length, HEAD), jnp.bfloat16),
            jax.ShapeDtypeStruct((3, clips, length, HEAD), jnp.bfloat16),
        ],
        scratch_shapes=[pltpu.VMEM((length, width), jnp.bfloat16)] * 2
        + [pltpu.VMEM((length, HEAD), jnp.float32)] * 2,
        compiler_params=pltpu.CompilerParams(vmem_limit_bytes=16 * 1024 * 1024),
        cost_estimate=pl.CostEstimate(
            flops=18 * area * HEAD,
            bytes_accessed=20 * clips * length * HEAD,
            transcendentals=2 * area,
        ),
        name="attention",
    )(side.reshape(1), kept, swapped, grad_out, *groups)


def per_device(latents, noise, noise_level, group_index, projections, upstream):
    planes = lax.axis_size("fsdp")
    sides = lax.axis_size("mesh")
    lanes = lax.axis_size("seq")
    plane = lax.axis_index("fsdp")
    side = lax.axis_index("mesh")
    lane = lax.axis_index("seq")
    half = planes // 2
    chains = 2 if half % 2 == 0 else 1
    share = half // chains
    cores = 2 if lanes % 2 == 0 else 1
    chips = lanes // cores
    order = [(sides, side), (chips, lane // cores), (cores, lane % cores)]
    low_half = plane < half
    first_side = side == 0
    distance = jnp.minimum(plane, planes - 1 - plane)
    swap = [(0, 1), (1, 0)]

    rows, _, head_cols = projections.shape[1:]
    length = group_index.shape[1]
    heads = head_cols // HEAD
    pairs = (heads + 1) // 2
    shard_rows = rows // sides

    def hop_pairs(hop):
        return [(hop - 1, hop), (planes - hop, planes - 1 - hop)]

    def send_hops(values):
        sent = {}
        for parity in range(2):
            hops = [hop for hop in sorted(values) if hop % 2 == parity]
            if not hops:
                continue
            value = values[hops[-1]]
            for hop in hops[-2::-1]:
                here = (plane == hop - 1) | (plane == planes - hop)
                value = jnp.where(here, values[hop], value)
            sent[parity] = lax.ppermute(value, "fsdp", sum([hop_pairs(h) for h in hops], []))
        return sent

    def pick(by_distance):
        picked = by_distance[-1]
        for d in range(len(by_distance) - 2, -1, -1):
            picked = jnp.where(distance == d, by_distance[d], picked)
        return picked

    piece = latents.shape[1] // lanes
    own_rows = lax.dynamic_slice_in_dim(latents[0], lane * piece, piece, 0)
    own_noise = lax.dynamic_slice_in_dim(noise[0], lane * piece, piece, 0)
    noise_rate = noise_level[0]
    noised = (
        (1.0 - noise_rate) * own_rows.astype(jnp.float32)
        + noise_rate * own_noise.astype(jnp.float32)
    ).astype(jnp.bfloat16)

    def block_from(blocks, d):
        to = lax.rem(plane + planes - d, planes)
        block = lax.dynamic_index_in_dim(blocks, to, 0, False)
        return shifted_by(block, "fsdp", d, 1, planes) if d else block

    def by_distance(found):
        found = [block.reshape(piece, rows) for block in found]
        near, far = [], []
        for k in range(half):
            for side_of, mirrored in ((near, False), (far, True)):
                picked = None
                for p in range(planes):
                    clip = k if (p < half) != mirrored else planes - 1 - k
                    block = found[(clip - p) % planes]
                    picked = block if picked is None else jnp.where(plane == p, block, picked)
                side_of.append(picked)
        return jnp.stack(near), jnp.stack(far)

    factors = jnp.swapaxes(projections[0].reshape(rows, 3, heads, HEAD), 1, 2)
    factors = factors.reshape(rows, heads * 3 * HEAD)
    own_up = own_order(upstream[0], order)
    kept_heads = [jnp.minimum(2 * j + side, heads - 1) for j in range(pairs)]
    kept_up = jnp.stack(
        [lax.dynamic_slice_in_dim(own_up, h * HEAD, HEAD, 1) for h in kept_heads]
    )
    blocks = jnp.swapaxes(noised.reshape(piece, planes, rows), 0, 1)
    blocks = [block_from(blocks, d) for d in range(planes)]
    column_blocks = jnp.transpose(
        noised.reshape(piece, sides, planes, shard_rows), (2, 0, 1, 3)
    ).reshape(planes, piece, rows)
    found, factors, kept_up, column_blocks = lax.optimization_barrier(
        (blocks, factors, kept_up, column_blocks)
    )
    tokens = by_distance(found)
    for step in range(3):
        tokens = gather_step(step, tokens, sides, chips, cores)

    def collected(value):
        found = [value]
        for k in range(1, half):
            found.append(lax.ppermute(value, "fsdp", [(k, 0), (planes - 1 - k, planes - 1)]))
        return found

    ready = [min(2 * j + 1, heads - 1) + planes - 1 for j in range(pairs)]
    leaves = []
    for j in range(pairs):
        leaves.append(max([ready[j] + 1, heads] + [stage + 1 for stage in leaves[-1:]]))
    stages = leaves[-1] + planes

    pending = [{} for _ in range(chains)]
    finals = [{} for _ in range(chains)]
    passed = [[[] for _ in range(pairs)] for _ in range(chains)]
    directions = [[] for _ in range(chains)]
    clip_directions = []
    sums = [None] * pairs
    size = share * length

    def own_tokens(chain):
        return [side_of[chain * size : (chain + 1) * size] for side_of in tokens]

    first = 3 * HEAD
    parts = [dots(own_tokens(chain)[1], factors[:, :first], ((1,), (0,))) for chain in range(chains)]
    wide = [None, None]
    (kept_up, column_blocks), parts[0] = lax.optimization_barrier(
        ((kept_up, column_blocks), parts[0])
    )
    ups = collected(kept_up)
    groups = collected(own_order(group_index[0], order))
    found, columns = [block_from(column_blocks, 0)], None
    summed = [jnp.zeros((3, shard_rows, head_cols), jnp.float32)]

    def settle(j, own_grad, other):
        head = 2 * j
        other = other.astype(jnp.float32)
        first = jnp.where(first_side, own_grad, other)
        second = jnp.where(first_side, other, own_grad)
        both = jnp.concatenate([first, second], axis=2)[:, :, : (heads - head) * HEAD]
        summed[0] = lax.dynamic_update_slice(summed[0], both, (0, 0, head * HEAD))

    for stage in range(stages):
        for chain in range(chains):
            rest = pending[chain]
            ahead = {key: rest.pop(key) for key in ("sums", "wide") if key in rest}
            cots = {key: rest.pop(key) for key in ("cots",) if key in rest}
            ahead, tokens = lax.optimization_barrier((ahead, tokens))
            tie = (ahead, cots) if stage >= ready[-1] + 2 else ahead
            rest = lax.optimization_barrier((rest, tie))[0]
            arrived = {**ahead, **cots, **rest}
            coming = {}
            if "wide" in arrived:
                wide[2 - stage] = arrived["wide"]
            if chain == 0 and stage == 0 and heads > 1:
                coming["wide"] = dots(tokens[1], factors[:, first:], ((1,), (0,)))
            if chain == 0 and stage == 1:
                coming["wide"] = dots(tokens[0], factors, ((1,), (0,)))
            for j, returned in arrived.get("other", {}).items():
                settle(j, *returned)
            values = {}
            for hop in range(1, planes + 1):
                head = stage - hop + 1
                if not 0 <= head < heads:
                    continue
                if hop <= half and head == 0:
                    total = parts[chain]
                else:
                    column = first * (head - (hop <= half))
                    total = wide[hop <= half][chain * size : (chain + 1) * size]
                    total = total[:, column : column + first]
                if hop > 1:
                    total = total + arrived["sums"][(hop - 1) % 2].astype(jnp.float32)
                values[hop] = total.astype(jnp.bfloat16)
            done = values.pop(planes, None)
            if values:
                coming["sums"] = send_hops(values)
            if done is not None:
                finals[chain][stage - planes + 1] = done
            slot = stage * chains + chain
            if "block" in arrived:
                found.append(arrived["block"])
            if 1 <= slot < planes:
                coming["block"] = block_from(column_blocks, slot)
            turn, odd_slot = divmod(slot - (planes - 1 + chains), chains)
            if odd_slot == 0 and turn >= 0:
                columns = by_distance(found) if turn == 0 else arrived.get("columns", columns)
                if turn < 3:
                    coming["columns"] = gather_step(turn, columns, sides, chips, cores)
                if turn == 3:
                    coming["columns"] = [jnp.swapaxes(each, 0, 1) for each in columns]
            if chain == chains - 1 and stage == 0:
                coming["ups"], coming["groups"] = ups, groups
            if chain == chains - 1 and stage == 1:
                ups, groups = arrived["ups"], arrived["groups"]
                group_forms = []
                for at in range(chains):
                    own = jnp.stack(groups[at * share : (at + 1) * share])
                    group_forms.append(
                        (
                            jnp.broadcast_to(own[:, None, :], (share, 8, length)),
                            jnp.broadcast_to(own[:, :, None], (share, length, HEAD)),
                        )
                    )
            for j in range(pairs):
                if stage == ready[j]:
                    even, odd = finals[chain][2 * j], finals[chain][min(2 * j + 1, heads - 1)]
                    kept = jnp.where(first_side, even, odd)
                    sent = jnp.where(first_side, odd, even)
                    coming["swapped"] = (kept, lax.ppermute(sent, "mesh", swap))
                if stage == ready[j] + 1:
                    kept, swapped = arrived["swapped"]
                    members = range(chain * share, (chain + 1) * share)
                    direction, cotangents = attention(
                        side,
                        sides,
                        kept.reshape(share, length, 3 * HEAD),
                        swapped.reshape(share, length, 3 * HEAD),
                        jnp.stack([ups[k][j] for k in members]),
                        group_forms[chain],
                    )
                    passed[chain][j].append(cotangents.reshape(3, size, HEAD))
                    directions[chain].append(direction)
                    if j < pairs - 1:
                        continue
                    joined = jnp.concatenate(directions[chain], axis=2)
                    coming["directions"] = []
                    for k in members:
                        moved = joined[k - chain * share]
                        if k > 0:
                            hops = [(0, k), (planes - 1, planes - 1 - k)]
                            moved = lax.ppermute(moved, "fsdp", hops)
                        coming["directions"].append(moved)
            if stage == ready[-1] + 2:
                clip_directions.extend(arrived["directions"])
            values = {}
            for j in range(pairs):
                hop = stage - leaves[j]
                if 1 <= hop < planes:
                    passed[chain][j].append(arrived["cots"][hop % 2])
                if 0 <= hop < planes - 1:
                    values[hop + 1] = passed[chain][j][hop]
            if values:
                coming["cots"] = send_hops(values)
            for j in range(pairs):
                late = j < pairs - 1
                if late and stage == leaves[j] + planes - 1:
                    coming["passed"] = passed[chain][j]
                if stage != leaves[j] + planes - 1 + late:
                    continue
                all_hops = arrived["passed"] if late else passed[chain][j]
                for is_far in range(2):
                    hops = all_hops[::-1] if is_far else all_hops
                    block = columns[is_far][:, chain * size : (chain + 1) * size]
                    added = dots(block, pick(hops[:half]), ((1,), (1,)))
                    sums[j] = added if sums[j] is None else sums[j] + added
                if chain < chains - 1:
                    continue
                grad = jnp.swapaxes(sums[j], 0, 1).reshape(3, sides, shard_rows, HEAD)
                own_grad = jnp.where(first_side, grad[:, 0], grad[:, 1])
                sent = jnp.where(first_side, grad[:, 1], grad[:, 0]).astype(jnp.bfloat16)
                returned = (own_grad, lax.ppermute(sent, "mesh", swap))
                coming.setdefault("other", {})[j] = returned
            pending[chain] = coming
        if stage == ready[-1] + 2:
            local = pick(clip_directions)
            local = local.reshape(sides, chips, cores, -1, pairs * HEAD)
            axes = [("mesh", 1, sides), ("seq", cores, chips), ("seq", 1, cores)]
            for at, (axis, inner, outer) in enumerate(axes):
                blocks = [lax.index_in_dim(local, -d % outer, at, False) for d in range(outer)]
                for d in range(1, outer):
                    blocks[d] = shifted_by(blocks[d], axis, d, inner, outer)
                local = jnp.stack(blocks, axis=at)
            local = own_order(local.reshape(sides * lanes, -1, pairs * HEAD), order, back=True)
    for j, returned in pending[-1]["other"].items():
        settle(j, *returned)
    summed = jnp.swapaxes(summed[0], 0, 1)

    local = local.reshape(sides, lanes, -1, pairs, HEAD)
    local = jnp.transpose(local, (2, 1, 3, 0, 4)).reshape(-1, lanes, pairs * sides, HEAD)
    direction = local[:, :, :heads].reshape(1, -1, lanes * head_cols)
    return (direction, summed)


def solution(mesh):
    in_specs = (
        P("fsdp", "mesh", None),
        P("fsdp", "mesh", None),
        P("fsdp"),
        P("fsdp", None),
        P("mesh", "fsdp", None, "seq"),
        P("fsdp", None, "seq"),
    )
    out_specs = (P("fsdp", ("mesh", "seq"), None), P(("mesh", "fsdp"), None, "seq"))
    return jax.shard_map(
        per_device, mesh=mesh, in_specs=in_specs, out_specs=out_specs, check_vma=False
    )
```

```python
import math

import jax
import jax.numpy as jnp
from jax import lax
from jax.experimental import pallas as pl
from jax.experimental.pallas import tpu as pltpu
from jax.sharding import PartitionSpec as P

HEAD = 128


def shifted_by(value, axis, d, inner=1, outer=1):
    pairs = []
    for i in range(lax.axis_size(axis)):
        place = i // inner % outer
        pairs.append((i + ((place + d) % outer - place) * inner, i))
    return lax.ppermute(value, axis, pairs)


def spread(value, axis, inner, outer, at):
    pieces = [value] + [shifted_by(value, axis, d, inner, outer) for d in range(1, outer)]
    return jnp.stack(pieces, axis=at)


def turned(value, at, start):
    size = value.shape[at]
    return lax.dynamic_slice_in_dim(jnp.concatenate([value, value], axis=at), start, size, at)


def own_order(value, factors, back=False):
    sizes = [size for size, _ in factors]
    parts = value.reshape(sizes + [-1] + list(value.shape[1:]))
    for at, (size, place) in enumerate(factors):
        parts = turned(parts, at, size - place if back else place)
    return parts.reshape(value.shape)


def gather_step(step, pair, sides, chips, cores):
    first, second = pair
    if step == 0:
        return spread(first, "mesh", 1, sides, 1), spread(second, "seq", cores, chips, 1)
    if step == 1:
        return spread(first, "seq", cores, chips, 2), spread(second, "mesh", 1, sides, 1)
    both = spread(jnp.stack([first, second]), "seq", 1, cores, 4)
    both = both.reshape(2, -1, both.shape[-1])
    return both[0], both[1]


def dots(left, right, dims):
    return lax.dot_general(left, right, (dims, ((), ())), preferred_element_type=jnp.float32)


def attention_kernel(
    block, sides, side_ref, kept_ref, swapped_ref, up_ref, key_group_ref, group_ref,
    direction_ref, cot_ref, teacher_ref, fake_ref, key_grad_ref, value_grad_ref,
):
    length = kept_ref.shape[1]
    span = length // sides
    score_scale = 1.0 / math.sqrt(HEAD)
    first_side = side_ref[0] == 0
    for at in range(sides):
        here = pl.ds(at * span, span)
        there = pl.ds((sides - 1 - at) * span, span)
        kept, swapped = kept_ref[0, here, :], swapped_ref[0, there, :]
        teacher_ref[here, :] = jnp.where(first_side, kept, swapped)
        fake_ref[here, :] = jnp.where(first_side, swapped, kept)
    queries, key_rows, values = (pl.ds(at * HEAD, HEAD) for at in range(3))

    def softmax(triple_ref, rows, visible):
        scores = dots(triple_ref[rows, queries], triple_ref[:, key_rows], ((1,), (1,)))
        scores = jnp.where(visible, scores * score_scale, jnp.float32(-1e30))
        weights = jnp.exp(scores - jnp.max(scores, axis=-1, keepdims=True))
        return weights * (1.0 / jnp.sum(weights, axis=-1, keepdims=True))

    for start in range(0, length, block):
        rows = pl.ds(start, block)
        visible = key_group_ref[0, :1, :] <= group_ref[0, rows, :1]
        prob_low = softmax(teacher_ref, rows, visible).astype(jnp.bfloat16)
        teacher_out = dots(prob_low, teacher_ref[:, values], ((1,), (0,))).astype(jnp.bfloat16)
        probabilities = softmax(fake_ref, rows, visible)
        prob_low = probabilities.astype(jnp.bfloat16)
        fake_out = dots(prob_low, fake_ref[:, values], ((1,), (0,))).astype(jnp.bfloat16)
        direction_ref[0, rows, :] = (
            fake_out.astype(jnp.float32) - teacher_out.astype(jnp.float32)
        ).astype(jnp.bfloat16)
        grad_out = up_ref[0, rows, :]
        prob_grad = dots(grad_out, fake_ref[:, values], ((1,), (1,)))
        row_inner = jnp.sum(probabilities * prob_grad, axis=-1, keepdims=True)
        score_grad = probabilities * (prob_grad - row_inner) * score_scale
        query_grad = dots(score_grad.astype(jnp.bfloat16), fake_ref[:, key_rows], ((1,), (0,)))
        cot_ref[0, 0, rows, :] = query_grad.astype(jnp.bfloat16)
        score_grad = jnp.transpose(score_grad).astype(jnp.bfloat16)
        key_part = dots(score_grad, fake_ref[rows, queries], ((1,), (0,)))
        prob_low = jnp.transpose(probabilities).astype(jnp.bfloat16)
        value_part = dots(prob_low, grad_out, ((1,), (0,)))
        if start == 0:
            key_grad_ref[...] = key_part
            value_grad_ref[...] = value_part
        else:
            key_grad_ref[...] += key_part
            value_grad_ref[...] += value_part
    cot_ref[1, 0] = key_grad_ref[...].astype(jnp.bfloat16)
    cot_ref[2, 0] = value_grad_ref[...].astype(jnp.bfloat16)


def attention(side, sides, kept, swapped, grad_out, groups):
    clips, length, width = kept.shape
    block = math.gcd(length, 256)
    area = clips * length * length

    def spec(rows, columns):
        return pl.BlockSpec((1, rows, columns), lambda clip: (clip, 0, 0))

    triple = spec(length, width)
    return pl.pallas_call(
        lambda *refs: attention_kernel(block, sides, *refs),
        grid=(clips,),
        in_specs=[
            pl.BlockSpec(memory_space=pltpu.SMEM),
            triple, triple, spec(length, HEAD), spec(8, length), spec(length, HEAD),
        ],
        out_specs=[
            spec(length, HEAD),
            pl.BlockSpec((3, 1, length, HEAD), lambda clip: (0, clip, 0, 0)),
        ],
        out_shape=[
            jax.ShapeDtypeStruct((clips, length, HEAD), jnp.bfloat16),
            jax.ShapeDtypeStruct((3, clips, length, HEAD), jnp.bfloat16),
        ],
        scratch_shapes=[pltpu.VMEM((length, width), jnp.bfloat16)] * 2
        + [pltpu.VMEM((length, HEAD), jnp.float32)] * 2,
        compiler_params=pltpu.CompilerParams(vmem_limit_bytes=16 * 1024 * 1024),
        cost_estimate=pl.CostEstimate(
            flops=18 * area * HEAD,
            bytes_accessed=20 * clips * length * HEAD,
            transcendentals=2 * area,
        ),
        name="attention",
    )(side.reshape(1), kept, swapped, grad_out, *groups)


def per_device(latents, noise, noise_level, group_index, projections, upstream):
    planes = lax.axis_size("fsdp")
    sides = lax.axis_size("mesh")
    lanes = lax.axis_size("seq")
    plane = lax.axis_index("fsdp")
    side = lax.axis_index("mesh")
    lane = lax.axis_index("seq")
    half = planes // 2
    chains = 2 if half % 2 == 0 else 1
    share = half // chains
    cores = 2 if lanes % 2 == 0 else 1
    chips = lanes // cores
    order = [(sides, side), (chips, lane // cores), (cores, lane % cores)]
    low_half = plane < half
    first_side = side == 0
    distance = jnp.minimum(plane, planes - 1 - plane)
    swap = [(0, 1), (1, 0)]

    rows, _, head_cols = projections.shape[1:]
    length = group_index.shape[1]
    heads = head_cols // HEAD
    pairs = (heads + 1) // 2
    shard_rows = rows // sides

    def hop_pairs(hop):
        return [(hop - 1, hop), (planes - hop, planes - 1 - hop)]

    def send_hops(values):
        sent = {}
        for parity in range(2):
            hops = [hop for hop in sorted(values) if hop % 2 == parity]
            if not hops:
                continue
            value = values[hops[-1]]
            for hop in hops[-2::-1]:
                here = (plane == hop - 1) | (plane == planes - hop)
                value = jnp.where(here, values[hop], value)
            sent[parity] = lax.ppermute(value, "fsdp", sum([hop_pairs(h) for h in hops], []))
        return sent

    def pick(by_distance):
        picked = by_distance[-1]
        for d in range(len(by_distance) - 2, -1, -1):
            picked = jnp.where(distance == d, by_distance[d], picked)
        return picked

    piece = latents.shape[1] // lanes
    own_rows = lax.dynamic_slice_in_dim(latents[0], lane * piece, piece, 0)
    own_noise = lax.dynamic_slice_in_dim(noise[0], lane * piece, piece, 0)
    noise_rate = noise_level[0]
    noised = (
        (1.0 - noise_rate) * own_rows.astype(jnp.float32)
        + noise_rate * own_noise.astype(jnp.float32)
    ).astype(jnp.bfloat16)

    def block_from(blocks, d):
        to = lax.rem(plane + planes - d, planes)
        block = lax.dynamic_index_in_dim(blocks, to, 0, False)
        return shifted_by(block, "fsdp", d, 1, planes) if d else block

    def by_distance(found):
        found = [block.reshape(piece, rows) for block in found]
        near, far = [], []
        for k in range(half):
            for side_of, mirrored in ((near, False), (far, True)):
                picked = None
                for p in range(planes):
                    clip = k if (p < half) != mirrored else planes - 1 - k
                    block = found[(clip - p) % planes]
                    picked = block if picked is None else jnp.where(plane == p, block, picked)
                side_of.append(picked)
        return jnp.stack(near), jnp.stack(far)

    factors = jnp.swapaxes(projections[0].reshape(rows, 3, heads, HEAD), 1, 2)
    factors = factors.reshape(rows, heads * 3 * HEAD)
    own_up = own_order(upstream[0], order)
    kept_heads = [jnp.minimum(2 * j + side, heads - 1) for j in range(pairs)]
    kept_up = jnp.stack(
        [lax.dynamic_slice_in_dim(own_up, h * HEAD, HEAD, 1) for h in kept_heads]
    )
    blocks = jnp.swapaxes(noised.reshape(piece, planes, rows), 0, 1)
    blocks = [block_from(blocks, d) for d in range(planes)]
    column_blocks = jnp.transpose(
        noised.reshape(piece, sides, planes, shard_rows), (2, 0, 1, 3)
    ).reshape(planes, piece, rows)
    found, factors, kept_up, column_blocks = lax.optimization_barrier(
        (blocks, factors, kept_up, column_blocks)
    )
    tokens = by_distance(found)
    for step in range(3):
        tokens = gather_step(step, tokens, sides, chips, cores)

    def collected(value):
        found = [value]
        for k in range(1, half):
            found.append(lax.ppermute(value, "fsdp", [(k, 0), (planes - 1 - k, planes - 1)]))
        return found

    ready = [min(2 * j + 1, heads - 1) + planes - 1 for j in range(pairs)]
    attends = [ready[j] + (2 if ready[j] < ready[-1] else 1) for j in range(pairs)]
    leaves = []
    for j in range(pairs):
        leaves.append(max([attends[j], heads] + [stage + 1 for stage in leaves[-1:]]))
    stages = leaves[-1] + planes

    pending = [{} for _ in range(chains)]
    finals = [{} for _ in range(chains)]
    passed = [[[] for _ in range(pairs)] for _ in range(chains)]
    made_at = [[[] for _ in range(pairs)] for _ in range(chains)]
    queue = [{} for _ in range(chains)]
    directions = [[] for _ in range(chains)]
    clip_directions = []
    sums = [None] * pairs
    size = share * length

    def own_tokens(chain):
        return [side_of[chain * size : (chain + 1) * size] for side_of in tokens]

    first = 3 * HEAD
    parts = [dots(own_tokens(chain)[1], factors[:, :first], ((1,), (0,))) for chain in range(chains)]
    wide = [None, None]
    (kept_up, column_blocks), parts[0] = lax.optimization_barrier(
        ((kept_up, column_blocks), parts[0])
    )
    ups = collected(kept_up)
    groups = collected(own_order(group_index[0], order))
    found, columns = [block_from(column_blocks, 0)], None
    summed = [jnp.zeros((3, shard_rows, head_cols), jnp.float32)]

    def settle(j, own_grad, other):
        head = 2 * j
        other = other.astype(jnp.float32)
        first = jnp.where(first_side, own_grad, other)
        second = jnp.where(first_side, other, own_grad)
        both = jnp.concatenate([first, second], axis=2)[:, :, : (heads - head) * HEAD]
        summed[0] = lax.dynamic_update_slice(summed[0], both, (0, 0, head * HEAD))

    for stage in range(stages):
        for chain in range(chains):
            coming = pending[chain]
            ahead = {key: coming[key] for key in ("sums", "wide") if key in coming}
            cots = {key: coming[key] for key in ("cots",) if key in coming}
            rest = queue[chain].pop(stage, {})
            if "sums" in ahead:
                made = {
                    (j, hop): cot
                    for j in range(pairs)
                    for hop, cot in enumerate(passed[chain][j])
                    if made_at[chain][j][hop] <= stage - 2
                }
                ahead, tokens, rest, made = lax.optimization_barrier((ahead, tokens, rest, made))
                for (j, hop), cot in made.items():
                    passed[chain][j][hop] = cot
            else:
                tie = (ahead, cots) if stage >= ready[-1] + 2 else ahead
                rest = lax.optimization_barrier((rest, tie))[0]
            arrived = {**ahead, **cots, **rest}
            coming = {}
            if "wide" in arrived:
                wide[2 - stage] = arrived["wide"]
            if chain == 0 and stage == 0 and heads > 1:
                coming["wide"] = dots(tokens[1], factors[:, first:], ((1,), (0,)))
            if chain == 0 and stage == 1:
                coming["wide"] = dots(tokens[0], factors, ((1,), (0,)))
            for j, returned in arrived.get("other", {}).items():
                settle(j, *returned)
            values = {}
            for hop in range(1, planes + 1):
                head = stage - hop + 1
                if not 0 <= head < heads:
                    continue
                if hop <= half and head == 0:
                    total = parts[chain]
                else:
                    column = first * (head - (hop <= half))
                    total = wide[hop <= half][chain * size : (chain + 1) * size]
                    total = total[:, column : column + first]
                if hop > 1:
                    total = total + arrived["sums"][(hop - 1) % 2].astype(jnp.float32)
                values[hop] = total.astype(jnp.bfloat16)
            done = values.pop(planes, None)
            if values:
                coming["sums"] = send_hops(values)
            if done is not None:
                finals[chain][stage - planes + 1] = done
            slot = stage * chains + chain
            if "block" in arrived:
                found.append(arrived["block"])
            if 1 <= slot < planes:
                coming["block"] = block_from(column_blocks, slot)
            turn, odd_slot = divmod(slot - (planes - 1 + 2 * chains), 2 * chains)
            if odd_slot == 0 and turn >= 0:
                columns = by_distance(found) if turn == 0 else arrived.get("columns", columns)
                if turn < 3:
                    coming["columns"] = gather_step(turn, columns, sides, chips, cores)
                if turn == 3:
                    columns = [jnp.swapaxes(each, 0, 1) for each in columns]
            if chain == chains - 1 and stage == 0:
                coming["ups"], coming["groups"] = ups, groups
            if "ups" in arrived:
                ups, groups = arrived["ups"], arrived["groups"]
                group_forms = []
                for at in range(chains):
                    own = jnp.stack(groups[at * share : (at + 1) * share])
                    group_forms.append(
                        (
                            jnp.broadcast_to(own[:, None, :], (share, 8, length)),
                            jnp.broadcast_to(own[:, :, None], (share, length, HEAD)),
                        )
                    )
            for j in range(pairs):
                if stage == ready[j]:
                    even, odd = finals[chain][2 * j], finals[chain][min(2 * j + 1, heads - 1)]
                    kept = jnp.where(first_side, even, odd)
                    sent = jnp.where(first_side, odd, even)
                    coming[f"swapped{j}"] = (kept, lax.ppermute(sent, "mesh", swap))
                if stage == attends[j]:
                    kept, swapped = arrived[f"swapped{j}"]
                    members = range(chain * share, (chain + 1) * share)
                    direction, cotangents = attention(
                        side,
                        sides,
                        kept.reshape(share, length, 3 * HEAD),
                        swapped.reshape(share, length, 3 * HEAD),
                        jnp.stack([ups[k][j] for k in members]),
                        group_forms[chain],
                    )
                    passed[chain][j].append(cotangents.reshape(3, size, HEAD))
                    made_at[chain][j].append(stage)
                    directions[chain].append(direction)
                    if j < pairs - 1:
                        continue
                    joined = jnp.concatenate(directions[chain], axis=2)
                    coming["directions"] = []
                    for k in members:
                        moved = joined[k - chain * share]
                        if k > 0:
                            hops = [(0, k), (planes - 1, planes - 1 - k)]
                            moved = lax.ppermute(moved, "fsdp", hops)
                        coming["directions"].append(moved)
            if stage == ready[-1] + 2:
                clip_directions.extend(arrived["directions"])
            values = {}
            for j in range(pairs):
                hop = stage - leaves[j]
                if 1 <= hop < planes:
                    passed[chain][j].append(arrived["cots"][hop % 2])
                    made_at[chain][j].append(stage)
                if 0 <= hop < planes - 1:
                    values[hop + 1] = passed[chain][j][hop]
            if values:
                coming["cots"] = send_hops(values)
            for j in range(pairs):
                late = j < pairs - 1
                if late and stage == leaves[j] + planes - 1:
                    coming["passed"] = passed[chain][j]
                if stage != leaves[j] + planes - 1 + late:
                    continue
                all_hops = arrived["passed"] if late else passed[chain][j]
                for is_far in range(2):
                    hops = all_hops[::-1] if is_far else all_hops
                    block = columns[is_far][:, chain * size : (chain + 1) * size]
                    added = dots(block, pick(hops[:half]), ((1,), (1,)))
                    sums[j] = added if sums[j] is None else sums[j] + added
                if chain < chains - 1:
                    continue
                grad = jnp.swapaxes(sums[j], 0, 1).reshape(3, sides, shard_rows, HEAD)
                own_grad = jnp.where(first_side, grad[:, 0], grad[:, 1])
                sent = jnp.where(first_side, grad[:, 1], grad[:, 0]).astype(jnp.bfloat16)
                returned = (own_grad, lax.ppermute(sent, "mesh", swap))
                coming.setdefault("other", {})[j] = returned
            pending[chain] = coming
            due = stage + (2 if stage < ready[-1] else 1)
            for key, value in coming.items():
                if key not in ("sums", "wide", "cots"):
                    queue[chain].setdefault(due, {})[key] = value
        if stage == ready[-1] + 2:
            local = pick(clip_directions)
            local = local.reshape(sides, chips, cores, -1, pairs * HEAD)
            axes = [("mesh", 1, sides), ("seq", cores, chips), ("seq", 1, cores)]
            for at, (axis, inner, outer) in enumerate(axes):
                blocks = [lax.index_in_dim(local, -d % outer, at, False) for d in range(outer)]
                for d in range(1, outer):
                    blocks[d] = shifted_by(blocks[d], axis, d, inner, outer)
                local = jnp.stack(blocks, axis=at)
            local = own_order(local.reshape(sides * lanes, -1, pairs * HEAD), order, back=True)
    for left in queue[-1].values():
        for j, returned in left.get("other", {}).items():
            settle(j, *returned)
    summed = jnp.swapaxes(summed[0], 0, 1)

    local = local.reshape(sides, lanes, -1, pairs, HEAD)
    local = jnp.transpose(local, (2, 1, 3, 0, 4)).reshape(-1, lanes, pairs * sides, HEAD)
    direction = local[:, :, :heads].reshape(1, -1, lanes * head_cols)
    return (direction, summed)


def solution(mesh):
    in_specs = (
        P("fsdp", "mesh", None),
        P("fsdp", "mesh", None),
        P("fsdp"),
        P("fsdp", None),
        P("mesh", "fsdp", None, "seq"),
        P("fsdp", None, "seq"),
    )
    out_specs = (P("fsdp", ("mesh", "seq"), None), P(("mesh", "fsdp"), None, "seq"))
    return jax.shard_map(
        per_device, mesh=mesh, in_specs=in_specs, out_specs=out_specs, check_vma=False
    )
```

```python
import math

import jax
import jax.numpy as jnp
from jax import lax
from jax.experimental import pallas as pl
from jax.experimental.pallas import tpu as pltpu
from jax.sharding import PartitionSpec as P

HEAD = 128


def shifted_by(value, axis, d, inner=1, outer=1):
    pairs = []
    for i in range(lax.axis_size(axis)):
        place = i // inner % outer
        pairs.append((i + ((place + d) % outer - place) * inner, i))
    return lax.ppermute(value, axis, pairs)


def spread(value, axis, inner, outer, at):
    pieces = [value] + [shifted_by(value, axis, d, inner, outer) for d in range(1, outer)]
    return jnp.stack(pieces, axis=at)


def turned(value, at, start):
    size = value.shape[at]
    return lax.dynamic_slice_in_dim(jnp.concatenate([value, value], axis=at), start, size, at)


def own_order(value, factors, back=False):
    sizes = [size for size, _ in factors]
    parts = value.reshape(sizes + [-1] + list(value.shape[1:]))
    for at, (size, place) in enumerate(factors):
        parts = turned(parts, at, size - place if back else place)
    return parts.reshape(value.shape)


def gather_step(step, pair, sides, chips, cores):
    first, second = pair
    if step == 0:
        return spread(first, "mesh", 1, sides, 1), spread(second, "seq", cores, chips, 1)
    if step == 1:
        return spread(first, "seq", cores, chips, 2), spread(second, "mesh", 1, sides, 1)
    both = spread(jnp.stack([first, second]), "seq", 1, cores, 4)
    both = both.reshape(2, -1, both.shape[-1])
    return both[0], both[1]


def dots(left, right, dims):
    return lax.dot_general(left, right, (dims, ((), ())), preferred_element_type=jnp.float32)


def attention_kernel(
    block, sides, side_ref, kept_ref, swapped_ref, up_ref, key_group_ref, group_ref,
    direction_ref, cot_ref, teacher_ref, fake_ref, key_grad_ref, value_grad_ref,
):
    length = kept_ref.shape[1]
    span = length // sides
    score_scale = 1.0 / math.sqrt(HEAD)
    first_side = side_ref[0] == 0
    for at in range(sides):
        here = pl.ds(at * span, span)
        there = pl.ds((sides - 1 - at) * span, span)
        kept, swapped = kept_ref[0, here, :], swapped_ref[0, there, :]
        teacher_ref[here, :] = jnp.where(first_side, kept, swapped)
        fake_ref[here, :] = jnp.where(first_side, swapped, kept)
    queries, key_rows, values = (pl.ds(at * HEAD, HEAD) for at in range(3))

    def softmax(triple_ref, rows, visible):
        scores = dots(triple_ref[rows, queries], triple_ref[:, key_rows], ((1,), (1,)))
        scores = jnp.where(visible, scores * score_scale, jnp.float32(-1e30))
        weights = jnp.exp(scores - jnp.max(scores, axis=-1, keepdims=True))
        return weights * (1.0 / jnp.sum(weights, axis=-1, keepdims=True))

    for start in range(0, length, block):
        rows = pl.ds(start, block)
        visible = key_group_ref[0, :1, :] <= group_ref[0, rows, :1]
        prob_low = softmax(teacher_ref, rows, visible).astype(jnp.bfloat16)
        teacher_out = dots(prob_low, teacher_ref[:, values], ((1,), (0,))).astype(jnp.bfloat16)
        probabilities = softmax(fake_ref, rows, visible)
        prob_low = probabilities.astype(jnp.bfloat16)
        fake_out = dots(prob_low, fake_ref[:, values], ((1,), (0,))).astype(jnp.bfloat16)
        direction_ref[0, rows, :] = (
            fake_out.astype(jnp.float32) - teacher_out.astype(jnp.float32)
        ).astype(jnp.bfloat16)
        grad_out = up_ref[0, rows, :]
        prob_grad = dots(grad_out, fake_ref[:, values], ((1,), (1,)))
        row_inner = jnp.sum(probabilities * prob_grad, axis=-1, keepdims=True)
        score_grad = probabilities * (prob_grad - row_inner) * score_scale
        query_grad = dots(score_grad.astype(jnp.bfloat16), fake_ref[:, key_rows], ((1,), (0,)))
        cot_ref[0, 0, rows, :] = query_grad.astype(jnp.bfloat16)
        score_grad = jnp.transpose(score_grad).astype(jnp.bfloat16)
        key_part = dots(score_grad, fake_ref[rows, queries], ((1,), (0,)))
        prob_low = jnp.transpose(probabilities).astype(jnp.bfloat16)
        value_part = dots(prob_low, grad_out, ((1,), (0,)))
        if start == 0:
            key_grad_ref[...] = key_part
            value_grad_ref[...] = value_part
        else:
            key_grad_ref[...] += key_part
            value_grad_ref[...] += value_part
    cot_ref[1, 0] = key_grad_ref[...].astype(jnp.bfloat16)
    cot_ref[2, 0] = value_grad_ref[...].astype(jnp.bfloat16)


def attention(side, sides, kept, swapped, grad_out, groups):
    clips, length, width = kept.shape
    block = math.gcd(length, 256)
    area = clips * length * length

    def spec(rows, columns):
        return pl.BlockSpec((1, rows, columns), lambda clip: (clip, 0, 0))

    triple = spec(length, width)
    return pl.pallas_call(
        lambda *refs: attention_kernel(block, sides, *refs),
        grid=(clips,),
        in_specs=[
            pl.BlockSpec(memory_space=pltpu.SMEM),
            triple, triple, spec(length, HEAD), spec(8, length), spec(length, HEAD),
        ],
        out_specs=[
            spec(length, HEAD),
            pl.BlockSpec((3, 1, length, HEAD), lambda clip: (0, clip, 0, 0)),
        ],
        out_shape=[
            jax.ShapeDtypeStruct((clips, length, HEAD), jnp.bfloat16),
            jax.ShapeDtypeStruct((3, clips, length, HEAD), jnp.bfloat16),
        ],
        scratch_shapes=[pltpu.VMEM((length, width), jnp.bfloat16)] * 2
        + [pltpu.VMEM((length, HEAD), jnp.float32)] * 2,
        compiler_params=pltpu.CompilerParams(vmem_limit_bytes=16 * 1024 * 1024),
        cost_estimate=pl.CostEstimate(
            flops=18 * area * HEAD,
            bytes_accessed=20 * clips * length * HEAD,
            transcendentals=2 * area,
        ),
        name="attention",
    )(side.reshape(1), kept, swapped, grad_out, *groups)


def per_device(latents, noise, noise_level, group_index, projections, upstream):
    planes = lax.axis_size("fsdp")
    sides = lax.axis_size("mesh")
    lanes = lax.axis_size("seq")
    plane = lax.axis_index("fsdp")
    side = lax.axis_index("mesh")
    lane = lax.axis_index("seq")
    half = planes // 2
    chains = 2 if half % 2 == 0 else 1
    share = half // chains
    cores = 2 if lanes % 2 == 0 else 1
    chips = lanes // cores
    order = [(sides, side), (chips, lane // cores), (cores, lane % cores)]
    low_half = plane < half
    first_side = side == 0
    distance = jnp.minimum(plane, planes - 1 - plane)
    swap = [(0, 1), (1, 0)]

    rows, _, head_cols = projections.shape[1:]
    length = group_index.shape[1]
    heads = head_cols // HEAD
    pairs = (heads + 1) // 2
    shard_rows = rows // sides

    def hop_pairs(hop):
        return [(hop - 1, hop), (planes - hop, planes - 1 - hop)]

    def send_hops(values):
        sent = {}
        for parity in range(2):
            hops = [hop for hop in sorted(values) if hop % 2 == parity]
            if not hops:
                continue
            value = values[hops[-1]]
            for hop in hops[-2::-1]:
                here = (plane == hop - 1) | (plane == planes - hop)
                value = jnp.where(here, values[hop], value)
            sent[parity] = lax.ppermute(value, "fsdp", sum([hop_pairs(h) for h in hops], []))
        return sent

    def pick(by_distance):
        picked = by_distance[-1]
        for d in range(len(by_distance) - 2, -1, -1):
            picked = jnp.where(distance == d, by_distance[d], picked)
        return picked

    piece = latents.shape[1] // lanes
    own_rows = lax.dynamic_slice_in_dim(latents[0], lane * piece, piece, 0)
    own_noise = lax.dynamic_slice_in_dim(noise[0], lane * piece, piece, 0)
    noise_rate = noise_level[0]
    noised = (
        (1.0 - noise_rate) * own_rows.astype(jnp.float32)
        + noise_rate * own_noise.astype(jnp.float32)
    ).astype(jnp.bfloat16)

    def block_from(blocks, d):
        to = lax.rem(plane + planes - d, planes)
        block = lax.dynamic_index_in_dim(blocks, to, 0, False)
        return shifted_by(block, "fsdp", d, 1, planes) if d else block

    def by_distance(found):
        found = [block.reshape(piece, rows) for block in found]
        near, far = [], []
        for k in range(half):
            for side_of, mirrored in ((near, False), (far, True)):
                picked = None
                for p in range(planes):
                    clip = k if (p < half) != mirrored else planes - 1 - k
                    block = found[(clip - p) % planes]
                    picked = block if picked is None else jnp.where(plane == p, block, picked)
                side_of.append(picked)
        return jnp.stack(near), jnp.stack(far)

    factors = jnp.swapaxes(projections[0].reshape(rows, 3, heads, HEAD), 1, 2)
    factors = factors.reshape(rows, heads * 3 * HEAD)
    own_up = own_order(upstream[0], order)
    kept_heads = [jnp.minimum(2 * j + side, heads - 1) for j in range(pairs)]
    kept_up = jnp.stack(
        [lax.dynamic_slice_in_dim(own_up, h * HEAD, HEAD, 1) for h in kept_heads]
    )
    blocks = jnp.swapaxes(noised.reshape(piece, planes, rows), 0, 1)
    blocks = [block_from(blocks, d) for d in range(planes)]
    column_blocks = jnp.transpose(
        noised.reshape(piece, sides, planes, shard_rows), (2, 0, 1, 3)
    ).reshape(planes, piece, rows)
    found, factors, kept_up, column_blocks = lax.optimization_barrier(
        (blocks, factors, kept_up, column_blocks)
    )
    tokens = by_distance(found)
    for step in range(3):
        tokens = gather_step(step, tokens, sides, chips, cores)

    def collected(value):
        found = [value]
        for k in range(1, half):
            found.append(lax.ppermute(value, "fsdp", [(k, 0), (planes - 1 - k, planes - 1)]))
        return found

    ready = [min(2 * j + 1, heads - 1) + planes - 1 for j in range(pairs)]
    attends = [ready[j] + (2 if ready[j] < ready[-1] else 1) for j in range(pairs)]
    leaves = []
    for j in range(pairs):
        leaves.append(max([attends[j], heads] + [stage + 1 for stage in leaves[-1:]]))
    stages = leaves[-1] + planes

    pending = [{} for _ in range(chains)]
    finals = [{} for _ in range(chains)]
    passed = [[[] for _ in range(pairs)] for _ in range(chains)]
    made_at = [[[] for _ in range(pairs)] for _ in range(chains)]
    queue = [{} for _ in range(chains)]
    directions = [[] for _ in range(chains)]
    clip_directions = []
    sums = [None] * pairs
    size = share * length

    def own_tokens(chain):
        return [side_of[chain * size : (chain + 1) * size] for side_of in tokens]

    first = 3 * HEAD
    parts = [dots(own_tokens(chain)[1], factors[:, :first], ((1,), (0,))) for chain in range(chains)]
    wide = [None, None]
    (kept_up, column_blocks), parts[0] = lax.optimization_barrier(
        ((kept_up, column_blocks), parts[0])
    )
    ups = collected(kept_up)
    groups = collected(own_order(group_index[0], order))
    found, columns = [block_from(column_blocks, 0)], None
    summed = [jnp.zeros((3, shard_rows, head_cols), jnp.float32)]

    def settle(j, own_grad, other):
        head = 2 * j
        other = other.astype(jnp.float32)
        first = jnp.where(first_side, own_grad, other)
        second = jnp.where(first_side, other, own_grad)
        both = jnp.concatenate([first, second], axis=2)[:, :, : (heads - head) * HEAD]
        summed[0] = lax.dynamic_update_slice(summed[0], both, (0, 0, head * HEAD))

    for stage in range(stages):
        for chain in range(chains):
            coming = pending[chain]
            ahead = {key: coming[key] for key in ("sums", "wide") if key in coming}
            cots = {key: coming[key] for key in ("cots",) if key in coming}
            rest = queue[chain].pop(stage, {})
            if "sums" in ahead and stage < ready[-1]:
                made = {
                    (j, hop): cot
                    for j in range(pairs)
                    for hop, cot in enumerate(passed[chain][j])
                    if made_at[chain][j][hop] <= stage - 2
                }
                ahead, tokens, rest, made = lax.optimization_barrier((ahead, tokens, rest, made))
                for (j, hop), cot in made.items():
                    passed[chain][j][hop] = cot
            else:
                tie = (ahead, cots) if stage >= ready[-1] + 2 else ahead
                rest = lax.optimization_barrier((rest, tie))[0]
            arrived = {**ahead, **cots, **rest}
            coming = {}
            if "wide" in arrived:
                wide[2 - stage] = arrived["wide"]
            if chain == 0 and stage == 0 and heads > 1:
                coming["wide"] = dots(tokens[1], factors[:, first:], ((1,), (0,)))
            if chain == 0 and stage == 1:
                coming["wide"] = dots(tokens[0], factors, ((1,), (0,)))
            for j, returned in arrived.get("other", {}).items():
                settle(j, *returned)
            values = {}
            for hop in range(1, planes + 1):
                head = stage - hop + 1
                if not 0 <= head < heads:
                    continue
                if hop <= half and head == 0:
                    total = parts[chain]
                else:
                    column = first * (head - (hop <= half))
                    total = wide[hop <= half][chain * size : (chain + 1) * size]
                    total = total[:, column : column + first]
                if hop > 1:
                    total = total + arrived["sums"][(hop - 1) % 2].astype(jnp.float32)
                values[hop] = total.astype(jnp.bfloat16)
            done = values.pop(planes, None)
            if values:
                coming["sums"] = send_hops(values)
            if done is not None:
                finals[chain][stage - planes + 1] = done
            slot = stage * chains + chain
            if "block" in arrived:
                found.append(arrived["block"])
            if 1 <= slot < planes:
                coming["block"] = block_from(column_blocks, slot)
            turn, odd_slot = divmod(slot - (planes - 1 + 2 * chains), 2 * chains)
            if odd_slot == 0 and turn >= 0:
                columns = by_distance(found) if turn == 0 else arrived.get("columns", columns)
                if turn < 3:
                    coming["columns"] = gather_step(turn, columns, sides, chips, cores)
                if turn == 3:
                    columns = [jnp.swapaxes(each, 0, 1) for each in columns]
            if chain == chains - 1 and stage == 0:
                coming["ups"], coming["groups"] = ups, groups
            if "ups" in arrived:
                ups, groups = arrived["ups"], arrived["groups"]
                group_forms = []
                for at in range(chains):
                    own = jnp.stack(groups[at * share : (at + 1) * share])
                    group_forms.append(
                        (
                            jnp.broadcast_to(own[:, None, :], (share, 8, length)),
                            jnp.broadcast_to(own[:, :, None], (share, length, HEAD)),
                        )
                    )
            for j in range(pairs):
                if stage == ready[j]:
                    even, odd = finals[chain][2 * j], finals[chain][min(2 * j + 1, heads - 1)]
                    kept = jnp.where(first_side, even, odd)
                    sent = jnp.where(first_side, odd, even)
                    coming[f"swapped{j}"] = (kept, lax.ppermute(sent, "mesh", swap))
                    last_sent = sent
                if stage == attends[j]:
                    kept, swapped = arrived[f"swapped{j}"]
                    members = range(chain * share, (chain + 1) * share)
                    direction, cotangents = attention(
                        side,
                        sides,
                        kept.reshape(share, length, 3 * HEAD),
                        swapped.reshape(share, length, 3 * HEAD),
                        jnp.stack([ups[k][j] for k in members]),
                        group_forms[chain],
                    )
                    passed[chain][j].append(cotangents.reshape(3, size, HEAD))
                    made_at[chain][j].append(stage)
                    directions[chain].append(direction)
                    if j < pairs - 1:
                        continue
                    joined = jnp.concatenate(directions[chain], axis=2)
                    coming["directions"] = []
                    for k in members:
                        moved = joined[k - chain * share]
                        if k > 0:
                            hops = [(0, k), (planes - 1, planes - 1 - k)]
                            moved = lax.ppermute(moved, "fsdp", hops)
                        coming["directions"].append(moved)
            if stage == ready[-1] + 2:
                clip_directions.extend(arrived["directions"])
            values = {}
            for j in range(pairs):
                hop = stage - leaves[j]
                if 1 <= hop < planes:
                    passed[chain][j].append(arrived["cots"][hop % 2])
                    made_at[chain][j].append(stage)
                if 0 <= hop < planes - 1:
                    values[hop + 1] = passed[chain][j][hop]
            if values and stage == ready[-1]:
                values = lax.optimization_barrier((values, last_sent))[0]
            if values:
                coming["cots"] = send_hops(values)
            for j in range(pairs):
                late = j < pairs - 1
                if late and stage == leaves[j] + planes - 1:
                    coming["passed"] = passed[chain][j]
                if stage != leaves[j] + planes - 1 + late:
                    continue
                all_hops = arrived["passed"] if late else passed[chain][j]
                for is_far in range(2):
                    hops = all_hops[::-1] if is_far else all_hops
                    block = columns[is_far][:, chain * size : (chain + 1) * size]
                    added = dots(block, pick(hops[:half]), ((1,), (1,)))
                    sums[j] = added if sums[j] is None else sums[j] + added
                if chain < chains - 1:
                    continue
                grad = jnp.swapaxes(sums[j], 0, 1).reshape(3, sides, shard_rows, HEAD)
                own_grad = jnp.where(first_side, grad[:, 0], grad[:, 1])
                sent = jnp.where(first_side, grad[:, 1], grad[:, 0]).astype(jnp.bfloat16)
                returned = (own_grad, lax.ppermute(sent, "mesh", swap))
                coming.setdefault("other", {})[j] = returned
            pending[chain] = coming
            due = stage + (2 if stage < ready[-1] else 1)
            for key, value in coming.items():
                if key not in ("sums", "wide", "cots"):
                    queue[chain].setdefault(due, {})[key] = value
        if stage == ready[-1] + 2:
            local = pick(clip_directions)
            local = local.reshape(sides, chips, cores, -1, pairs * HEAD)
            axes = [("mesh", 1, sides), ("seq", cores, chips), ("seq", 1, cores)]
            for at, (axis, inner, outer) in enumerate(axes):
                blocks = [lax.index_in_dim(local, -d % outer, at, False) for d in range(outer)]
                for d in range(1, outer):
                    blocks[d] = shifted_by(blocks[d], axis, d, inner, outer)
                local = jnp.stack(blocks, axis=at)
            local = own_order(local.reshape(sides * lanes, -1, pairs * HEAD), order, back=True)
    for left in queue[-1].values():
        for j, returned in left.get("other", {}).items():
            settle(j, *returned)
    summed = jnp.swapaxes(summed[0], 0, 1)

    local = local.reshape(sides, lanes, -1, pairs, HEAD)
    local = jnp.transpose(local, (2, 1, 3, 0, 4)).reshape(-1, lanes, pairs * sides, HEAD)
    direction = local[:, :, :heads].reshape(1, -1, lanes * head_cols)
    return (direction, summed)


def solution(mesh):
    in_specs = (
        P("fsdp", "mesh", None),
        P("fsdp", "mesh", None),
        P("fsdp"),
        P("fsdp", None),
        P("mesh", "fsdp", None, "seq"),
        P("fsdp", None, "seq"),
    )
    out_specs = (P("fsdp", ("mesh", "seq"), None), P(("mesh", "fsdp"), None, "seq"))
    return jax.shard_map(
        per_device, mesh=mesh, in_specs=in_specs, out_specs=out_specs, check_vma=False
    )
```

```python
import math

import jax
import jax.numpy as jnp
from jax import lax
from jax.experimental import pallas as pl
from jax.experimental.pallas import tpu as pltpu
from jax.sharding import PartitionSpec as P

HEAD = 128


def shifted_by(value, axis, d, inner=1, outer=1):
    pairs = []
    for i in range(lax.axis_size(axis)):
        place = i // inner % outer
        pairs.append((i + ((place + d) % outer - place) * inner, i))
    return lax.ppermute(value, axis, pairs)


def spread(value, axis, inner, outer, at):
    pieces = [value] + [shifted_by(value, axis, d, inner, outer) for d in range(1, outer)]
    return jnp.stack(pieces, axis=at)


def turned(value, at, start):
    size = value.shape[at]
    return lax.dynamic_slice_in_dim(jnp.concatenate([value, value], axis=at), start, size, at)


def own_order(value, factors, back=False):
    sizes = [size for size, _ in factors]
    parts = value.reshape(sizes + [-1] + list(value.shape[1:]))
    for at, (size, place) in enumerate(factors):
        parts = turned(parts, at, size - place if back else place)
    return parts.reshape(value.shape)


def gather_step(step, pair, sides, chips, cores):
    first, second = pair
    if step == 0:
        return spread(first, "mesh", 1, sides, 1), spread(second, "seq", cores, chips, 1)
    if step == 1:
        return spread(first, "seq", cores, chips, 2), spread(second, "mesh", 1, sides, 1)
    both = spread(jnp.stack([first, second]), "seq", 1, cores, 4)
    both = both.reshape(2, -1, both.shape[-1])
    return both[0], both[1]


def dots(left, right, dims):
    return lax.dot_general(left, right, (dims, ((), ())), preferred_element_type=jnp.float32)


def attention_kernel(
    block, sides, side_ref, kept_ref, swapped_ref, up_ref, key_group_ref, group_ref,
    direction_ref, cot_ref, teacher_ref, fake_ref, key_grad_ref, value_grad_ref,
):
    length = kept_ref.shape[1]
    span = length // sides
    score_scale = 1.0 / math.sqrt(HEAD)
    first_side = side_ref[0] == 0
    for at in range(sides):
        here = pl.ds(at * span, span)
        there = pl.ds((sides - 1 - at) * span, span)
        kept, swapped = kept_ref[0, here, :], swapped_ref[0, there, :]
        teacher_ref[here, :] = jnp.where(first_side, kept, swapped)
        fake_ref[here, :] = jnp.where(first_side, swapped, kept)
    queries, key_rows, values = (pl.ds(at * HEAD, HEAD) for at in range(3))

    def softmax(triple_ref, rows, visible):
        scores = dots(triple_ref[rows, queries], triple_ref[:, key_rows], ((1,), (1,)))
        scores = jnp.where(visible, scores * score_scale, jnp.float32(-1e30))
        weights = jnp.exp(scores - jnp.max(scores, axis=-1, keepdims=True))
        return weights * (1.0 / jnp.sum(weights, axis=-1, keepdims=True))

    for start in range(0, length, block):
        rows = pl.ds(start, block)
        visible = key_group_ref[0, :1, :] <= group_ref[0, rows, :1]
        prob_low = softmax(teacher_ref, rows, visible).astype(jnp.bfloat16)
        teacher_out = dots(prob_low, teacher_ref[:, values], ((1,), (0,))).astype(jnp.bfloat16)
        probabilities = softmax(fake_ref, rows, visible)
        prob_low = probabilities.astype(jnp.bfloat16)
        fake_out = dots(prob_low, fake_ref[:, values], ((1,), (0,))).astype(jnp.bfloat16)
        direction_ref[0, rows, :] = (
            fake_out.astype(jnp.float32) - teacher_out.astype(jnp.float32)
        ).astype(jnp.bfloat16)
        grad_out = up_ref[0, rows, :]
        prob_grad = dots(grad_out, fake_ref[:, values], ((1,), (1,)))
        row_inner = jnp.sum(probabilities * prob_grad, axis=-1, keepdims=True)
        score_grad = probabilities * (prob_grad - row_inner) * score_scale
        query_grad = dots(score_grad.astype(jnp.bfloat16), fake_ref[:, key_rows], ((1,), (0,)))
        cot_ref[0, 0, rows, :] = query_grad.astype(jnp.bfloat16)
        score_grad = jnp.transpose(score_grad).astype(jnp.bfloat16)
        key_part = dots(score_grad, fake_ref[rows, queries], ((1,), (0,)))
        prob_low = jnp.transpose(probabilities).astype(jnp.bfloat16)
        value_part = dots(prob_low, grad_out, ((1,), (0,)))
        if start == 0:
            key_grad_ref[...] = key_part
            value_grad_ref[...] = value_part
        else:
            key_grad_ref[...] += key_part
            value_grad_ref[...] += value_part
    cot_ref[1, 0] = key_grad_ref[...].astype(jnp.bfloat16)
    cot_ref[2, 0] = value_grad_ref[...].astype(jnp.bfloat16)


def attention(side, sides, kept, swapped, grad_out, groups):
    clips, length, width = kept.shape
    block = math.gcd(length, 256)
    area = clips * length * length

    def spec(rows, columns):
        return pl.BlockSpec((1, rows, columns), lambda clip: (clip, 0, 0))

    triple = spec(length, width)
    return pl.pallas_call(
        lambda *refs: attention_kernel(block, sides, *refs),
        grid=(clips,),
        in_specs=[
            pl.BlockSpec(memory_space=pltpu.SMEM),
            triple, triple, spec(length, HEAD), spec(8, length), spec(length, HEAD),
        ],
        out_specs=[
            spec(length, HEAD),
            pl.BlockSpec((3, 1, length, HEAD), lambda clip: (0, clip, 0, 0)),
        ],
        out_shape=[
            jax.ShapeDtypeStruct((clips, length, HEAD), jnp.bfloat16),
            jax.ShapeDtypeStruct((3, clips, length, HEAD), jnp.bfloat16),
        ],
        scratch_shapes=[pltpu.VMEM((length, width), jnp.bfloat16)] * 2
        + [pltpu.VMEM((length, HEAD), jnp.float32)] * 2,
        compiler_params=pltpu.CompilerParams(vmem_limit_bytes=16 * 1024 * 1024),
        cost_estimate=pl.CostEstimate(
            flops=18 * area * HEAD,
            bytes_accessed=20 * clips * length * HEAD,
            transcendentals=2 * area,
        ),
        name="attention",
    )(side.reshape(1), kept, swapped, grad_out, *groups)


def per_device(latents, noise, noise_level, group_index, projections, upstream):
    planes = lax.axis_size("fsdp")
    sides = lax.axis_size("mesh")
    lanes = lax.axis_size("seq")
    plane = lax.axis_index("fsdp")
    side = lax.axis_index("mesh")
    lane = lax.axis_index("seq")
    half = planes // 2
    chains = 2 if half % 2 == 0 else 1
    share = half // chains
    cores = 2 if lanes % 2 == 0 else 1
    chips = lanes // cores
    order = [(sides, side), (chips, lane // cores), (cores, lane % cores)]
    low_half = plane < half
    first_side = side == 0
    distance = jnp.minimum(plane, planes - 1 - plane)
    swap = [(0, 1), (1, 0)]

    rows, _, head_cols = projections.shape[1:]
    length = group_index.shape[1]
    heads = head_cols // HEAD
    pairs = (heads + 1) // 2
    shard_rows = rows // sides

    def hop_pairs(hop):
        return [(hop - 1, hop), (planes - hop, planes - 1 - hop)]

    def send_hops(values):
        sent = {}
        for parity in range(2):
            hops = [hop for hop in sorted(values) if hop % 2 == parity]
            if not hops:
                continue
            value = values[hops[-1]]
            for hop in hops[-2::-1]:
                here = (plane == hop - 1) | (plane == planes - hop)
                value = jnp.where(here, values[hop], value)
            sent[parity] = lax.ppermute(value, "fsdp", sum([hop_pairs(h) for h in hops], []))
        return sent

    def pick(by_distance):
        picked = by_distance[-1]
        for d in range(len(by_distance) - 2, -1, -1):
            picked = jnp.where(distance == d, by_distance[d], picked)
        return picked

    piece = latents.shape[1] // lanes
    own_rows = lax.dynamic_slice_in_dim(latents[0], lane * piece, piece, 0)
    own_noise = lax.dynamic_slice_in_dim(noise[0], lane * piece, piece, 0)
    noise_rate = noise_level[0]
    noised = (
        (1.0 - noise_rate) * own_rows.astype(jnp.float32)
        + noise_rate * own_noise.astype(jnp.float32)
    ).astype(jnp.bfloat16)

    def exchanged(blocks, beside=()):
        found = []
        for d in range(planes):
            to = lax.rem(plane + planes - d, planes)
            block = lax.dynamic_index_in_dim(blocks, to, 1, False)
            found.append(shifted_by(block, "fsdp", d, 1, planes) if d else block)
        found, beside = lax.optimization_barrier((found, beside))
        found = [block.reshape(piece, rows) for block in found]
        near, far = [], []
        for k in range(half):
            for side_of, mirrored in ((near, False), (far, True)):
                picked = None
                for p in range(planes):
                    clip = k if (p < half) != mirrored else planes - 1 - k
                    block = found[(clip - p) % planes]
                    picked = block if picked is None else jnp.where(plane == p, block, picked)
                side_of.append(picked)
        return (jnp.stack(near), jnp.stack(far)), beside

    factors = jnp.transpose(projections[0].reshape(rows, 3, heads, HEAD), (2, 0, 1, 3))
    factors = factors.reshape(heads, rows, 3 * HEAD)
    tokens, factors = exchanged(noised.reshape(piece, planes, rows), factors)
    tokens = gather_step(0, tokens, sides, chips, cores)
    for step in range(1, 3):
        tokens = gather_step(step, tokens, sides, chips, cores)

    def collected(value):
        found = [value]
        for k in range(1, half):
            found.append(lax.ppermute(value, "fsdp", [(k, 0), (planes - 1 - k, planes - 1)]))
        return found

    ready = [min(2 * j + 1, heads - 1) + planes - 1 for j in range(pairs)]
    leaves = []
    for j in range(pairs):
        leaves.append(max([ready[j] + 1, heads] + [stage + 1 for stage in leaves[-1:]]))
    stages = leaves[-1] + planes

    pending = [{} for _ in range(chains)]
    finals = [{} for _ in range(chains)]
    passed = [[[] for _ in range(pairs)] for _ in range(chains)]
    directions = [[] for _ in range(chains)]
    clip_directions = []
    sums = [None] * pairs
    size = share * length

    def own_tokens(chain):
        return [side_of[chain * size : (chain + 1) * size] for side_of in tokens]

    def product(chain, is_far, head):
        return dots(own_tokens(chain)[is_far], factors[head], ((1,), (0,)))

    parts = [{(1, 0): product(chain, 1, 0)} for chain in range(chains)]
    (own_up, noised), parts = lax.optimization_barrier(((upstream[0], noised), parts))
    own_up = own_order(own_up, order)
    kept_heads = [jnp.minimum(2 * j + side, heads - 1) for j in range(pairs)]
    ups = collected(
        jnp.stack([lax.dynamic_slice_in_dim(own_up, h * HEAD, HEAD, 1) for h in kept_heads])
    )
    groups = collected(own_order(group_index[0], order))
    summed = [jnp.zeros((3, shard_rows, head_cols), jnp.float32)]

    def settle(j, own_grad, other):
        head = 2 * j
        other = other.astype(jnp.float32)
        first = jnp.where(first_side, own_grad, other)
        second = jnp.where(first_side, other, own_grad)
        both = jnp.concatenate([first, second], axis=2)[:, :, : (heads - head) * HEAD]
        summed[0] = lax.dynamic_update_slice(summed[0], both, (0, 0, head * HEAD))

    for stage in range(stages):
        for chain in range(chains):
            arrived, tokens = lax.optimization_barrier((pending[chain], tokens))
            coming = {}
            parts[chain].update(arrived.get("parts", {}))
            coming["parts"] = {
                (is_far, head): product(chain, is_far, head)
                for is_far, head in ((1, stage + 1), (0, stage + 1 - half))
                if 0 <= head < heads
            }
            for j, returned in arrived.get("other", {}).items():
                settle(j, *returned)
            values = {}
            for hop in range(1, planes + 1):
                head = stage - hop + 1
                if not 0 <= head < heads:
                    continue
                total = parts[chain][hop <= half, head]
                if hop > 1:
                    total = total + arrived["sums"][(hop - 1) % 2].astype(jnp.float32)
                values[hop] = total.astype(jnp.bfloat16)
            done = values.pop(planes, None)
            if values:
                coming["sums"] = send_hops(values)
            if done is not None:
                finals[chain][stage - planes + 1] = done
            if chain == chains - 1 and stage == 0:
                columns = noised.reshape(piece, sides, planes, shard_rows)
                coming["columns"] = exchanged(columns.swapaxes(1, 2))[0]
                coming["ups"], coming["groups"] = ups, groups
            if chain == chains - 1 and stage == 1:
                ups, groups = arrived["ups"], arrived["groups"]
                group_forms = []
                for at in range(chains):
                    own = jnp.stack(groups[at * share : (at + 1) * share])
                    group_forms.append(
                        (
                            jnp.broadcast_to(own[:, None, :], (share, 8, length)),
                            jnp.broadcast_to(own[:, :, None], (share, length, HEAD)),
                        )
                    )
            if chain == chains - 1 and 1 <= stage <= 3:
                coming["columns"] = gather_step(
                    stage - 1, arrived["columns"], sides, chips, cores
                )
            if chain == chains - 1 and stage == 4:
                columns = arrived["columns"]
            for j in range(pairs):
                if stage == ready[j]:
                    even, odd = finals[chain][2 * j], finals[chain][min(2 * j + 1, heads - 1)]
                    kept = jnp.where(first_side, even, odd)
                    sent = jnp.where(first_side, odd, even)
                    coming["swapped"] = (kept, lax.ppermute(sent, "mesh", swap))
                if stage == ready[j] + 1:
                    kept, swapped = arrived["swapped"]
                    members = range(chain * share, (chain + 1) * share)
                    direction, cotangents = attention(
                        side,
                        sides,
                        kept.reshape(share, length, 3 * HEAD),
                        swapped.reshape(share, length, 3 * HEAD),
                        jnp.stack([ups[k][j] for k in members]),
                        group_forms[chain],
                    )
                    passed[chain][j].append(cotangents.reshape(3, size, HEAD))
                    directions[chain].append(direction)
                    if j < pairs - 1:
                        continue
                    joined = jnp.concatenate(directions[chain], axis=2)
                    coming["directions"] = []
                    for k in members:
                        moved = joined[k - chain * share]
                        if k > 0:
                            hops = [(0, k), (planes - 1, planes - 1 - k)]
                            moved = lax.ppermute(moved, "fsdp", hops)
                        coming["directions"].append(moved)
            if stage == ready[-1] + 2:
                clip_directions.extend(arrived["directions"])
            values = {}
            for j in range(pairs):
                hop = stage - leaves[j]
                if 1 <= hop < planes:
                    passed[chain][j].append(arrived["cots"][hop % 2])
                if 0 <= hop < planes - 1:
                    values[hop + 1] = passed[chain][j][hop]
            if values:
                coming["cots"] = send_hops(values)
            for j in range(pairs):
                late = j < pairs - 1
                if late and stage == leaves[j] + planes - 1:
                    coming["passed"] = passed[chain][j]
                if stage != leaves[j] + planes - 1 + late:
                    continue
                all_hops = arrived["passed"] if late else passed[chain][j]
                for is_far in range(2):
                    hops = all_hops[::-1] if is_far else all_hops
                    block = columns[is_far][chain * size : (chain + 1) * size]
                    added = dots(block, pick(hops[:half]), ((0,), (1,)))
                    sums[j] = added if sums[j] is None else sums[j] + added
                if chain < chains - 1:
                    continue
                grad = jnp.swapaxes(sums[j], 0, 1).reshape(3, sides, shard_rows, HEAD)
                own_grad = jnp.where(first_side, grad[:, 0], grad[:, 1])
                sent = jnp.where(first_side, grad[:, 1], grad[:, 0]).astype(jnp.bfloat16)
                returned = (own_grad, lax.ppermute(sent, "mesh", swap))
                coming.setdefault("other", {})[j] = returned
            pending[chain] = coming
        if stage == ready[-1] + 2:
            local = pick(clip_directions)
            local = local.reshape(sides, chips, cores, -1, pairs * HEAD)
            axes = [("mesh", 1, sides), ("seq", cores, chips), ("seq", 1, cores)]
            for at, (axis, inner, outer) in enumerate(axes):
                blocks = [lax.index_in_dim(local, -d % outer, at, False) for d in range(outer)]
                for d in range(1, outer):
                    blocks[d] = shifted_by(blocks[d], axis, d, inner, outer)
                local = jnp.stack(blocks, axis=at)
            local = own_order(local.reshape(sides * lanes, -1, pairs * HEAD), order, back=True)
    for j, returned in pending[-1]["other"].items():
        settle(j, *returned)
    summed = jnp.swapaxes(summed[0], 0, 1)

    local = local.reshape(sides, lanes, -1, pairs, HEAD)
    local = jnp.transpose(local, (2, 1, 3, 0, 4)).reshape(-1, lanes, pairs * sides, HEAD)
    direction = local[:, :, :heads].reshape(1, -1, lanes * head_cols)
    return (direction, summed)


def solution(mesh):
    in_specs = (
        P("fsdp", "mesh", None),
        P("fsdp", "mesh", None),
        P("fsdp"),
        P("fsdp", None),
        P("mesh", "fsdp", None, "seq"),
        P("fsdp", None, "seq"),
    )
    out_specs = (P("fsdp", ("mesh", "seq"), None), P(("mesh", "fsdp"), None, "seq"))
    return jax.shard_map(
        per_device, mesh=mesh, in_specs=in_specs, out_specs=out_specs, check_vma=False
    )
```
